32 devices in a mesh: dp: 8 (over z, x), seq: 4 (over y, core).
Axes of the slice: x: 2, y: 2, z: 4, core: 2. Of those that a mesh axis runs over, the one named last changes fastest.
Arguments:
- latents: bfloat16 [16, 512, 1152], P('dp', 'seq'), may hold values from -16 to 16
- conditioning: bfloat16 [16, 1152], P('dp'), may hold values from -5 to 5
- w_mod: bfloat16 [1152, 6912], P(('dp', 'seq')), may hold values from -0.1875 to 0.1875
- b_mod: bfloat16 [6912], P(('dp', 'seq')), may hold values from -4 to 4
- w_qkv: bfloat16 [1152, 3456], P(('dp', 'seq')), may hold values from -0.1875 to 0.1875
- b_qv: bfloat16 [2304], P(('dp', 'seq')), may hold values from -1.5 to 1.5
- w_out: bfloat16 [1152, 1152], P(('dp', 'seq')), may hold values from -0.75 to 0.75
- b_out: bfloat16 [1152], P(('dp', 'seq')), may hold values from -3 to 3
- w_fc1: bfloat16 [1152, 4608], P(('dp', 'seq')), may hold values from -0.1875 to 0.1875
- b_fc1: bfloat16 [4608], P(('dp', 'seq')), may hold values from -3 to 3
- w_fc2: bfloat16 [4608, 1152], P(('dp', 'seq')), may hold values from -0.09375 to 0.09375
- b_fc2: bfloat16 [1152], P(('dp', 'seq')), may hold values from -3 to 3
- out_grad: bfloat16 [16, 512, 1152], P('dp', 'seq'), may hold values from -6 to 6
Outputs:
- output: bfloat16 [16, 512, 1152], P('dp', 'seq')
- latents_grad: bfloat16 [16, 512, 1152], P('dp', 'seq')
- conditioning_grad: bfloat16 [16, 1152], P('dp')
- w_mod_grad: float32 [1152, 6912], P(('dp', 'seq'))
- b_mod_grad: float32 [6912], P(('dp', 'seq'))
- w_qkv_grad: float32 [1152, 3456], P(('dp', 'seq'))
- b_qv_grad: float32 [2304], P(('dp', 'seq'))
- w_out_grad: float32 [1152, 1152], P(('dp', 'seq'))
- b_out_grad: float32 [1152], P(('dp', 'seq'))
- w_fc1_grad: float32 [1152, 4608], P(('dp', 'seq'))
- b_fc1_grad: float32 [4608], P(('dp', 'seq'))
- w_fc2_grad: float32 [4608, 1152], P(('dp', 'seq'))
- b_fc2_grad: float32 [1152], P(('dp', 'seq'))
The draws below stay inside these ranges and needn't reach their ends.
All inputs are finite; a program needn't handle non-finite values.
Results may differ from the reference program's by a relative error of at most 0.015.
The reference program's roundings to bfloat16 on the way count: a program that leaves them out, or rounds other values in their place, can miss the bound.
Values may be sent and summed in bfloat16 or wider, within the bound.
A program may use at most 320 MiB of HBM per device.

```python
import math
from functools import partial
import jax
import jax.numpy as jnp
from jax import lax

D = 1152
HEADS = 16
HEAD_DIM = 72
FF = 4608
LATENTS = 16
SEQ_LEN = 512


def draw_latents(key, part):
    key_one, key_two, key_three = jax.random.split(jax.random.fold_in(key, 11), 3)
    base = jax.random.truncated_normal(key_one, -4.0, 4.0, (LATENTS, SEQ_LEN, D), jnp.float32)
    row_scale = jnp.exp(jax.random.uniform(key_two, (LATENTS, SEQ_LEN, 1), jnp.float32, math.log(0.5), math.log(2.0)))
    column_scale = jnp.exp(jax.random.uniform(key_three, (1, 1, D), jnp.float32, math.log(0.5), math.log(2.0)))
    return (base * row_scale * column_scale).astype(jnp.bfloat16)


def block_levels(key, extent, shards, low, high):
    gain, own = 1.0, jax.random.fold_in(key, 6)
    for dim, parts in shards:
        draws = jnp.exp(jax.random.uniform(jax.random.fold_in(own, dim), (parts,), jnp.float32, low / len(shards), high / len(shards)))
        gain = gain * jnp.repeat(draws, extent[dim] // parts).reshape([-1 if axis == dim else 1 for axis in range(len(extent))])
    return gain


def normal_values(rng, dims, spread, most, shards=(), dtype=jnp.bfloat16):
    array = spread * jax.random.normal(rng, dims, jnp.float32)
    if shards:
        array = array * block_levels(rng, dims, shards, -0.22, 0.18)
    return jnp.clip(array, -most, most).astype(dtype)


def setup_inputs(seed: int = 0) -> dict:
    key_of = jax.random.split(jax.random.key(seed), 14)
    latents = draw_latents(jax.random.fold_in(key_of[13], 71), 0)
    conditioning = normal_values(key_of[1], (LATENTS, D), 1.0, 5.0, ((0, 8),))
    w_mod = normal_values(key_of[2], (D, 6 * D), D ** -0.5, 0.1875, ((0, 32),))
    b_mod = normal_values(key_of[3], (6 * D,), 0.7, 4.0, ((0, 32),))
    w_qkv = normal_values(key_of[4], (D, 3 * D), D ** -0.5, 0.1875, ((0, 32),))
    b_qv = normal_values(key_of[5], (2 * D,), 0.25, 1.5, ((0, 32),))
    w_out = normal_values(key_of[6], (D, D), (max(D // 16, 1)) ** -0.5, 0.75, ((0, 32),))
    b_out = normal_values(key_of[7], (D,), 0.5, 3.0, ((0, 32),))
    w_fc1 = normal_values(key_of[8], (D, FF), D ** -0.5, 0.1875, ((0, 32),))
    b_fc1 = normal_values(key_of[9], (FF,), 0.5, 3.0, ((0, 32),))
    w_fc2 = normal_values(key_of[10], (FF, D), FF ** -0.5, 0.09375, ((0, 32),))
    b_fc2 = normal_values(key_of[11], (D,), 0.5, 3.0, ((0, 32),))
    out_grad = normal_values(key_of[12], (LATENTS, SEQ_LEN, D), 1.0, 6.0, ((0, 8), (1, 4)))
    return dict(latents=latents, conditioning=conditioning, w_mod=w_mod, b_mod=b_mod, w_qkv=w_qkv, b_qv=b_qv, w_out=w_out, b_out=b_out, w_fc1=w_fc1, b_fc1=b_fc1, w_fc2=w_fc2, b_fc2=b_fc2, out_grad=out_grad)


EPSILON = 1e-06

@jax.custom_vjp
def low(v):
    return lax.optimization_barrier(v.astype(jnp.bfloat16)).astype(jnp.float32)

@jax.custom_vjp
def low_back(v):
    return v

def low_keep(v):
    return (low(v), None)

def low_pass(kept, grad):
    return (grad,)

def back_keep(v):
    return (v, None)

def back_low(kept, grad):
    return (low(grad),)
low.defvjp(low_keep, low_pass)
low_back.defvjp(back_keep, back_low)

def matmul(left, right):
    return jnp.dot(left, right, precision=lax.Precision.HIGHEST)

def layer_norm(values):
    center = values - lax.optimization_barrier(jnp.mean(values, axis=-1, keepdims=True))
    return center * lax.rsqrt(lax.optimization_barrier(jnp.mean(center * center, axis=-1, keepdims=True)) + EPSILON)

def block(params, inputs):
    w_qkv, b_qv, w_out, b_out, w_fc1, b_fc1, w_fc2, b_fc2 = params
    tokens, modulation = inputs
    shift_att, scale_att, gate_att, shift_mlp, scale_mlp, gate_mlp = jnp.split(modulation, 6)
    length = tokens.shape[0]
    modded = low(layer_norm(tokens) * (1.0 + scale_att) + shift_att)
    joined = matmul(modded, w_qkv)
    queries = low(low_back(joined[:, :D] + b_qv[:D]))
    key_rows = low(low_back(joined[:, D:2 * D]))
    values = low(low_back(joined[:, 2 * D:] + b_qv[D:]))
    head_q = queries.reshape(length, HEADS, HEAD_DIM)
    head_k = key_rows.reshape(length, HEADS, HEAD_DIM)
    head_v = values.reshape(length, HEADS, HEAD_DIM)
    scores = low_back(jnp.einsum('qhd,khd->hqk', head_q, head_k, precision=lax.Precision.HIGHEST) * HEAD_DIM ** (-0.5))
    soft_weights = jax.nn.softmax(scores, axis=-1)
    mixed_heads = jnp.einsum('hqk,khd->qhd', low(soft_weights), head_v, precision=lax.Precision.HIGHEST).reshape(length, D)
    mixed_heads = low(low_back(mixed_heads))
    attended = low_back(matmul(mixed_heads, w_out) + b_out)
    middle = tokens + gate_att * attended
    modded_two = low(layer_norm(middle) * (1.0 + scale_mlp) + shift_mlp)
    hidden = low_back(matmul(modded_two, w_fc1) + b_fc1)
    active = low(jax.nn.gelu(hidden, approximate=True))
    branch = low_back(matmul(active, w_fc2) + b_fc2)
    return middle + gate_mlp * branch

def forward(weights, latents, conditioning):
    cond_act = low(jax.nn.silu(conditioning))
    modulation = low_back(matmul(cond_act, weights[0]) + weights[1])
    per_latent = jax.checkpoint(partial(block, weights[2:]))
    return lax.map(per_latent, (latents, modulation))

def reference(latents, conditioning, w_mod, b_mod, w_qkv, b_qv, w_out, b_out, w_fc1, b_fc1, w_fc2, b_fc2, out_grad):
    weights = tuple((item.astype(jnp.float32) for item in (w_mod, b_mod, w_qkv, b_qv, w_out, b_out, w_fc1, b_fc1, w_fc2, b_fc2)))
    output, pullback = jax.vjp(forward, weights, latents.astype(jnp.float32), conditioning.astype(jnp.float32))
    weight_grads, latents_grad, cond_grad = pullback(out_grad.astype(jnp.float32))
    return (output.astype(jnp.bfloat16), latents_grad.astype(jnp.bfloat16), cond_grad.astype(jnp.bfloat16), weight_grads[0], weight_grads[1], weight_grads[2], weight_grads[3], weight_grads[4], weight_grads[5], weight_grads[6], weight_grads[7], weight_grads[8], weight_grads[9])
```

```python
from functools import partial

import jax
import jax.numpy as jnp
from jax import lax
from jax.sharding import PartitionSpec as P

HEADS = 16
HEAD_DIM = 72
EPSILON = 1e-06
BF16 = jnp.bfloat16
F32 = jnp.float32


def layer_norm(values):
    center = values - jnp.mean(values, axis=-1, keepdims=True)
    inverse = lax.rsqrt(jnp.mean(center * center, axis=-1, keepdims=True) + EPSILON)
    return (center * inverse, inverse)


def norm_back(incoming, normed, inverse):
    return inverse * (
        incoming
        - jnp.mean(incoming, axis=-1, keepdims=True)
        - normed * jnp.mean(incoming * normed, axis=-1, keepdims=True)
    )


def dot(left, right):
    return jnp.dot(left, right, preferred_element_type=F32)


def dot_right_t(left, right):
    return lax.dot_general(left, right, (((1,), (1,)), ((), ())), preferred_element_type=F32)


def dot_left_t(left, right):
    return lax.dot_general(left, right, (((0,), (0,)), ((), ())), preferred_element_type=F32)


def body(
    latents,
    conditioning,
    w_mod,
    b_mod,
    w_qkv,
    b_qv,
    w_out,
    b_out,
    w_fc1,
    b_fc1,
    w_fc2,
    b_fc2,
    out_grad,
):
    count, tokens, width = latents.shape
    dp, seq = lax.axis_size("dp"), lax.axis_size("seq")
    both = ("dp", "seq")
    my_dp, my_seq = lax.axis_index("dp"), lax.axis_index("seq")
    me = my_dp * seq + my_seq
    rows, units = w_qkv.shape[0], w_fc2.shape[0]
    part = width // seq
    heads = HEADS // seq
    length = seq * tokens

    cond = conditioning.astype(F32)
    cond_act, silu_back = jax.vjp(jax.nn.silu, cond)
    cond_low = lax.all_gather(cond_act.astype(BF16), "dp", axis=0, tiled=True)
    cond_mine = lax.dynamic_slice_in_dim(cond_low, me * rows, rows, axis=1)
    mod_part = dot(cond_mine, w_mod)
    mod_sum = lax.psum(lax.psum_scatter(mod_part, "dp", scatter_dimension=0, tiled=True), "seq")
    biases = lax.all_gather(jnp.concatenate([b_mod, b_qv, b_out, b_fc1, b_fc2]), both, axis=0)
    pieces, start = [], 0
    for item in (b_mod, b_qv, b_out, b_fc1, b_fc2):
        pieces.append(biases[:, start : start + item.shape[0]].reshape(-1).astype(F32))
        start += item.shape[0]
    bias_mod, bias_qv, bias_out, bias_fc1, bias_fc2 = pieces
    bias_qv = lax.dynamic_index_in_dim(bias_qv.reshape(2, seq, part), my_seq, 1, keepdims=False)
    bias_fc1 = lax.dynamic_index_in_dim(
        bias_fc1.reshape(dp, seq, units), my_seq, 1, keepdims=False
    ).reshape(-1)
    modulation = (mod_sum + bias_mod).reshape(count, 6, 1, width)
    shift_att, scale_att, gate_att, shift_mlp, scale_mlp, gate_mlp = [
        modulation[:, index] for index in range(6)
    ]

    qkv_blocks = w_qkv.reshape(rows, 3, seq, part).transpose(2, 0, 1, 3).reshape(seq, rows, -1)
    fc1_blocks = w_fc1.reshape(rows, dp, seq, units).transpose(2, 0, 1, 3).reshape(seq, rows, -1)

    def to_columns(blocks):
        mine = lax.all_to_all(blocks, "seq", 0, 0, tiled=True).reshape(seq * rows, -1)
        return lax.all_gather(mine, "dp", axis=0, tiled=True)

    full_qkv = to_columns(qkv_blocks)
    full_out = lax.all_gather(w_out, both, axis=0, tiled=True)
    full_fc1 = to_columns(fc1_blocks)
    full_fc2 = lax.all_gather(w_fc2, "dp", axis=0, tiled=True)

    def gather_tokens(values):
        return lax.all_gather(values, "seq", axis=1, tiled=True)

    def flat(values):
        return values.reshape(-1, values.shape[-1])

    tokens_f = latents.astype(F32)
    normed, inverse = layer_norm(tokens_f)
    modded = (normed * (1.0 + scale_att) + shift_att).astype(BF16)
    modded_all = flat(gather_tokens(modded))
    joined = dot(modded_all, full_qkv).reshape(count, length, 3, heads, HEAD_DIM)
    bias_q = bias_qv[0].reshape(heads, HEAD_DIM)
    bias_v = bias_qv[1].reshape(heads, HEAD_DIM)
    queries = (joined[:, :, 0] + bias_q).astype(BF16)
    keys = joined[:, :, 1].astype(BF16)
    values = (joined[:, :, 2] + bias_v).astype(BF16)
    scores = jnp.einsum("bqhd,bkhd->bhqk", queries, keys, preferred_element_type=F32) * (
        HEAD_DIM ** (-0.5)
    )
    soft = jax.nn.softmax(scores, axis=-1)
    soft_low = soft.astype(BF16)
    mixed = jnp.einsum("bhqk,bkhd->bqhd", soft_low, values, preferred_element_type=F32)
    mixed = mixed.astype(BF16).reshape(count, length, part)
    mixed_mine = lax.all_to_all(mixed, "seq", 1, 2, tiled=True)
    attended = dot(mixed_mine, full_out) + bias_out
    middle = tokens_f + gate_att * attended
    normed_two, inverse_two = layer_norm(middle)
    modded_two = (normed_two * (1.0 + scale_mlp) + shift_mlp).astype(BF16)
    modded_two_all = flat(gather_tokens(modded_two))
    hidden = dot(modded_two_all, full_fc1) + bias_fc1
    active, gelu_back = jax.vjp(partial(jax.nn.gelu, approximate=True), hidden)
    active = active.astype(BF16)

    def sum_tokens(partial_sums):
        parts = partial_sums.astype(BF16).reshape(count, length, width)
        return lax.psum_scatter(parts, "seq", scatter_dimension=1, tiled=True).astype(F32)

    branch = sum_tokens(dot(active, full_fc2)) + bias_fc2
    output = middle + gate_mlp * branch

    grad_output = out_grad.astype(F32)
    grad_gate_mlp = jnp.sum(grad_output * branch, axis=1)
    grad_branch = (gate_mlp * grad_output).astype(BF16)
    grad_branch_all = flat(gather_tokens(grad_branch))
    grad_hidden = gelu_back(dot_right_t(grad_branch_all, full_fc2))[0].astype(BF16)
    grad_modded_two = sum_tokens(dot_right_t(grad_hidden, full_fc1))
    grad_shift_mlp = jnp.sum(grad_modded_two, axis=1)
    grad_scale_mlp = jnp.sum(grad_modded_two * normed_two, axis=1)
    grad_middle = grad_output + norm_back(
        grad_modded_two * (1.0 + scale_mlp), normed_two, inverse_two
    )
    grad_gate_att = jnp.sum(grad_middle * attended, axis=1)
    grad_attended = (gate_att * grad_middle).astype(BF16)
    grad_mixed = dot_right_t(flat(grad_attended), full_out).astype(BF16)
    grad_mixed = lax.all_to_all(grad_mixed.reshape(latents.shape), "seq", 2, 1, tiled=True)
    grad_mixed = grad_mixed.reshape(count, length, heads, HEAD_DIM)
    grad_soft = jnp.einsum("bqhd,bkhd->bhqk", grad_mixed, values, preferred_element_type=F32)
    delta = jnp.sum(soft * grad_soft, axis=-1, keepdims=True)
    grad_scores = (soft * (grad_soft - delta)).astype(BF16)
    scale = HEAD_DIM ** (-0.5)
    grad_q = jnp.einsum("bhqk,bkhd->bqhd", grad_scores, keys, preferred_element_type=F32) * scale
    grad_k = jnp.einsum("bhqk,bqhd->bkhd", grad_scores, queries, preferred_element_type=F32) * scale
    grad_v = jnp.einsum("bhqk,bqhd->bkhd", soft_low, grad_mixed, preferred_element_type=F32)
    grad_joined = jnp.concatenate(
        [item.astype(BF16).reshape(count * length, part) for item in (grad_q, grad_k, grad_v)],
        axis=1,
    )
    grad_modded = sum_tokens(dot_right_t(grad_joined, full_qkv))
    grad_shift_att = jnp.sum(grad_modded, axis=1)
    grad_scale_att = jnp.sum(grad_modded * normed, axis=1)
    grad_tokens = grad_middle + norm_back(grad_modded * (1.0 + scale_att), normed, inverse)

    def from_columns(sums, groups):
        mine = lax.psum_scatter(sums.astype(BF16), "dp", scatter_dimension=0, tiled=True)
        blocks = lax.all_to_all(mine.reshape(seq, rows, -1), "seq", 0, 0, tiled=True)
        blocks = blocks.astype(F32).reshape(seq, rows, groups, -1)
        return blocks.transpose(1, 2, 0, 3).reshape(rows, -1)

    sums_fc2 = lax.psum_scatter(
        dot_left_t(active, grad_branch_all).astype(BF16), "dp", scatter_dimension=0, tiled=True
    ).astype(F32)
    sums_fc1 = from_columns(dot_left_t(modded_two_all, grad_hidden), dp)
    sums_out = lax.psum_scatter(
        dot_left_t(flat(mixed_mine), flat(grad_attended)).astype(BF16),
        both,
        scatter_dimension=0,
        tiled=True,
    ).astype(F32)
    sums_qkv = from_columns(dot_left_t(modded_all, grad_joined), 3)

    grad_mod = jnp.concatenate(
        [
            grad_shift_att,
            grad_scale_att,
            grad_gate_att,
            grad_shift_mlp,
            grad_scale_mlp,
            grad_gate_mlp,
        ],
        axis=1,
    )
    grad_mod = lax.psum(grad_mod, "seq").astype(BF16)
    grad_mod = lax.all_gather(grad_mod, "dp", axis=0, tiled=True)
    sums_mod = dot_left_t(cond_mine, grad_mod)
    own = b_mod.shape[0]
    sums_bias_mod = jnp.sum(
        lax.dynamic_slice_in_dim(grad_mod, me * own, own, axis=1).astype(F32), axis=0
    )
    grad_cond_act = lax.all_gather(dot_right_t(grad_mod, w_mod), both, axis=0)
    grad_cond_act = lax.dynamic_slice_in_dim(grad_cond_act, my_dp * count, count, axis=1)
    grad_cond = silu_back(grad_cond_act.transpose(1, 0, 2).reshape(count, width))[0]

    def spread(values, shape):
        blank = jnp.zeros(shape, F32)
        return lax.dynamic_update_slice_in_dim(blank, values, my_seq, 1).reshape(-1)

    joined_sums = jnp.sum(grad_joined.astype(F32), axis=0)
    qv_sums = jnp.stack([joined_sums[:part], joined_sums[2 * part :]])
    fc1_sums = jnp.sum(grad_hidden.astype(F32), axis=0)
    bias_sums = [
        spread(qv_sums.reshape(2, 1, part), (2, seq, part)),
        jnp.sum(flat(grad_attended).astype(F32), axis=0),
        spread(fc1_sums.reshape(dp, 1, units), (dp, seq, units)),
        jnp.sum(flat(grad_branch).astype(F32), axis=0),
    ]
    joint = jnp.concatenate([item.reshape(dp * seq, -1) for item in bias_sums], axis=1)
    joint = lax.psum_scatter(joint, both, scatter_dimension=0, tiled=True).reshape(-1)
    cuts = [b_qv.shape[0], b_out.shape[0], b_fc1.shape[0]]
    sums_bias_qv, sums_bias_out, sums_bias_fc1, sums_bias_fc2 = jnp.split(
        joint, [cuts[0], cuts[0] + cuts[1], sum(cuts)]
    )
    return (
        output.astype(BF16),
        grad_tokens.astype(BF16),
        grad_cond.astype(BF16),
        sums_mod,
        sums_bias_mod,
        sums_qkv,
        sums_bias_qv,
        sums_out,
        sums_bias_out,
        sums_fc1,
        sums_bias_fc1,
        sums_fc2,
        sums_bias_fc2,
    )


def solution(mesh):
    both = P(("dp", "seq"))
    wide = P(("dp", "seq"), None)
    tokens = P("dp", "seq", None)
    in_specs = (
        tokens,
        P("dp", None),
        wide,
        both,
        wide,
        both,
        wide,
        both,
        wide,
        both,
        wide,
        both,
        tokens,
    )
    out_specs = (tokens, tokens, P("dp", None)) + (wide, both) * 5
    return jax.shard_map(body, mesh=mesh, in_specs=in_specs, out_specs=out_specs, check_vma=False)
```

```python
from functools import partial
from types import SimpleNamespace
from typing import NamedTuple

import jax
import jax.numpy as jnp
from jax import lax
from jax.experimental import pallas as pl
from jax.experimental.pallas import tpu as pltpu
from jax.sharding import PartitionSpec as P

HEADS = 16
HEAD_DIM = 72
EPSILON = 1e-06
BF16 = jnp.bfloat16
F32 = jnp.float32


def layer_norm(values):
    center = values - jnp.mean(values, axis=-1, keepdims=True)
    inverse = lax.rsqrt(jnp.mean(center * center, axis=-1, keepdims=True) + EPSILON)
    return (center * inverse, inverse)


def norm_back(incoming, normed, inverse):
    return inverse * (
        incoming
        - jnp.mean(incoming, axis=-1, keepdims=True)
        - normed * jnp.mean(incoming * normed, axis=-1, keepdims=True)
    )


def dot(left, right):
    return jnp.dot(left, right, preferred_element_type=F32)


def dot_right_t(left, right):
    return lax.dot_general(left, right, (((1,), (1,)), ((), ())), preferred_element_type=F32)


def dot_left_t(left, right):
    return lax.dot_general(left, right, (((0,), (0,)), ((), ())), preferred_element_type=F32)


MESH = pl.DeviceIdType.MESH
ROOT = HEAD_DIM ** (-0.5)
LANES = 128
ROWS = 32


class Sizes:
    def __init__(self, dp, seq, latents, w_qkv, w_fc2):
        self.dp, self.seq, self.line = dp, seq, dp // 2
        self.count, self.tokens, self.width = latents.shape
        self.rows, self.units = w_qkv.shape[0], w_fc2.shape[0]
        self.chunk = seq * self.rows
        self.hidden = dp * self.units
        self.heads = HEADS // seq
        self.part = self.width // seq
        self.length = seq * self.tokens
        self.total = self.count * self.length
        self.own = self.count * self.tokens
        self.padded_rows = -(-self.rows // 16) * 16
        self.joined = -(-3 * self.part // LANES) * LANES
        self.mod_part = -(-6 * self.width // (seq * LANES)) * LANES

    def fits(self):
        return (
            self.seq == 4
            and self.dp % 2 == 0
            and self.dp == 8
            and self.count == 2
            and self.width == self.dp * self.chunk
            and self.chunk % 16 == 0
            and self.units % 16 == 0
            and self.tokens % 128 == 0
            and self.width % LANES == 0
            and self.hidden == self.width
            and self.chunk == self.units
        )


def column_cuts(width, most=512):
    cuts, start = [], 0
    while start < width:
        size = min(most, width - start)
        cuts.append((start, size))
        start += size
    return cuts


def one_hot(rows, columns, group, padded, flip):
    shape = (columns, rows) if flip else (rows, columns)
    tight = lax.broadcasted_iota(jnp.int32, shape, 1 if flip else 0)
    loose = lax.broadcasted_iota(jnp.int32, shape, 0 if flip else 1)
    hit = jnp.zeros(shape, F32)
    for index in range(rows // group):
        inside = (tight >= index * group) & (tight < (index + 1) * group)
        match = loose == tight + index * (padded - group)
        hit = jnp.where(inside & match, 1.0, hit)
    return hit.astype(BF16)


def block_kernel(sz, *refs):
    names = Inputs._fields + Outputs._fields + tuple(kernel_scratch(sz))
    r = SimpleNamespace(**dict(zip(names, refs)))
    dp_me, s_me = lax.axis_index("dp"), lax.axis_index("seq")
    z_me, x_me = dp_me // 2, dp_me % 2
    y_me, c_me = s_me // 2, s_me % 2
    count, tokens, width = sz.count, sz.tokens, sz.width
    line, seq = sz.line, sz.seq

    def seq_peer(mask):
        flip_y, flip_c = mask // 2, mask % 2
        y = 1 - y_me if flip_y else y_me
        c = 1 - c_me if flip_c else c_me
        return y * 2 + c

    def z_peer(step):
        return lax.rem(z_me + step, line)

    def device_seq(mask):
        return (dp_me, seq_peer(mask))

    def device_z(step):
        return (z_peer(step) * 2 + x_me, s_me)

    device_x = (z_me * 2 + (1 - x_me), s_me)
    used = [0, 0]

    def send(src, dst, device):
        index = used[0]
        used[0] += 1
        copy = pltpu.make_async_remote_copy(
            src_ref=src,
            dst_ref=dst,
            send_sem=r.send_sems.at[index],
            recv_sem=r.recv_sems.at[index],
            device_id=device,
            device_id_type=MESH,
        )
        copy.start()
        return copy

    def local(src, dst):
        index = used[1]
        used[1] += 1
        copy = pltpu.make_async_copy(src, dst, r.local_sems.at[index])
        copy.start()
        return copy

    def rows_of(ref, start, size):
        return ref.at[pl.ds(start, size)]

    peers = [device_seq(mask) for mask in (1, 2, 3)]
    peers += [device_z(step) for step in range(1, line)] + [device_x]
    barrier = pltpu.get_barrier_semaphore()
    for peer in peers:
        pl.semaphore_signal(barrier, inc=1, device_id=peer, device_id_type=MESH)
    pl.semaphore_wait(barrier, len(peers))

    pending = []
    far_moves = []
    sum_own = r.attended

    def release(copy):
        copy.wait_send()
        pending[:] = [item for item in pending if item is not copy]

    def token_rows(ref, latent, position):
        return rows_of(ref, (latent * seq + position) * tokens, tokens)

    class GatherTokens:
        def __init__(self, ref, latent, source=None):
            self.ref, self.latent = ref, latent
            slot = token_rows(ref, latent, s_me)
            mine = slot if source is None else source
            self.core = send(mine, slot, device_seq(1))
            self.chip = send(mine, slot, device_seq(2))

        def forward(self):
            self.chip.wait_recv()
            slot = token_rows(self.ref, self.latent, seq_peer(2))
            self.last = send(slot, slot, device_seq(1))

        def finish(self):
            self.core.wait_recv()
            self.last.wait_recv()
            for copy in (self.core, self.chip, self.last):
                pending.append(copy)

    class SumTokens:
        def __init__(self, part, slot, latent):
            self.part, self.slot, self.latent = part, slot, latent
            self.first = [
                send(
                    token_rows(part, latent, y * 2 + 1 - c_me),
                    r.sum_core.at[slot, y, latent],
                    device_seq(1),
                )
                for y in range(2)
            ]

        def forward(self):
            for copy in self.first:
                copy.wait_recv()
            other = 1 - y_me
            total = token_rows(self.part, self.latent, other * 2 + c_me)[...].astype(F32)
            total = total + r.sum_core[self.slot, other, self.latent].astype(F32)
            r.sum_send[self.slot, self.latent] = total.astype(BF16)
            self.last = send(
                r.sum_send.at[self.slot, self.latent],
                r.sum_chip.at[self.slot, self.latent],
                device_seq(2),
            )

        def finish(self):
            self.last.wait_recv()
            for copy in self.first + [self.last]:
                copy.wait_send()

        def rows(self, start):
            place = pl.ds((self.latent * seq + s_me) * tokens + start, ROWS)
            here = pl.ds(start, ROWS)
            total = self.part[place, :].astype(F32)
            total = total + r.sum_core[self.slot, y_me, self.latent, here, :].astype(F32)
            return total + r.sum_chip[self.slot, self.latent, here, :].astype(F32)

    def exchange(pick, place):
        return [send(pick(seq_peer(mask)), place(s_me), device_seq(mask)) for mask in (1, 2, 3)]

    def settle(copies):
        for copy in copies:
            copy.wait_recv()
        pending.extend(copies)

    class GatherWeights:
        def __init__(self, ref, chunk):
            self.ref, self.chunk = ref, chunk

        def slot(self, dp):
            return rows_of(self.ref, dp * self.chunk, self.chunk)

        def push(self, source=None):
            own = self.slot(dp_me)
            mine = own if source is None else source
            self.along = [send(mine, own, device_z(step)) for step in range(1, line)]
            self.across = [send(mine, own, device_x)]

        def forward(self):
            for step, copy in zip(range(1, line), self.along):
                copy.wait_recv()
                came = lax.rem(z_me + line - step, line) * 2 + x_me
                self.across.append(send(self.slot(came), self.slot(came), device_x))

        def finish(self):
            for copy in self.across:
                copy.wait_recv()

        def drain(self):
            for copy in self.along + self.across:
                copy.wait_send()

    class SumWeights:
        def __init__(self, ref, chunk, across_ref, along_ref, columns):
            self.ref, self.chunk, self.columns = ref, chunk, columns
            self.across_ref, self.along_ref = across_ref, along_ref

        def view(self, ref, index):
            return ref.at[index, :, pl.ds(0, self.columns)]

        def slot(self, dp):
            return rows_of(self.ref, dp * self.chunk, self.chunk)

        def push(self):
            self.across = []
            for step in range(line):
                z = lax.rem(z_me + step, line)
                self.across.append(
                    send(self.slot(z * 2 + 1 - x_me), self.view(self.across_ref, step), device_x)
                )

        def forward(self):
            self.along = []
            for step in list(range(1, line)) + [0]:
                self.across[step].wait_recv()
                z = lax.rem(z_me + step, line)
                slot = self.slot(z * 2 + x_me)
                total = slot[...].astype(F32) + self.view(self.across_ref, step)[...].astype(F32)
                if step:
                    slot[...] = total.astype(BF16)
                    self.along.append(send(slot, self.view(self.along_ref, step), device_z(step)))
                else:
                    sum_own[pl.ds(0, self.chunk), pl.ds(0, self.columns)] = total

        def finish(self):
            total = sum_own[pl.ds(0, self.chunk), pl.ds(0, self.columns)]
            for copy, step in zip(self.along, range(1, line)):
                copy.wait_recv()
                total = total + self.view(self.along_ref, step)[...].astype(F32)
            for copy in self.along + self.across:
                copy.wait_send()
            return total

    pad = sz.padded_rows
    qkv_blocks, fc1_blocks = r.qkv_blocks, r.fc1_blocks
    out_wide = sz.dp * pad
    out_mine = rows_of(r.out_blocks, s_me * out_wide, out_wide)

    cond = r.conditioning[...].astype(F32)
    gate_cond = 1.0 / (1.0 + jnp.exp(-cond))
    low_rows = jnp.concatenate([cond * gate_cond, jnp.zeros((16 - count, width), F32)], axis=0)
    rows_of(r.cond_all, dp_me * 16, 16)[...] = low_rows.astype(BF16)
    gather_cond = GatherWeights(r.cond_all, 16)
    gather_cond.push()
    qkv_moves = exchange(
        lambda peer: r.qkv_src.at[peer], lambda me: rows_of(qkv_blocks, me * pad, pad)
    )
    qkv_local = local(r.qkv_src.at[s_me], rows_of(qkv_blocks, s_me * pad, pad))
    lat_local, og_local = [
        [local(source.at[latent], token_rows(target, latent, s_me)) for latent in range(count)]
        for source, target in ((r.latents, r.lat_all), (r.out_grad, r.grad_branch))
    ]
    lat_moves = [
        GatherTokens(r.lat_all, latent, r.latents.at[latent]) for latent in range(count)
    ]
    fc1_local = local(r.fc1_src.at[s_me], rows_of(fc1_blocks, s_me * pad, pad))
    out_local = local(r.out_src, rows_of(out_mine, dp_me * pad, pad))
    fc2_local = local(r.fc2_src, rows_of(r.fc2, dp_me * sz.units, sz.units))

    def place(values, start, size):
        blank = jnp.zeros((1, size - values.shape[1]), F32)
        row = jnp.concatenate([values.astype(F32), blank], axis=1)
        return pltpu.roll(jnp.broadcast_to(row, (8, size)), start, 1)[0:1, :]

    def when(hit, values):
        return jnp.where(hit, values, jnp.zeros_like(values))

    me = dp_me * seq + s_me
    lengths = (6 * sz.rows, 2 * sz.rows, sz.rows, sz.units, sz.rows)
    starts = [sum(lengths[:index]) for index in range(len(lengths))]
    own_mod, own_qv, own_out, own_fc1, own_fc2 = [
        r.bias[:, start : start + size] for start, size in zip(starts, lengths)
    ]
    devices = sz.dp * seq
    half_way = devices // 2
    qv_row = place(own_qv, lax.rem(me, half_way) * (2 * sz.rows), width)
    fc1_row = place(own_fc1, dp_me * sz.units, width)
    bias_rows = [
        place(own_out, me * sz.rows, width),
        place(own_fc2, me * sz.rows, width),
        when(me < half_way, qv_row),
        when(me >= half_way, qv_row),
    ] + [when(s_me == position, fc1_row) for position in range(seq)]
    bias_rows.append(jnp.zeros((16 - len(bias_rows), width), F32))
    bias_mine = rows_of(r.bias_blocks, s_me * 16, 16)
    bias_mine[...] = jnp.concatenate(bias_rows, axis=0).astype(BF16)
    bias_moves = exchange(lambda peer: bias_mine, lambda me: rows_of(r.bias_blocks, me * 16, 16))

    tighten = one_hot(sz.chunk, seq * pad, sz.rows, pad, False)
    loosen = one_hot(sz.chunk, seq * pad, sz.rows, pad, True)
    gather_out = GatherWeights(out_mine, pad)
    gather_qkv = GatherWeights(r.qkv, sz.chunk)
    gather_fc1 = GatherWeights(r.fc1, sz.chunk)
    gather_fc2 = GatherWeights(r.fc2, sz.units)
    qkv_local.wait()
    settle(qkv_moves)
    rows_of(r.qkv, dp_me * sz.chunk, sz.chunk)[...] = dot(tighten, qkv_blocks[...]).astype(BF16)
    gather_qkv.push()

    gather_cond.forward()
    gather_cond.finish()
    iota = partial(lax.broadcasted_iota, jnp.int32)
    hit = iota((width, LANES), 0) == iota((width, LANES), 1) + me * sz.rows
    hit = hit & (iota((width, LANES), 1) < sz.rows)
    cond_mine = dot(r.cond_all[...], jnp.where(hit, 1.0, 0.0).astype(BF16)).astype(BF16)
    r.cond_mine[...] = cond_mine
    order = iota((16, sz.dp * 16), 0)
    across, along, which = order >> 3, (order >> 1) & (line - 1), order & 1
    hit = iota((16, sz.dp * 16), 1) == (along * 2 + across) * 16 + which
    cond_rows = dot(jnp.where(hit, 1.0, 0.0).astype(BF16), cond_mine).astype(BF16)
    cond_rows = cond_rows[:, : sz.rows]
    mod_wide = sz.mod_part * seq
    own_row = place(own_mod, me * (6 * sz.rows), mod_wide)
    for comp in range(6):
        here = slice(comp * width, (comp + 1) * width)
        r.mod_sums[:, here] = dot(cond_rows, r.w_mod[:, here]) + own_row[:, here]
    r.mod_sums[:, 6 * width :] = jnp.zeros((16, mod_wide - 6 * width), F32)

    def mod_part(position):
        return r.mod_sums.at[:, pl.ds(pl.multiple_of(position * sz.mod_part, LANES), sz.mod_part)]

    mod_core = [
        send(mod_part(y * 2 + 1 - c_me), r.mod_core.at[y], device_seq(1)) for y in range(2)
    ]
    for move in lat_moves:
        move.forward()
    fc1_moves = exchange(
        lambda peer: r.fc1_src.at[peer], lambda me: rows_of(fc1_blocks, me * pad, pad)
    )
    for copy in mod_core:
        copy.wait_recv()
    r.mod_send[...] = mod_part((1 - y_me) * 2 + c_me)[...] + r.mod_core[1 - y_me]
    mod_chip = send(r.mod_send, r.mod_chip, device_seq(2))
    settle(bias_moves)
    bias_sum = sum(
        r.bias_blocks[position * 16 : (position + 1) * 16, :].astype(F32) for position in range(seq)
    )
    rows_of(r.bias_all, dp_me * 16, 16)[...] = bias_sum.astype(BF16)
    gather_bias = GatherWeights(r.bias_all, 16)
    gather_bias.push()
    mod_chip.wait_recv()
    r.mod_sum[...] = mod_part(s_me)[...] + r.mod_core[y_me] + r.mod_chip[...]
    mod_x = send(rows_of(r.mod_sum, (1 - x_me) * 8, 8), r.mod_x, device_x)
    fc1_local.wait()
    settle(fc1_moves)
    rows_of(r.fc1, dp_me * sz.chunk, sz.chunk)[...] = dot(tighten, fc1_blocks[...]).astype(BF16)
    mod_x.wait_recv()
    r.mod_half[...] = rows_of(r.mod_sum, x_me * 8, 8)[...] + r.mod_x[...]
    mod_z = [send(r.mod_half, r.mod_z.at[step], device_z(step)) for step in range(1, line)]
    gather_bias.forward()
    gather_qkv.forward()
    gather_out.push(r.out_src)
    mod_total = r.mod_half[...]
    for copy, step in zip(mod_z, range(1, line)):
        copy.wait_recv()
        mod_total = mod_total + r.mod_z[step]
    hit = iota((8, sz.mod_part), 0)
    picked = [
        jnp.sum(jnp.where(hit == z_me * count + latent, mod_total, 0.0), axis=0, keepdims=True)
        for latent in range(count)
    ]
    picked.append(jnp.zeros((8 - count, sz.mod_part), F32))
    mod_slot = r.mod_all.at[s_me]
    mod_slot[...] = jnp.concatenate(picked, axis=0)
    mod_moves = [send(mod_slot, mod_slot, device_seq(mask)) for mask in (1, 2)]
    gather_out.forward()
    gather_fc1.push()
    og_moves = [
        GatherTokens(r.grad_branch, latent, r.out_grad.at[latent]) for latent in range(count)
    ]
    mod_moves[1].wait_recv()
    mod_slot = r.mod_all.at[seq_peer(2)]
    mod_moves.append(send(mod_slot, mod_slot, device_seq(1)))
    gather_bias.finish()
    bias = jnp.sum(r.bias_all[...].astype(F32).reshape(sz.dp, 16, width), axis=0)
    bias_out, bias_fc2 = bias[0:1, :], bias[1:2, :]
    part = sz.part

    def own_part(row):
        return sum(
            when(s_me == position, row[:, position * part : (position + 1) * part])
            for position in range(seq)
        )

    r.bias_joined[...] = jnp.concatenate(
        [
            own_part(bias[2:3, :]),
            jnp.zeros((1, part), F32),
            own_part(bias[3:4, :]),
            jnp.zeros((1, sz.joined - 3 * part), F32),
        ],
        axis=1,
    )
    r.bias_fc1[...] = sum(
        when(s_me == position, bias[4 + position : 5 + position, :]) for position in range(seq)
    )
    r.bias_out[...] = bias_out
    r.bias_fc2[...] = bias_fc2
    mod_moves[0].wait_recv()
    mod_moves[2].wait_recv()
    wide = jnp.concatenate([r.mod_all[position] for position in range(seq)], axis=1)
    mod = r.modulation
    for latent in range(count):
        for comp in range(6):
            mod[latent, comp : comp + 1, :] = wide[
                latent : latent + 1, comp * width : (comp + 1) * width
            ]
    pending.extend(mod_core + [mod_chip, mod_x] + mod_z + mod_moves)

    for copy in lat_local:
        copy.wait()
    for move in lat_moves:
        move.finish()

    heads, length = sz.heads, sz.length

    def modulate_tokens(step, carry):
        latent = step // (length // ROWS)
        here = pl.ds(pl.multiple_of(step * ROWS, ROWS), ROWS)
        normed, _ = layer_norm(r.lat_all[here, :].astype(F32))
        shift, scale = mod[latent, 0:1, :], mod[latent, 1:2, :]
        r.modded[here, :] = (normed * (1.0 + scale) + shift).astype(BF16)
        return carry

    lax.fori_loop(0, count * length // ROWS, modulate_tokens, 0)

    out_local.wait()
    gather_out.finish()
    out_core = send(out_mine, out_mine, device_seq(1))
    out_chip = send(out_mine, out_mine, device_seq(2))

    gather_qkv.finish()
    tile = 2 * tokens
    per_latent = length // tile

    def pad_head(values):
        return jnp.concatenate(
            [values, jnp.zeros((values.shape[0], LANES - HEAD_DIM), values.dtype)], axis=1
        )

    def project(step, carry):
        start = pl.multiple_of(step * tile, tile)
        latent = step // per_latent
        row = pl.multiple_of((step % per_latent) * tile, tile)
        joined = dot(r.modded[pl.ds(start, tile), :], r.qkv[...]) + r.bias_joined[...]
        for kind, target in enumerate((r.q_heads, r.k_heads, r.v_heads)):
            for head in range(heads):
                column = kind * part + head * HEAD_DIM
                piece = pad_head(joined[:, column : column + HEAD_DIM]).astype(BF16)
                target[latent * heads + head, pl.ds(row, tile), :] = piece
        return carry

    lax.fori_loop(0, count * per_latent, project, 0)

    half = length // 2

    def attend(index, carry):
        keys, values = r.k_heads[index], r.v_heads[index]

        def rows(step, carry):
            here = pl.ds(pl.multiple_of(step * half, half), half)
            scores = dot_right_t(r.q_heads[index, here, :], keys) * ROOT
            expon = jnp.exp(scores - jnp.max(scores, axis=-1, keepdims=True))
            soft = (expon * (1.0 / jnp.sum(expon, axis=-1, keepdims=True))).astype(BF16)
            r.soft[index, here, :] = soft
            r.o_heads[index, here, :] = dot(soft, values).astype(BF16)
            return carry

        return lax.fori_loop(0, 2, rows, carry)

    mixed_moves = []
    for latent in range(count):
        lax.fori_loop(latent * heads, (latent + 1) * heads, attend, 0)

        def assemble(block, carry, latent=latent):
            row = pl.multiple_of(block * tokens, tokens)
            pieces = [
                r.o_heads[latent * heads + head, pl.ds(row, tokens), :][:, :HEAD_DIM]
                for head in range(heads)
            ]
            r.mixed_send[block, latent] = jnp.concatenate(pieces, axis=1)
            return carry

        lax.fori_loop(0, seq, assemble, 0)
        own = local(r.mixed_send.at[s_me, latent], r.mixed_recv.at[s_me, latent])
        mixed_moves.append(
            (
                own,
                exchange(
                    lambda peer, latent=latent: r.mixed_send.at[peer, latent],
                    lambda me, latent=latent: r.mixed_recv.at[me, latent],
                ),
            )
        )
        if latent == 0:
            out_chip.wait_recv()
            other = rows_of(r.out_blocks, seq_peer(2) * out_wide, out_wide)
            out_last = send(other, other, device_seq(1))
            for move in og_moves:
                move.forward()
    gather_fc1.forward()
    fc2_local.wait()
    gather_fc2.push()

    for copy in og_local:
        copy.wait()
    for move in og_moves:
        move.finish()
    for move in lat_moves + og_moves:
        release(move.last)

    def gate_grads(step, carry):
        here = pl.ds(pl.multiple_of(step * ROWS, ROWS), ROWS)
        gate = mod[step // (length // ROWS), 5:6, :]
        r.grad_branch[here, :] = (r.grad_branch[here, :].astype(F32) * gate).astype(BF16)
        return carry

    lax.fori_loop(0, count * length // ROWS, gate_grads, 0)

    out_core.wait_recv()
    out_last.wait_recv()
    pending.extend([out_core, out_chip, out_last])

    def tighten_out(step, carry):
        blocks = [
            r.out_blocks[pl.ds(pl.multiple_of(block * out_wide + step * pad, 16), pad), :]
            for block in range(seq)
        ]
        start = pl.multiple_of(step * sz.chunk, 16)
        packed = dot(tighten, jnp.concatenate(blocks, axis=0))
        r.out[pl.ds(start, sz.chunk), :] = packed.astype(BF16)
        return carry

    lax.fori_loop(0, sz.dp, tighten_out, 0)

    gather_fc1.finish()
    m2_moves = []
    for latent in range(count):
        own, moves = mixed_moves[latent]
        own.wait()
        settle(moves)
        pieces = [r.mixed_recv[block, latent] for block in range(seq)]
        mixed = jnp.concatenate(pieces, axis=1)
        here = pl.ds(latent * tokens, tokens)
        r.mixed[here, :] = mixed
        r.attended[here, :] = dot(mixed, r.out[...]) + r.bias_out[...]

        def second_norm(step, carry, latent=latent):
            start = pl.multiple_of(step * ROWS, ROWS)
            here = pl.ds(latent * tokens + start, ROWS)
            tokens_in = r.latents[latent, pl.ds(start, ROWS), :].astype(F32)
            middle = tokens_in + mod[latent, 2:3, :] * r.attended[here, :]
            r.middle[here, :] = middle
            normed, _ = layer_norm(middle)
            modded = normed * (1.0 + mod[latent, 4:5, :]) + mod[latent, 3:4, :]
            place = pl.multiple_of((latent * seq + s_me) * tokens + start, ROWS)
            r.modded_two[pl.ds(place, ROWS), :] = modded.astype(BF16)
            return carry

        lax.fori_loop(0, tokens // ROWS, second_norm, 0)
        m2_moves.append(GatherTokens(r.modded_two, latent))

    gather_fc2.forward()
    for move in m2_moves:
        move.forward()
    gather_fc2.finish()

    cuts = column_cuts(sz.hidden, 256)
    r.fc1_sums[...] = jnp.zeros_like(r.fc1_sums)
    grad_moves = []
    for latent in range(count):
        m2_moves[latent].finish()

        def mlp(step, carry, latent=latent):
            start = pl.multiple_of(latent * length + step * tile, tile)
            rows = r.modded_two[pl.ds(start, tile), :]
            incoming = r.grad_branch[pl.ds(start, tile), :]
            for column, size in cuts:
                here = slice(column, column + size)
                hidden = dot(rows, r.fc1[:, here]) + r.bias_fc1[:, here]
                square = hidden * hidden
                inner = 0.7978845608028654 * (hidden + 0.044715 * square * hidden)
                bent = jnp.tanh(inner)
                r.lat_all[pl.ds(start, tile), here] = (0.5 * hidden * (1.0 + bent)).astype(BF16)
                slope = 0.5 * (1.0 + bent) + 0.5 * hidden * (1.0 - bent * bent) * (
                    0.7978845608028654 * (1.0 + 3 * 0.044715 * square)
                )
                grads = (dot_right_t(incoming, r.fc2[here, :]) * slope).astype(BF16)
                r.grad_hidden[pl.ds(start, tile), here] = grads
                r.fc1_sums[:, here] += jnp.sum(grads.astype(F32), axis=0, keepdims=True)
            return carry

        lax.fori_loop(0, per_latent, mlp, 0)

        def back_fc1(step, carry, latent=latent):
            start = pl.multiple_of(latent * length + step * tile, tile)
            rows = r.grad_hidden[pl.ds(start, tile), :]
            for column, size in column_cuts(width):
                here = slice(column, column + size)
                sums = dot_right_t(rows, r.fc1[here, :])
                r.part_a[pl.ds(start, tile), here] = sums.astype(BF16)
            return carry

        lax.fori_loop(0, per_latent, back_fc1, 0)
        grad_moves.append(SumTokens(r.part_a, 0, latent))

    for copy in (out_core, out_chip, out_last):
        release(copy)
    gather_out.drain()
    for latent in range(count):

        def branch_out(step, carry, latent=latent):
            start = pl.multiple_of(latent * length + step * tile, tile)
            sums = dot(r.lat_all[pl.ds(start, tile), :], r.fc2[...])
            r.out_blocks[pl.ds(start, tile), :] = sums.astype(BF16)
            return carry

        lax.fori_loop(0, per_latent, branch_out, 0)
        grad_moves[latent].forward()

    gather_fc2.drain()

    def weight_grad(left, right, target):
        size = 384 if width % 384 == 0 else LANES

        def tiles(step, carry):
            start = pl.multiple_of(step * size, LANES)
            sums = dot_left_t(left[:, pl.ds(start, size)], right[...])
            target[pl.ds(start, size), :] = sums.astype(BF16)
            return carry

        lax.fori_loop(0, left.shape[1] // size, tiles, 0)

    weight_grad(r.lat_all, r.grad_branch, r.fc2)
    sum_fc2 = SumWeights(r.fc2, sz.units, r.across_b, r.along_b, width)
    sum_fc2.push()

    grad_mod = r.grad_mod
    grad_mod[...] = jnp.zeros_like(grad_mod)

    def total_rows(values):
        return jnp.sum(values, axis=0, keepdims=True)

    r.bias_sums[...] = jnp.zeros_like(r.bias_sums)
    mix_moves = []
    for latent in range(count):
        grad_moves[latent].finish()

        def second_back(step, carry, latent=latent):
            start = pl.multiple_of(step * ROWS, ROWS)
            here = pl.ds(latent * tokens + start, ROWS)
            incoming = grad_moves[latent].rows(start)
            normed, inverse = layer_norm(r.middle[here, :])
            grad_mod[latent, 3:4, :] += total_rows(incoming)
            grad_mod[latent, 4:5, :] += total_rows(incoming * normed)
            grad_middle = r.out_grad[latent, pl.ds(start, ROWS), :].astype(F32) + norm_back(
                incoming * (1.0 + mod[latent, 4:5, :]), normed, inverse
            )
            r.grad_middle[here, :] = grad_middle
            grad_mod[latent, 2:3, :] += total_rows(grad_middle * r.attended[here, :])
            grad_attended = (mod[latent, 2:3, :] * grad_middle).astype(BF16)
            r.grad_attended[here, :] = grad_attended
            r.bias_sums[0:1, :] += total_rows(grad_attended.astype(F32))
            return carry

        lax.fori_loop(0, tokens // ROWS, second_back, 0)
        here = pl.ds(latent * tokens, tokens)
        grad_mixed = dot_right_t(r.grad_attended[here, :], r.out[...])
        for copy in mixed_moves[latent][1]:
            release(copy)
        for block in range(seq):
            piece = grad_mixed[:, block * part : (block + 1) * part].astype(BF16)
            r.mixed_send[block, latent] = piece
        own = local(r.mixed_send.at[s_me, latent], r.mixed_recv.at[s_me, latent])
        mix_moves.append(
            (
                own,
                exchange(
                    lambda peer, latent=latent: r.mixed_send.at[peer, latent],
                    lambda me, latent=latent: r.mixed_recv.at[me, latent],
                ),
            )
        )

    branch_moves = [SumTokens(r.out_blocks, 1, latent) for latent in range(count)]

    gather_fc1.drain()
    weight_grad(r.modded_two, r.grad_hidden, r.fc1)
    sum_fc1 = SumWeights(r.fc1, sz.chunk, r.across_a, r.along_a, sz.hidden)
    sum_fc2.forward()
    sum_fc1.push()
    for move in branch_moves:
        move.forward()

    def attend_back(index, carry):
        queries, keys, values = r.q_heads[index], r.k_heads[index], r.v_heads[index]
        incoming = r.o_heads[index]
        r.v_heads[index] = dot_left_t(r.soft[index], incoming).astype(BF16)

        def rows(step, carry):
            here = pl.ds(pl.multiple_of(step * half, half), half)
            soft = r.soft[index, here, :].astype(F32)
            grad_soft = dot_right_t(r.o_heads[index, here, :], values)
            delta = jnp.sum(soft * grad_soft, axis=-1, keepdims=True)
            r.soft[index, here, :] = (soft * (grad_soft - delta)).astype(BF16)
            return carry

        lax.fori_loop(0, 2, rows, 0)
        r.q_heads[index] = (dot(r.soft[index], keys) * ROOT).astype(BF16)
        r.k_heads[index] = (dot_left_t(r.soft[index], queries) * ROOT).astype(BF16)
        return carry

    joined_sums = r.joined_sums
    grad_joined = r.grad_hidden.at[:, pl.ds(0, sz.joined)]
    joined_sums[...] = jnp.zeros_like(joined_sums)
    token_moves = []
    for latent in range(count):
        own, moves = mix_moves[latent]
        own.wait()
        settle(moves)

        def unpack(block, carry, latent=latent):
            row = pl.multiple_of(block * tokens, tokens)
            values = r.mixed_recv[block, latent]
            for head in range(heads):
                piece = pad_head(values[:, head * HEAD_DIM : (head + 1) * HEAD_DIM])
                r.o_heads[latent * heads + head, pl.ds(row, tokens), :] = piece
            return carry

        lax.fori_loop(0, seq, unpack, 0)
        lax.fori_loop(latent * heads, (latent + 1) * heads, attend_back, 0)

        def join(block, carry, latent=latent):
            row = pl.multiple_of(block * tokens, tokens)
            start = pl.multiple_of(latent * length + block * tokens, tokens)
            pieces = [
                source[latent * heads + head, pl.ds(row, tokens), :][:, :HEAD_DIM]
                for source in (r.q_heads, r.k_heads, r.v_heads)
                for head in range(heads)
            ]
            if sz.joined > 3 * part:
                pieces.append(jnp.zeros((tokens, sz.joined - 3 * part), BF16))
            values = jnp.concatenate(pieces, axis=1)
            joined_sums[...] += total_rows(values.astype(F32))
            grad_joined[pl.ds(start, tokens), :] = values
            return carry

        lax.fori_loop(0, seq, join, 0)

        def back_qkv(step, carry, latent=latent):
            start = pl.multiple_of(latent * length + step * tile, tile)
            rows = grad_joined[pl.ds(start, tile), :]
            for column, size in column_cuts(width):
                here = slice(column, column + size)
                sums = dot_right_t(rows, r.qkv[here, :])
                r.part_a[pl.ds(start, tile), here] = sums.astype(BF16)
            return carry

        lax.fori_loop(0, per_latent, back_qkv, 0)
        token_moves.append(SumTokens(r.part_a, 0, latent))
        if latent == 0:
            fc2_rows = rows_of(sum_own, 0, sz.units)
            fc2_rows[...] = sum_fc2.finish()
            local(fc2_rows, r.fc2_out).wait()
            sum_fc1.forward()

    gather_qkv.drain()
    weight_grad(r.modded, grad_joined, r.qkv)
    for move in token_moves:
        move.forward()

    sum_qkv = SumWeights(r.qkv, sz.chunk, r.across_b, r.along_b, sz.joined)
    sum_qkv.push()

    for move in m2_moves:
        for copy in (move.core, move.chip, move.last):
            release(copy)
    for latent in range(count):
        branch_moves[latent].finish()

        def final_output(step, carry, latent=latent):
            start = pl.multiple_of(step * ROWS, ROWS)
            here = pl.ds(latent * tokens + start, ROWS)
            branch = branch_moves[latent].rows(start) + r.bias_fc2[...]
            grad_output = r.out_grad[latent, pl.ds(start, ROWS), :].astype(F32)
            gate = mod[latent, 5:6, :]
            r.modded_two[here, :] = (r.middle[here, :] + gate * branch).astype(BF16)
            grad_mod[latent, 5:6, :] += total_rows(grad_output * branch)
            r.bias_sums[1:2, :] += total_rows((gate * grad_output).astype(BF16).astype(F32))
            return carry

        lax.fori_loop(0, tokens // ROWS, final_output, 0)
        slot = rows_of(r.modded_two, latent * tokens, tokens)
        far_moves.append(local(slot, r.output.at[latent]))
    for latent in range(count):
        token_moves[latent].finish()

        def final_grads(step, carry, latent=latent):
            start = pl.multiple_of(step * ROWS, ROWS)
            here = pl.ds(latent * tokens + start, ROWS)
            incoming = token_moves[latent].rows(start)
            normed, inverse = layer_norm(r.latents[latent, pl.ds(start, ROWS), :].astype(F32))
            grad_mod[latent, 0:1, :] += total_rows(incoming)
            grad_mod[latent, 1:2, :] += total_rows(incoming * normed)
            grads = r.grad_middle[here, :] + norm_back(
                incoming * (1.0 + mod[latent, 1:2, :]), normed, inverse
            )
            place = pl.ds((count + latent) * tokens + start, ROWS)
            r.modded_two[place, :] = grads.astype(BF16)
            return carry

        lax.fori_loop(0, tokens // ROWS, final_grads, 0)
        slot = rows_of(r.modded_two, (count + latent) * tokens, tokens)
        far_moves.append(local(slot, r.latents_grad.at[latent]))

    weight_grad(r.mixed, r.grad_attended, r.out)

    def loosen_out(step, carry):
        start = pl.multiple_of(step * sz.chunk, 16)
        spread = dot(loosen, r.out[pl.ds(start, sz.chunk), :]).astype(BF16)
        for block in range(seq):
            place = pl.multiple_of(block * out_wide + step * pad, 16)
            r.out_blocks[pl.ds(place, pad), :] = spread[block * pad : (block + 1) * pad, :]
        return carry

    lax.fori_loop(0, sz.dp, loosen_out, 0)
    out_first = [
        send(
            rows_of(r.out_blocks, (y * 2 + 1 - c_me) * out_wide, out_wide),
            rows_of(r.lat_all, y * out_wide, out_wide),
            device_seq(1),
        )
        for y in range(2)
    ]

    def return_rows(total, send_ref, recv_ref):
        send_ref[...] = dot(loosen, total.astype(BF16)).astype(BF16)
        mine = rows_of(send_ref, s_me * pad, pad)
        own = local(mine, rows_of(recv_ref, s_me * pad, pad))
        moves = exchange(
            lambda peer: rows_of(send_ref, peer * pad, pad),
            lambda me: rows_of(recv_ref, me * pad, pad),
        )
        return own, moves

    def small(values):
        return values.reshape(count * 8, width)

    r.grad_core_send[...] = small(grad_mod[...])
    mod_core = send(r.grad_core_send, r.grad_core, device_seq(1))

    def own_place(sums, column):
        return place(sums[:, column : column + part], s_me * part, width)

    sums = joined_sums[...]
    r.bias_sums[2:3, :] = own_place(sums, 0)
    r.bias_sums[3:4, :] = own_place(sums, 2 * part)
    for position in range(seq):
        r.bias_sums[4 + position : 5 + position, :] = when(s_me == position, r.fc1_sums[...])
    bias_x = send(r.bias_sums, r.bias_x, device_x)
    mod_core.wait_recv()
    r.grad_chip_send[...] = r.grad_core_send[...] + r.grad_core[...]
    mod_chip = send(r.grad_chip_send, r.grad_chip, device_seq(2))
    bias_x.wait_recv()
    r.bias_half[...] = r.bias_sums[...] + r.bias_x[...]
    bias_z = [send(r.bias_half, r.bias_z.at[step], device_z(step)) for step in range(1, line)]
    mod_chip.wait_recv()
    rows_of(r.grad_all, dp_me * 16, 16)[...] = (r.grad_chip_send[...] + r.grad_chip[...]).astype(
        BF16
    )
    gather_grad = GatherWeights(r.grad_all, 16)
    gather_grad.push()
    pending.extend([mod_core, bias_x, mod_chip] + bias_z)

    for copy in out_first:
        copy.wait_recv()

    def out_from_core(y):
        return rows_of(r.lat_all, y * out_wide, out_wide)[...].astype(F32)

    other = rows_of(r.out_blocks, ((1 - y_me) * 2 + c_me) * out_wide, out_wide)
    other[...] = (other[...].astype(F32) + out_from_core(1 - y_me)).astype(BF16)
    out_chip_sum = rows_of(r.grad_branch, 0, out_wide)
    out_second = send(other, out_chip_sum, device_seq(2))

    for copy in fc1_moves:
        release(copy)
    fc1_own, fc1_back = return_rows(sum_fc1.finish(), r.fc1_blocks, r.fc1_rows)
    sum_qkv.forward()
    gather_grad.forward()
    bias_total = r.bias_half[...]
    for copy, step in zip(bias_z, range(1, line)):
        copy.wait_recv()
        bias_total = bias_total + r.bias_z[step]
    r.bias_line[...] = bias_total
    bias_core = send(r.bias_line, r.bias_core, device_seq(1))

    out_second.wait_recv()
    mine = out_mine[...].astype(F32) + out_from_core(y_me)
    out_mine[...] = (mine + out_chip_sum[...].astype(F32)).astype(BF16)
    pending.extend(out_first + [out_second])
    sum_out = SumWeights(out_mine, pad, r.across_out, r.along_out, width)
    sum_out.push()

    gather_grad.finish()
    all_grads = r.grad_all[...]
    rows = sz.dp * 16
    comp_of = iota((rows, rows), 0) & 7
    source = (iota((rows, rows), 0) & ~15) + ((iota((rows, rows), 0) >> 3) & 1)
    spread = jnp.where(iota((rows, rows), 1) == source, 1.0, 0.0).astype(BF16)
    cond_spread = dot(spread, r.cond_mine[...])
    comp_of = iota((rows, LANES), 0) & 7
    cond_grads = jnp.zeros((rows, sz.rows), F32)
    mod_rows = r.mod_out.shape[0]
    for comp in range(6):
        here = slice(comp * width, (comp + 1) * width)
        chosen = jnp.where(comp_of == comp, cond_spread, 0.0).astype(BF16)
        place_rows = rows_of(r.grad_middle, comp * mod_rows, mod_rows)
        place_rows[...] = dot_left_t(chosen, all_grads)[:mod_rows, :]
        far_moves.append(local(place_rows, r.mod_out.at[:, pl.ds(comp * width, width)]))
        back = dot_right_t(all_grads, r.w_mod[:, here])
        cond_grads = cond_grads + jnp.where(comp_of[:, : sz.rows] == comp, back, 0.0)
    cond_grads = jnp.sum(cond_grads.reshape(rows // 8, 8, sz.rows), axis=1)
    blank = jnp.zeros((16, width - sz.rows), F32)
    cond_grads = pltpu.roll(jnp.concatenate([cond_grads, blank], axis=1), me * sz.rows, 1)
    keep = iota((8, 16), 0)
    hits = []
    for side in range(2):
        hits.append(
            sum(
                when(
                    iota((8, width), 0) == along * count + latent,
                    jnp.broadcast_to(
                        cond_grads[
                            (along * 2 + side) * count + latent : (along * 2 + side) * count
                            + latent
                            + 1,
                            :,
                        ],
                        (8, width),
                    ),
                )
                for along in range(line)
                for latent in range(count)
            )
        )
    r.cond_sides[0] = hits[0]
    r.cond_sides[1] = hits[1]
    cond_x = send(r.cond_sides.at[1 - x_me], r.cond_x, device_x)
    bias_core.wait_recv()
    r.bias_pair[...] = r.bias_line[...] + r.bias_core[...]
    bias_chip = send(r.bias_pair, r.bias_chip, device_seq(2))
    comp_rows = iota((8, rows), 0) == (iota((8, rows), 1) & 7)
    mod_bias = dot(jnp.where(comp_rows, 1.0, 0.0).astype(BF16), all_grads)
    cond_x.wait_recv()
    r.cond_half[...] = r.cond_sides[x_me] + r.cond_x[...]
    cond_z = [send(r.cond_half, r.cond_z.at[step], device_z(step)) for step in range(1, line)]
    bias_chip.wait_recv()
    bias_full = r.bias_pair[...] + r.bias_chip[...]

    def own_lanes(row, start):
        size = row.shape[1]
        turned = pltpu.roll(jnp.broadcast_to(row, (8, size)), lax.rem(size - start, size), 1)
        return turned[0:1, : 2 * LANES]

    qv_total = when(me < half_way, bias_full[2:3, :]) + when(me >= half_way, bias_full[3:4, :])
    fc1_total = sum(
        when(s_me == position, bias_full[4 + position : 5 + position, :])
        for position in range(seq)
    )
    first = me * (6 * sz.rows) // width
    comp_row = iota((8, width), 0)
    pair = [
        jnp.sum(jnp.where(comp_row == first + more, mod_bias, 0.0), axis=0, keepdims=True)
        for more in range(2)
    ]
    r.small_out[...] = jnp.concatenate(
        [
            own_lanes(bias_full[0:1, :], me * sz.rows),
            own_lanes(bias_full[1:2, :], me * sz.rows),
            own_lanes(qv_total, lax.rem(me, half_way) * (2 * sz.rows)),
            own_lanes(fc1_total, dp_me * sz.units),
            own_lanes(jnp.concatenate(pair, axis=1), me * (6 * sz.rows) - first * width),
            jnp.zeros((3, 2 * LANES), F32),
        ],
        axis=0,
    )
    for copy in qkv_moves:
        release(copy)
    qkv_own, qkv_back = return_rows(sum_qkv.finish(), r.qkv_blocks, r.qkv_rows)
    sum_out.forward()
    cond_total = r.cond_half[...]
    for copy, step in zip(cond_z, range(1, line)):
        copy.wait_recv()
        cond_total = cond_total + r.cond_z[step]
    r.cond_line[...] = cond_total
    cond_core = send(r.cond_line, r.cond_core, device_seq(1))
    r.out_out[...] = sum_out.finish()
    cond_core.wait_recv()
    r.cond_pair[...] = r.cond_line[...] + r.cond_core[...]
    cond_chip = send(r.cond_pair, r.cond_chip, device_seq(2))
    gather_grad.drain()
    gather_bias.drain()
    gather_cond.drain()
    cond_chip.wait_recv()
    cond_full = r.cond_pair[...] + r.cond_chip[...]
    picked = [
        jnp.sum(
            jnp.where(comp_row == z_me * count + latent, cond_full, 0.0), axis=0, keepdims=True
        )
        for latent in range(count)
    ]
    slope = gate_cond * (1.0 + cond * (1.0 - gate_cond))
    r.cond_grad[...] = (jnp.concatenate(picked, axis=0) * slope).astype(BF16)
    pending.extend([bias_core, bias_chip, cond_x, cond_core, cond_chip] + cond_z)
    for own, moves in ((fc1_own, fc1_back), (qkv_own, qkv_back)):
        own.wait()
        settle(moves)
    far_moves.append(local(r.fc1_rows, r.fc1_out))
    far_moves.append(local(r.qkv_rows, r.qkv_out))
    for copy in far_moves:
        copy.wait()
    for copy in pending:
        copy.wait_send()


class Inputs(NamedTuple):
    latents: object
    out_grad: object
    conditioning: object
    bias: object
    w_mod: object
    qkv_src: object
    fc1_src: object
    out_src: object
    fc2_src: object


class Outputs(NamedTuple):
    output: object
    latents_grad: object
    cond_grad: object
    mod_out: object
    small_out: object
    qkv_out: object
    out_out: object
    fc1_out: object
    fc2_out: object


def kernel_scratch(sz):
    low = lambda *shape: pltpu.VMEM(shape, BF16)
    full = lambda *shape: pltpu.VMEM(shape, F32)
    count, tokens, width, seq = sz.count, sz.tokens, sz.width, sz.seq
    pad, groups = sz.padded_rows, sz.count * sz.heads
    tall = sz.chunk if sz.chunk > sz.units else sz.units
    wide = max(sz.joined, sz.hidden, width)
    return dict(
        lat_all=low(sz.total, max(width, sz.hidden)),
        grad_branch=low(sz.total, width),
        modded=low(sz.total, width),
        q_heads=low(groups, sz.length, LANES),
        k_heads=low(groups, sz.length, LANES),
        v_heads=low(groups, sz.length, LANES),
        o_heads=low(groups, sz.length, LANES),
        soft=low(groups, sz.length, sz.length),
        mixed_send=low(seq, count, tokens, sz.part),
        mixed_recv=low(seq, count, tokens, sz.part),
        mixed=low(sz.own, width),
        attended=full(sz.own, width),
        middle=full(sz.own, width),
        grad_middle=full(sz.own, width),
        grad_attended=low(sz.own, width),
        modded_two=low(sz.total, width),
        grad_hidden=low(sz.total, sz.hidden),
        part_a=low(sz.total, width),
        sum_core=low(2, 2, count, tokens, width),
        sum_send=low(2, count, tokens, width),
        sum_chip=low(2, count, tokens, width),
        qkv_blocks=low(seq * pad, sz.joined),
        fc1_blocks=low(seq * pad, sz.hidden),
        qkv_rows=low(seq * pad, sz.joined),
        fc1_rows=low(seq * pad, sz.hidden),
        out_blocks=low(seq * sz.dp * pad, width),
        qkv=low(width, sz.joined),
        fc1=low(width, sz.hidden),
        fc2=low(sz.hidden, width),
        out=low(width, width),
        across_a=low(sz.line, sz.chunk, wide),
        along_a=low(sz.line, sz.chunk, wide),
        across_b=low(sz.line, tall, wide),
        along_b=low(sz.line, tall, wide),
        across_out=low(sz.line, pad, width),
        along_out=low(sz.line, pad, width),
        cond_all=low(sz.dp * 16, width),
        cond_mine=low(sz.dp * 16, LANES),
        bias_blocks=low(seq * 16, width),
        bias_all=low(sz.dp * 16, width),
        mod_sums=full(16, sz.mod_part * seq),
        mod_core=full(2, 16, sz.mod_part),
        mod_send=full(16, sz.mod_part),
        mod_chip=full(16, sz.mod_part),
        mod_sum=full(16, sz.mod_part),
        mod_x=full(8, sz.mod_part),
        mod_half=full(8, sz.mod_part),
        mod_z=full(sz.line, 8, sz.mod_part),
        mod_all=full(seq, 8, sz.mod_part),
        modulation=full(count, 8, width),
        bias_joined=full(1, sz.joined),
        bias_out=full(1, width),
        bias_fc1=full(1, width),
        bias_fc2=full(1, width),
        joined_sums=full(1, sz.joined),
        fc1_sums=full(1, sz.hidden),
        grad_mod=full(count, 8, width),
        grad_core_send=full(16, width),
        grad_core=full(16, width),
        grad_chip_send=full(16, width),
        grad_chip=full(16, width),
        grad_all=low(sz.dp * 16, width),
        bias_sums=full(8, width),
        bias_x=full(8, width),
        bias_half=full(8, width),
        bias_z=full(sz.line, 8, width),
        bias_line=full(8, width),
        bias_core=full(8, width),
        bias_pair=full(8, width),
        bias_chip=full(8, width),
        cond_sides=full(2, 8, width),
        cond_x=full(8, width),
        cond_half=full(8, width),
        cond_z=full(sz.line, 8, width),
        cond_line=full(8, width),
        cond_core=full(8, width),
        cond_pair=full(8, width),
        cond_chip=full(8, width),
        send_sems=pltpu.SemaphoreType.DMA((200,)),
        recv_sems=pltpu.SemaphoreType.DMA((200,)),
        local_sems=pltpu.SemaphoreType.DMA((40,)),
    )


def kernel_outputs(sz):
    low = lambda *shape: jax.ShapeDtypeStruct(shape, BF16)
    full = lambda *shape: jax.ShapeDtypeStruct(shape, F32)
    count, tokens, width, pad = sz.count, sz.tokens, sz.width, sz.padded_rows
    return [
        low(count, tokens, width),
        low(count, tokens, width),
        low(count, width),
        full(-(-sz.rows // 8) * 8, 6 * width),
        full(8, 2 * LANES),
        low(sz.seq * pad, sz.joined),
        full(pad, width),
        low(sz.seq * pad, sz.hidden),
        full(sz.units, width),
    ]


def run_kernel(sz, *operands):
    vmem = pl.BlockSpec(memory_space=pltpu.VMEM)
    far = pl.BlockSpec(memory_space=pl.ANY)
    outputs = kernel_outputs(sz)
    return pl.pallas_call(
        partial(block_kernel, sz),
        out_shape=outputs,
        in_specs=[vmem] * 5 + [far] * 4,
        out_specs=[far, far, vmem, far, vmem, far, vmem, far, far],
        scratch_shapes=list(kernel_scratch(sz).values()),
        compiler_params=pltpu.CompilerParams(
            collective_id=0, has_side_effects=True, vmem_limit_bytes=66584576
        ),
    )(*operands)


def general_path(
    latents, out_grad, modulation, blocks, w_out, w_fc2, bias_qv, bias_out, bias_fc1, bias_fc2
):
    count, tokens, width = latents.shape
    dp, seq = lax.axis_size("dp"), lax.axis_size("seq")
    both = ("dp", "seq")
    qkv_blocks, fc1_blocks = blocks
    rows = qkv_blocks.shape[1]
    part, heads, length = width // seq, HEADS // seq, seq * tokens
    shift_att, scale_att, gate_att, shift_mlp, scale_mlp, gate_mlp = [
        modulation[:, index : index + 1] for index in range(6)
    ]

    def to_columns(blocks):
        mine = lax.all_to_all(blocks, "seq", 0, 0, tiled=True).reshape(seq * rows, -1)
        return lax.all_gather(mine, "dp", axis=0, tiled=True)

    full_qkv = to_columns(qkv_blocks)
    full_out = lax.all_gather(w_out, both, axis=0, tiled=True)
    full_fc1 = to_columns(fc1_blocks)
    full_fc2 = lax.all_gather(w_fc2, "dp", axis=0, tiled=True)

    def gather_tokens(values):
        return lax.all_gather(values, "seq", axis=1, tiled=True)

    def flat(values):
        return values.reshape(-1, values.shape[-1])

    tokens_f = latents.astype(F32)
    normed, inverse = layer_norm(tokens_f)
    modded = (normed * (1.0 + scale_att) + shift_att).astype(BF16)
    modded_all = flat(gather_tokens(modded))
    joined = dot(modded_all, full_qkv).reshape(count, length, 3, heads, HEAD_DIM)
    bias_q = bias_qv[0].reshape(heads, HEAD_DIM)
    bias_v = bias_qv[1].reshape(heads, HEAD_DIM)
    queries = (joined[:, :, 0] + bias_q).astype(BF16)
    keys = joined[:, :, 1].astype(BF16)
    values = (joined[:, :, 2] + bias_v).astype(BF16)
    scores = jnp.einsum("bqhd,bkhd->bhqk", queries, keys, preferred_element_type=F32) * (
        HEAD_DIM ** (-0.5)
    )
    soft = jax.nn.softmax(scores, axis=-1)
    soft_low = soft.astype(BF16)
    mixed = jnp.einsum("bhqk,bkhd->bqhd", soft_low, values, preferred_element_type=F32)
    mixed = mixed.astype(BF16).reshape(count, length, part)
    mixed_mine = lax.all_to_all(mixed, "seq", 1, 2, tiled=True)
    attended = dot(mixed_mine, full_out) + bias_out
    middle = tokens_f + gate_att * attended
    normed_two, inverse_two = layer_norm(middle)
    modded_two = (normed_two * (1.0 + scale_mlp) + shift_mlp).astype(BF16)
    modded_two_all = flat(gather_tokens(modded_two))
    hidden = dot(modded_two_all, full_fc1) + bias_fc1
    active, gelu_back = jax.vjp(partial(jax.nn.gelu, approximate=True), hidden)
    active = active.astype(BF16)

    def sum_tokens(partial_sums):
        parts = partial_sums.astype(BF16).reshape(count, length, width)
        return lax.psum_scatter(parts, "seq", scatter_dimension=1, tiled=True).astype(F32)

    branch = sum_tokens(dot(active, full_fc2)) + bias_fc2
    output = middle + gate_mlp * branch

    grad_output = out_grad.astype(F32)
    grad_gate_mlp = jnp.sum(grad_output * branch, axis=1)
    grad_branch = (gate_mlp * grad_output).astype(BF16)
    grad_branch_all = flat(gather_tokens(grad_branch))
    grad_hidden = gelu_back(dot_right_t(grad_branch_all, full_fc2))[0].astype(BF16)
    grad_modded_two = sum_tokens(dot_right_t(grad_hidden, full_fc1))
    grad_shift_mlp = jnp.sum(grad_modded_two, axis=1)
    grad_scale_mlp = jnp.sum(grad_modded_two * normed_two, axis=1)
    grad_middle = grad_output + norm_back(
        grad_modded_two * (1.0 + scale_mlp), normed_two, inverse_two
    )
    grad_gate_att = jnp.sum(grad_middle * attended, axis=1)
    grad_attended = (gate_att * grad_middle).astype(BF16)
    grad_mixed = dot_right_t(flat(grad_attended), full_out).astype(BF16)
    grad_mixed = lax.all_to_all(grad_mixed.reshape(latents.shape), "seq", 2, 1, tiled=True)
    grad_mixed = grad_mixed.reshape(count, length, heads, HEAD_DIM)
    grad_soft = jnp.einsum("bqhd,bkhd->bhqk", grad_mixed, values, preferred_element_type=F32)
    delta = jnp.sum(soft * grad_soft, axis=-1, keepdims=True)
    grad_scores = (soft * (grad_soft - delta)).astype(BF16)
    scale = HEAD_DIM ** (-0.5)
    grad_q = jnp.einsum("bhqk,bkhd->bqhd", grad_scores, keys, preferred_element_type=F32) * scale
    grad_k = jnp.einsum("bhqk,bqhd->bkhd", grad_scores, queries, preferred_element_type=F32) * scale
    grad_v = jnp.einsum("bhqk,bqhd->bkhd", soft_low, grad_mixed, preferred_element_type=F32)
    grad_joined = jnp.concatenate(
        [item.astype(BF16).reshape(count * length, part) for item in (grad_q, grad_k, grad_v)],
        axis=1,
    )
    grad_modded = sum_tokens(dot_right_t(grad_joined, full_qkv))
    grad_shift_att = jnp.sum(grad_modded, axis=1)
    grad_scale_att = jnp.sum(grad_modded * normed, axis=1)
    grad_tokens = grad_middle + norm_back(grad_modded * (1.0 + scale_att), normed, inverse)

    def from_columns(sums, groups):
        mine = lax.psum_scatter(sums.astype(BF16), "dp", scatter_dimension=0, tiled=True)
        blocks = lax.all_to_all(mine.reshape(seq, rows, -1), "seq", 0, 0, tiled=True)
        blocks = blocks.astype(F32).reshape(seq, rows, groups, -1)
        return blocks.transpose(1, 2, 0, 3).reshape(rows, -1)

    sums_fc2 = lax.psum_scatter(
        dot_left_t(active, grad_branch_all).astype(BF16), "dp", scatter_dimension=0, tiled=True
    ).astype(F32)
    sums_fc1 = from_columns(dot_left_t(modded_two_all, grad_hidden), dp)
    sums_out = lax.psum_scatter(
        dot_left_t(flat(mixed_mine), flat(grad_attended)).astype(BF16),
        both,
        scatter_dimension=0,
        tiled=True,
    ).astype(F32)
    sums_qkv = from_columns(dot_left_t(modded_all, grad_joined), 3)

    grad_mod = jnp.stack(
        [
            grad_shift_att,
            grad_scale_att,
            grad_gate_att,
            grad_shift_mlp,
            grad_scale_mlp,
            grad_gate_mlp,
        ],
        axis=1,
    )
    bias_sums = [
        jnp.sum(item.astype(F32), axis=0)
        for item in (grad_joined, flat(grad_attended), grad_hidden, flat(grad_branch))
    ]
    weight_sums = [sums_qkv, sums_out, sums_fc1, sums_fc2]
    return output.astype(BF16), grad_tokens.astype(BF16), grad_mod, bias_sums, weight_sums


def kernel_path(sz, latents, conditioning, w_mod, w_qkv, w_out, w_fc1, w_fc2, biases, out_grad):
    more = sz.padded_rows - sz.rows
    gap = sz.joined - 3 * sz.part
    part, seq, pad, rows = sz.part, sz.seq, sz.padded_rows, sz.rows
    qkv_blocks, fc1_blocks = column_blocks(seq, sz.dp, w_qkv, w_fc1, sz.units)
    output, grad_tokens, grad_cond, sums_mod, small, sums_qkv, sums_out, sums_fc1, sums_fc2 = (
        run_kernel(
            sz,
            latents,
            out_grad,
            conditioning,
            jnp.concatenate(biases).reshape(1, -1),
            w_mod,
            jnp.pad(qkv_blocks, ((0, 0), (0, more), (0, gap))),
            jnp.pad(fc1_blocks, ((0, 0), (0, more), (0, 0))),
            jnp.pad(w_out, ((0, more), (0, 0))),
            w_fc2,
        )
    )

    def spread(sums, columns, groups):
        sums = sums.reshape(seq, pad, -1)[:, :rows, :columns].astype(F32)
        return sums.reshape(seq, rows, groups, -1).transpose(1, 2, 0, 3).reshape(rows, -1)

    return (
        output,
        grad_tokens,
        grad_cond,
        sums_mod[:rows],
        small[4, : 6 * rows],
        spread(sums_qkv, 3 * part, 3),
        small[2, : 2 * rows],
        sums_out[:rows],
        small[0, :rows],
        spread(sums_fc1, sz.hidden, sz.dp),
        small[3, : sz.units],
        sums_fc2,
        small[1, :rows],
    )


def column_blocks(seq, dp, w_qkv, w_fc1, units):
    rows = w_qkv.shape[0]
    qkv_blocks = w_qkv.reshape(rows, 3, seq, -1).transpose(2, 0, 1, 3).reshape(seq, rows, -1)
    fc1_blocks = w_fc1.reshape(rows, dp, seq, units).transpose(2, 0, 1, 3).reshape(seq, rows, -1)
    return qkv_blocks, fc1_blocks


def body(
    latents,
    conditioning,
    w_mod,
    b_mod,
    w_qkv,
    b_qv,
    w_out,
    b_out,
    w_fc1,
    b_fc1,
    w_fc2,
    b_fc2,
    out_grad,
):
    count, tokens, width = latents.shape
    dp, seq = lax.axis_size("dp"), lax.axis_size("seq")
    sz = Sizes(dp, seq, latents, w_qkv, w_fc2)
    if sz.fits():
        biases = (b_mod, b_qv, b_out, b_fc1, b_fc2)
        return kernel_path(
            sz, latents, conditioning, w_mod, w_qkv, w_out, w_fc1, w_fc2, biases, out_grad
        )
    both = ("dp", "seq")
    my_dp, my_seq = lax.axis_index("dp"), lax.axis_index("seq")
    me = my_dp * seq + my_seq
    rows, units = w_qkv.shape[0], w_fc2.shape[0]
    part = width // seq

    cond = conditioning.astype(F32)
    cond_act, silu_back = jax.vjp(jax.nn.silu, cond)
    cond_low = lax.all_gather(cond_act.astype(BF16), "dp", axis=0, tiled=True)
    cond_mine = lax.dynamic_slice_in_dim(cond_low, me * rows, rows, axis=1)
    mod_part = dot(cond_mine, w_mod)
    mod_sum = lax.psum(lax.psum_scatter(mod_part, "dp", scatter_dimension=0, tiled=True), "seq")
    biases = lax.all_gather(jnp.concatenate([b_mod, b_qv, b_out, b_fc1, b_fc2]), both, axis=0)
    pieces, start = [], 0
    for item in (b_mod, b_qv, b_out, b_fc1, b_fc2):
        pieces.append(biases[:, start : start + item.shape[0]].reshape(-1).astype(F32))
        start += item.shape[0]
    bias_mod, bias_qv, bias_out, bias_fc1, bias_fc2 = pieces
    bias_qv = lax.dynamic_index_in_dim(bias_qv.reshape(2, seq, part), my_seq, 1, keepdims=False)
    bias_fc1 = lax.dynamic_index_in_dim(
        bias_fc1.reshape(dp, seq, units), my_seq, 1, keepdims=False
    ).reshape(-1)
    modulation = (mod_sum + bias_mod).reshape(count, 6, width)

    blocks = column_blocks(seq, dp, w_qkv, w_fc1, units)
    output, grad_tokens, grad_mod, bias_sums, weight_sums = general_path(
        latents,
        out_grad,
        modulation,
        blocks,
        w_out,
        w_fc2,
        bias_qv,
        bias_out,
        bias_fc1,
        bias_fc2,
    )
    sums_qkv, sums_out, sums_fc1, sums_fc2 = weight_sums

    grad_mod = grad_mod.reshape(count, -1)
    grad_mod = lax.psum(grad_mod, "seq").astype(BF16)
    grad_mod = lax.all_gather(grad_mod, "dp", axis=0, tiled=True)
    sums_mod = dot_left_t(cond_mine, grad_mod)
    own = b_mod.shape[0]
    sums_bias_mod = jnp.sum(
        lax.dynamic_slice_in_dim(grad_mod, me * own, own, axis=1).astype(F32), axis=0
    )
    grad_cond_act = lax.all_gather(dot_right_t(grad_mod, w_mod), both, axis=0)
    grad_cond_act = lax.dynamic_slice_in_dim(grad_cond_act, my_dp * count, count, axis=1)
    grad_cond = silu_back(grad_cond_act.transpose(1, 0, 2).reshape(count, width))[0]

    def spread(values, shape):
        blank = jnp.zeros(shape, F32)
        return lax.dynamic_update_slice_in_dim(blank, values, my_seq, 1).reshape(-1)

    joined_sums, out_sums, fc1_sums, fc2_sums = bias_sums
    qv_sums = jnp.stack([joined_sums[:part], joined_sums[2 * part : 3 * part]])
    bias_sums = [
        spread(qv_sums.reshape(2, 1, part), (2, seq, part)),
        out_sums,
        spread(fc1_sums.reshape(dp, 1, units), (dp, seq, units)),
        fc2_sums,
    ]
    joint = jnp.concatenate([item.reshape(dp * seq, -1) for item in bias_sums], axis=1)
    joint = lax.psum_scatter(joint, both, scatter_dimension=0, tiled=True).reshape(-1)
    cuts = [b_qv.shape[0], b_out.shape[0], b_fc1.shape[0]]
    sums_bias_qv, sums_bias_out, sums_bias_fc1, sums_bias_fc2 = jnp.split(
        joint, [cuts[0], cuts[0] + cuts[1], sum(cuts)]
    )
    return (
        output,
        grad_tokens,
        grad_cond.astype(BF16),
        sums_mod,
        sums_bias_mod,
        sums_qkv,
        sums_bias_qv,
        sums_out,
        sums_bias_out,
        sums_fc1,
        sums_bias_fc1,
        sums_fc2,
        sums_bias_fc2,
    )


def solution(mesh):
    both = P(("dp", "seq"))
    wide = P(("dp", "seq"), None)
    tokens = P("dp", "seq", None)
    in_specs = (
        tokens,
        P("dp", None),
        wide,
        both,
        wide,
        both,
        wide,
        both,
        wide,
        both,
        wide,
        both,
        tokens,
    )
    out_specs = (tokens, tokens, P("dp", None)) + (wide, both) * 5
    return jax.shard_map(body, mesh=mesh, in_specs=in_specs, out_specs=out_specs, check_vma=False)
```

```python
from functools import partial
from types import SimpleNamespace
from typing import NamedTuple

import jax
import jax.numpy as jnp
from jax import lax
from jax.experimental import pallas as pl
from jax.experimental.pallas import tpu as pltpu
from jax.sharding import PartitionSpec as P

HEADS = 16
HEAD_DIM = 72
EPSILON = 1e-06
BF16 = jnp.bfloat16
F32 = jnp.float32


def layer_norm(values):
    center = values - jnp.mean(values, axis=-1, keepdims=True)
    inverse = lax.rsqrt(jnp.mean(center * center, axis=-1, keepdims=True) + EPSILON)
    return (center * inverse, inverse)


def norm_back(incoming, normed, inverse):
    return inverse * (
        incoming
        - jnp.mean(incoming, axis=-1, keepdims=True)
        - normed * jnp.mean(incoming * normed, axis=-1, keepdims=True)
    )


def dot(left, right):
    return jnp.dot(left, right, preferred_element_type=F32)


def dot_right_t(left, right):
    return lax.dot_general(left, right, (((1,), (1,)), ((), ())), preferred_element_type=F32)


def dot_left_t(left, right):
    return lax.dot_general(left, right, (((0,), (0,)), ((), ())), preferred_element_type=F32)


MESH = pl.DeviceIdType.MESH
ROOT = HEAD_DIM ** (-0.5)
LANES = 128
ROWS = 32


class Sizes:
    def __init__(self, dp, seq, latents, w_qkv, w_fc2):
        self.dp, self.seq, self.line = dp, seq, dp // 2
        self.count, self.tokens, self.width = latents.shape
        self.rows, self.units = w_qkv.shape[0], w_fc2.shape[0]
        self.chunk = seq * self.rows
        self.hidden = dp * self.units
        self.heads = HEADS // seq
        self.part = self.width // seq
        self.length = seq * self.tokens
        self.total = self.count * self.length
        self.own = self.count * self.tokens
        self.padded_rows = -(-self.rows // 16) * 16
        self.joined = -(-3 * self.part // LANES) * LANES
        self.mod_part = -(-6 * self.width // (seq * LANES)) * LANES

    def fits(self):
        return (
            self.seq == 4
            and self.dp % 2 == 0
            and self.dp == 8
            and self.count == 2
            and self.width == self.dp * self.chunk
            and self.chunk % 16 == 0
            and self.units % 16 == 0
            and self.tokens % 128 == 0
            and self.width % LANES == 0
            and self.hidden == self.width
            and self.chunk == self.units
        )


def column_cuts(width, most=512):
    cuts, start = [], 0
    while start < width:
        size = min(most, width - start)
        cuts.append((start, size))
        start += size
    return cuts


def one_hot(rows, columns, group, padded, flip):
    shape = (columns, rows) if flip else (rows, columns)
    tight = lax.broadcasted_iota(jnp.int32, shape, 1 if flip else 0)
    loose = lax.broadcasted_iota(jnp.int32, shape, 0 if flip else 1)
    hit = jnp.zeros(shape, F32)
    for index in range(rows // group):
        inside = (tight >= index * group) & (tight < (index + 1) * group)
        match = loose == tight + index * (padded - group)
        hit = jnp.where(inside & match, 1.0, hit)
    return hit.astype(BF16)


def block_kernel(sz, *refs):
    names = Inputs._fields + Outputs._fields + tuple(kernel_scratch(sz))
    r = SimpleNamespace(**dict(zip(names, refs)))
    dp_me, s_me = lax.axis_index("dp"), lax.axis_index("seq")
    z_me, x_me = dp_me // 2, dp_me % 2
    y_me, c_me = s_me // 2, s_me % 2
    count, tokens, width = sz.count, sz.tokens, sz.width
    line, seq = sz.line, sz.seq

    def seq_peer(mask):
        flip_y, flip_c = mask // 2, mask % 2
        y = 1 - y_me if flip_y else y_me
        c = 1 - c_me if flip_c else c_me
        return y * 2 + c

    def z_peer(step):
        return lax.rem(z_me + step, line)

    def device_seq(mask):
        return (dp_me, seq_peer(mask))

    def device_z(step):
        return (z_peer(step) * 2 + x_me, s_me)

    inner = z_me % 3 != 0
    outer = z_me % 3 == 0

    def z_flip(mask):
        return (z_me, z_me + 1 - 2 * (z_me % 2), lax.rem(z_me + 2, line), line - 1 - z_me)[mask]

    def device_flip(mask):
        return (z_flip(mask) * 2 + x_me, s_me)

    device_x = (z_me * 2 + (1 - x_me), s_me)
    used = [0, 0]

    def copy_to(src, dst, device, arrival=None):
        index = used[0]
        used[0] += 1
        return pltpu.make_async_remote_copy(
            src_ref=src,
            dst_ref=dst,
            send_sem=r.send_sems.at[index],
            recv_sem=r.recv_sems.at[index] if arrival is None else arrival,
            device_id=device,
            device_id_type=MESH,
        )

    def send(src, dst, device, arrival=None):
        copy = copy_to(src, dst, device, arrival)
        copy.start()
        return copy

    def local(src, dst):
        index = used[1]
        used[1] += 1
        copy = pltpu.make_async_copy(src, dst, r.local_sems.at[index])
        copy.start()
        return copy

    def rows_of(ref, start, size):
        return ref.at[pl.ds(start, size)]

    peers = [device_seq(mask) for mask in (1, 2, 3)]
    peers += [device_z(step) for step in range(1, line)] + [device_x]
    barrier = pltpu.get_barrier_semaphore()
    for peer in peers:
        pl.semaphore_signal(barrier, inc=1, device_id=peer, device_id_type=MESH)
    pl.semaphore_wait(barrier, len(peers))

    pending = []
    far_moves = []

    def release(copy):
        copy.wait_send()
        pending[:] = [item for item in pending if item is not copy]

    def token_rows(ref, latent, position):
        return rows_of(ref, (latent * seq + position) * tokens, tokens)

    class GatherTokens:
        def __init__(self, ref, latent, source=None):
            self.ref, self.latent = ref, latent
            slot = token_rows(ref, latent, s_me)
            mine = slot if source is None else source
            self.core = send(mine, slot, device_seq(1))
            self.chip = send(mine, slot, device_seq(2))

        def forward(self):
            self.chip.wait_recv()
            slot = token_rows(self.ref, self.latent, seq_peer(2))
            self.last = send(slot, slot, device_seq(1))

        def finish(self):
            self.core.wait_recv()
            self.last.wait_recv()
            for copy in (self.core, self.chip, self.last):
                pending.append(copy)

    class SumTokens:
        def __init__(self, part, slot, latent):
            self.part, self.slot, self.latent = part, slot, latent
            self.first = [
                send(
                    token_rows(part, latent, y * 2 + 1 - c_me),
                    r.sum_core.at[slot, y, latent],
                    device_seq(1),
                )
                for y in range(2)
            ]

        def forward(self):
            for copy in self.first:
                copy.wait_recv()
            other = 1 - y_me
            total = token_rows(self.part, self.latent, other * 2 + c_me)[...].astype(F32)
            total = total + r.sum_core[self.slot, other, self.latent].astype(F32)
            r.sum_send[self.slot, self.latent] = total.astype(BF16)
            self.last = send(
                r.sum_send.at[self.slot, self.latent],
                r.sum_chip.at[self.slot, self.latent],
                device_seq(2),
            )

        def finish(self):
            self.last.wait_recv()
            for copy in self.first + [self.last]:
                copy.wait_send()

        def rows(self, start):
            place = pl.ds((self.latent * seq + s_me) * tokens + start, ROWS)
            here = pl.ds(start, ROWS)
            total = self.part[place, :].astype(F32)
            total = total + r.sum_core[self.slot, y_me, self.latent, here, :].astype(F32)
            return total + r.sum_chip[self.slot, self.latent, here, :].astype(F32)

    def exchange(pick, place):
        return [send(pick(seq_peer(mask)), place(s_me), device_seq(mask)) for mask in (1, 2, 3)]

    def settle(copies):
        for copy in copies:
            copy.wait_recv()
        pending.extend(copies)

    class GatherWeights:
        def __init__(self, ref, chunk):
            self.ref, self.chunk = ref, chunk

        def slot(self, dp):
            return rows_of(self.ref, dp * self.chunk, self.chunk)

        def push_along(self, source=None):
            own = self.slot(dp_me)
            mine = own if source is None else source
            self.along = [send(mine, own, device_flip(mask)) for mask in (2, 1)]
            self.arrival = r.recv_sems.at[used[0]]
            self.last = copy_to(mine, own, device_flip(3))
            pl.when(inner)(self.last.start)
            self.across, self.passed = [], 0

        def push_across(self, source=None):
            own = self.slot(dp_me)
            mine = own if source is None else source
            self.across.append(send(mine, own, device_x))

        def push(self, source=None):
            self.push_along(source)
            self.push_across(source)

        def forward(self, limit=3):
            for mask in (2, 1, 3)[self.passed :][:limit]:
                (self.along + [self.last])[self.passed].wait_recv()
                self.passed += 1
                came = self.slot(z_flip(mask) * 2 + x_me)
                if mask == 2:
                    self.relay = copy_to(came, came, device_flip(1), self.arrival)
                    pl.when(inner)(self.relay.start)
                self.across.append(send(came, came, device_x))

        def finish(self):
            for copy in self.across:
                copy.wait_recv()

        def drain(self):
            for copy in self.along + self.across:
                copy.wait_send()

            @pl.when(inner)
            def _():
                self.last.wait_send()
                self.relay.wait_send()

    class SumWeights:
        def __init__(self, ref, chunk, across_ref, along_ref, columns):
            self.ref, self.chunk, self.columns = ref, chunk, columns
            self.across_ref, self.along_ref = across_ref, along_ref
            self.across = {}

        def view(self, ref, index):
            return ref.at[index, :, pl.ds(0, self.columns)]

        def slot(self, dp):
            return rows_of(self.ref, dp * self.chunk, self.chunk)

        def push(self, masks=(3, 2, 1, 0)):
            if not self.across:
                self.across, self.passed = {}, []
            for mask in masks:
                self.across[mask] = send(
                    self.slot(z_flip(mask) * 2 + 1 - x_me),
                    self.view(self.across_ref, mask),
                    device_x,
                )

        def forward(self, limit=3):
            for mask in (3, 2, 1)[len(self.passed) :][:limit]:
                self.passed.append(mask)
                self.across[mask].wait_recv()
                slot = self.slot(z_flip(mask) * 2 + x_me)
                came = self.view(self.across_ref, mask)

                def total():
                    return slot[...].astype(F32) + came[...].astype(F32)

                extra = self.view(self.along_ref, 0)
                if mask == 3:
                    slot[...] = total().astype(BF16)
                    self.direct = copy_to(slot, self.view(self.along_ref, 3), device_flip(3))
                    self.relay = copy_to(slot, extra, device_flip(1))
                    pl.when(inner)(self.direct.start)
                    pl.when(outer)(self.relay.start)
                elif mask == 2:

                    @pl.when(inner)
                    def _():
                        self.relay.wait_recv()
                        slot[...] = (total() + extra[...].astype(F32)).astype(BF16)

                    @pl.when(outer)
                    def _():
                        slot[...] = total().astype(BF16)

                    self.two = send(slot, self.view(self.along_ref, 2), device_flip(2))
                else:
                    slot[...] = total().astype(BF16)
                    self.one = send(slot, self.view(self.along_ref, 1), device_flip(1))

        def finish(self, target):
            self.across[0].wait_recv()
            total = self.slot(dp_me)[...].astype(F32)
            total = total + self.view(self.across_ref, 0)[...].astype(F32)
            for copy, mask in ((self.one, 1), (self.two, 2)):
                copy.wait_recv()
                total = total + self.view(self.along_ref, mask)[...].astype(F32)
            target[...] = total

            @pl.when(inner)
            def _():
                self.direct.wait_recv()
                target[...] += self.view(self.along_ref, 3)[...].astype(F32)
                self.direct.wait_send()

            @pl.when(outer)
            def _():
                self.relay.wait_send()

            for copy in [self.one, self.two] + list(self.across.values()):
                copy.wait_send()

    pad = sz.padded_rows
    qkv_blocks, fc1_blocks = r.qkv_blocks, r.fc1_blocks
    out_wide = sz.dp * pad
    out_mine = rows_of(r.out_blocks, s_me * out_wide, out_wide)

    cond = r.conditioning[...].astype(F32)
    gate_cond = 1.0 / (1.0 + jnp.exp(-cond))
    low_rows = jnp.concatenate([cond * gate_cond, jnp.zeros((16 - count, width), F32)], axis=0)
    rows_of(r.cond_all, dp_me * 16, 16)[...] = low_rows.astype(BF16)
    gather_cond = GatherWeights(r.cond_all, 16)
    gather_cond.push()
    gather_out = GatherWeights(out_mine, pad)
    gather_out.push(r.out_src)
    qkv_local = local(r.qkv_src.at[s_me], rows_of(qkv_blocks, s_me * pad, pad))
    fc1_local = local(r.fc1_src.at[s_me], rows_of(fc1_blocks, s_me * pad, pad))
    lat_local, og_local = [
        [local(source.at[latent], token_rows(target, latent, s_me)) for latent in range(count)]
        for source, target in ((r.latents, r.lat_all), (r.out_grad, r.grad_branch))
    ]
    out_local = local(r.out_src, rows_of(out_mine, dp_me * pad, pad))
    fc2_local = local(r.fc2_src, rows_of(r.fc2, dp_me * sz.units, sz.units))

    def place(values, start, size):
        blank = jnp.zeros((1, size - values.shape[1]), F32)
        row = jnp.concatenate([values.astype(F32), blank], axis=1)
        return pltpu.roll(jnp.broadcast_to(row, (8, size)), start, 1)[0:1, :]

    def when(hit, values):
        return jnp.where(hit, values, jnp.zeros_like(values))

    me = dp_me * seq + s_me
    lengths = (6 * sz.rows, 2 * sz.rows, sz.rows, sz.units, sz.rows)
    starts = [sum(lengths[:index]) for index in range(len(lengths))]
    own_mod, own_qv, own_out, own_fc1, own_fc2 = [
        r.bias[:, start : start + size] for start, size in zip(starts, lengths)
    ]
    devices = sz.dp * seq
    half_way = devices // 2
    qv_row = place(own_qv, lax.rem(me, half_way) * (2 * sz.rows), width)
    fc1_row = place(own_fc1, dp_me * sz.units, width)
    bias_rows = [
        place(own_out, me * sz.rows, width),
        place(own_fc2, me * sz.rows, width),
        when(me < half_way, qv_row),
        when(me >= half_way, qv_row),
    ] + [when(s_me == position, fc1_row) for position in range(seq)]
    bias_rows.append(jnp.zeros((16 - len(bias_rows), width), F32))
    bias_mine = rows_of(r.bias_blocks, s_me * 16, 16)
    bias_mine[...] = jnp.concatenate(bias_rows, axis=0).astype(BF16)
    bias_moves = exchange(lambda peer: bias_mine, lambda me: rows_of(r.bias_blocks, me * 16, 16))
    qkv_moves = exchange(
        lambda peer: r.qkv_src.at[peer], lambda me: rows_of(qkv_blocks, me * pad, pad)
    )
    fc1_moves = exchange(
        lambda peer: r.fc1_src.at[peer], lambda me: rows_of(fc1_blocks, me * pad, pad)
    )
    lat_moves = [GatherTokens(r.lat_all, 0, r.latents.at[0])]

    tighten = one_hot(sz.chunk, seq * pad, sz.rows, pad, False)
    loosen = one_hot(sz.chunk, seq * pad, sz.rows, pad, True)
    gather_qkv = GatherWeights(r.qkv, sz.chunk)
    gather_fc1 = GatherWeights(r.fc1, sz.chunk)
    gather_fc2 = GatherWeights(r.fc2, sz.units)
    settle(bias_moves)
    bias_sum = sum(
        r.bias_blocks[position * 16 : (position + 1) * 16, :].astype(F32) for position in range(seq)
    )
    rows_of(r.bias_all, dp_me * 16, 16)[...] = bias_sum.astype(BF16)
    gather_bias = GatherWeights(r.bias_all, 16)
    gather_bias.push()
    gather_cond.forward()
    gather_out.forward(1)
    qkv_local.wait()
    settle(qkv_moves)
    rows_of(r.qkv, dp_me * sz.chunk, sz.chunk)[...] = dot(tighten, qkv_blocks[...]).astype(BF16)
    gather_qkv.push_along()

    gather_cond.finish()
    gather_qkv.push_across()
    iota = partial(lax.broadcasted_iota, jnp.int32)
    hit = iota((width, LANES), 0) == iota((width, LANES), 1) + me * sz.rows
    hit = hit & (iota((width, LANES), 1) < sz.rows)
    cond_mine = dot(r.cond_all[...], jnp.where(hit, 1.0, 0.0).astype(BF16)).astype(BF16)
    r.cond_mine[...] = cond_mine
    order = iota((16, sz.dp * 16), 0)
    across, along, which = order >> 3, (order >> 1) & (line - 1), order & 1
    hit = iota((16, sz.dp * 16), 1) == (along * 2 + across) * 16 + which
    cond_rows = dot(jnp.where(hit, 1.0, 0.0).astype(BF16), cond_mine).astype(BF16)
    cond_rows = cond_rows[:, : sz.rows]
    mod_wide = sz.mod_part * seq
    own_row = place(own_mod, me * (6 * sz.rows), mod_wide)
    for comp in range(6):
        here = slice(comp * width, (comp + 1) * width)
        r.mod_sums[:, here] = dot(cond_rows, r.w_mod[:, here]) + own_row[:, here]
    r.mod_sums[:, 6 * width :] = jnp.zeros((16, mod_wide - 6 * width), F32)

    def mod_part(position):
        return r.mod_sums.at[:, pl.ds(pl.multiple_of(position * sz.mod_part, LANES), sz.mod_part)]

    mod_core = [
        send(mod_part(y * 2 + 1 - c_me), r.mod_core.at[y], device_seq(1)) for y in range(2)
    ]
    gather_out.forward()
    fc1_local.wait()
    settle(fc1_moves)
    rows_of(r.fc1, dp_me * sz.chunk, sz.chunk)[...] = dot(tighten, fc1_blocks[...]).astype(BF16)
    for copy in mod_core:
        copy.wait_recv()
    r.mod_send[...] = mod_part((1 - y_me) * 2 + c_me)[...] + r.mod_core[1 - y_me]
    mod_chip = send(r.mod_send, r.mod_chip, device_seq(2))
    for latent in range(1, count):
        lat_moves.append(GatherTokens(r.lat_all, latent, r.latents.at[latent]))
    mod_chip.wait_recv()
    r.mod_sum[...] = mod_part(s_me)[...] + r.mod_core[y_me] + r.mod_chip[...]
    mod_x = send(rows_of(r.mod_sum, (1 - x_me) * 8, 8), r.mod_x, device_x)
    lat_moves[0].forward()
    gather_bias.forward(1)
    gather_qkv.forward(1)
    mod_x.wait_recv()
    r.mod_half[...] = rows_of(r.mod_sum, x_me * 8, 8)[...] + r.mod_x[...]
    mod_z = [send(r.mod_half, r.mod_z.at[step], device_z(step)) for step in range(1, line)]
    gather_fc1.push_along()
    gather_bias.forward()
    og_moves = [GatherTokens(r.grad_branch, 0, r.out_grad.at[0])]
    gather_fc1.push_across()
    gather_qkv.forward()
    for move in lat_moves[1:]:
        move.forward()
    out_local.wait()
    gather_out.finish()
    mod_total = r.mod_half[...]
    for copy, step in zip(mod_z, range(1, line)):
        copy.wait_recv()
        mod_total = mod_total + r.mod_z[step]
    hit = iota((8, sz.mod_part), 0)
    picked = [
        jnp.sum(jnp.where(hit == z_me * count + latent, mod_total, 0.0), axis=0, keepdims=True)
        for latent in range(count)
    ]
    picked.append(jnp.zeros((8 - count, sz.mod_part), F32))
    mod_slot = r.mod_all.at[s_me]
    mod_slot[...] = jnp.concatenate(picked, axis=0)
    mod_moves = [send(mod_slot, mod_slot, device_seq(mask)) for mask in (1, 2)]
    out_core = send(out_mine, out_mine, device_seq(1))
    out_chip = send(out_mine, out_mine, device_seq(2))
    mod_moves[1].wait_recv()
    mod_slot = r.mod_all.at[seq_peer(2)]
    mod_moves.append(send(mod_slot, mod_slot, device_seq(1)))
    gather_bias.finish()
    bias = jnp.sum(r.bias_all[...].astype(F32).reshape(sz.dp, 16, width), axis=0)
    bias_out, bias_fc2 = bias[0:1, :], bias[1:2, :]
    part = sz.part

    def own_part(row):
        return sum(
            when(s_me == position, row[:, position * part : (position + 1) * part])
            for position in range(seq)
        )

    r.bias_joined[...] = jnp.concatenate(
        [
            own_part(bias[2:3, :]),
            jnp.zeros((1, part), F32),
            own_part(bias[3:4, :]),
            jnp.zeros((1, sz.joined - 3 * part), F32),
        ],
        axis=1,
    )
    r.bias_fc1[...] = sum(
        when(s_me == position, bias[4 + position : 5 + position, :]) for position in range(seq)
    )
    r.bias_out[...] = bias_out
    r.bias_fc2[...] = bias_fc2
    mod_moves[0].wait_recv()
    mod_moves[2].wait_recv()
    wide = jnp.concatenate([r.mod_all[position] for position in range(seq)], axis=1)
    mod = r.modulation
    for latent in range(count):
        for comp in range(6):
            mod[latent, comp : comp + 1, :] = wide[
                latent : latent + 1, comp * width : (comp + 1) * width
            ]
    pending.extend(mod_core + [mod_chip, mod_x] + mod_z + mod_moves)
    gather_fc1.forward(1)
    fc2_local.wait()
    gather_fc2.push()

    for copy in lat_local:
        copy.wait()
    for move in lat_moves:
        move.finish()

    heads, length = sz.heads, sz.length

    def modulate_tokens(step, carry):
        latent = step // (length // ROWS)
        here = pl.ds(pl.multiple_of(step * ROWS, ROWS), ROWS)
        normed, _ = layer_norm(r.lat_all[here, :].astype(F32))
        shift, scale = mod[latent, 0:1, :], mod[latent, 1:2, :]
        r.modded[here, :] = (normed * (1.0 + scale) + shift).astype(BF16)
        return carry

    lax.fori_loop(0, count * length // ROWS, modulate_tokens, 0)

    gather_qkv.finish()
    tile = 2 * tokens
    per_latent = length // tile

    def pad_head(values):
        return jnp.concatenate(
            [values, jnp.zeros((values.shape[0], LANES - HEAD_DIM), values.dtype)], axis=1
        )

    def project(step, carry):
        start = pl.multiple_of(step * tile, tile)
        latent = step // per_latent
        row = pl.multiple_of((step % per_latent) * tile, tile)
        joined = dot(r.modded[pl.ds(start, tile), :], r.qkv[...]) + r.bias_joined[...]
        for kind, target in enumerate((r.q_heads, r.k_heads, r.v_heads)):
            for head in range(heads):
                column = kind * part + head * HEAD_DIM
                piece = pad_head(joined[:, column : column + HEAD_DIM]).astype(BF16)
                target[latent * heads + head, pl.ds(row, tile), :] = piece
        return carry

    lax.fori_loop(0, count * per_latent, project, 0)
    gather_fc1.forward(1)

    half = length // 2

    def attend(index, carry):
        keys, values = r.k_heads[index], r.v_heads[index]

        def rows(step, carry):
            here = pl.ds(pl.multiple_of(step * half, half), half)
            scores = dot_right_t(r.q_heads[index, here, :], keys) * ROOT
            expon = jnp.exp(scores - jnp.max(scores, axis=-1, keepdims=True))
            soft = (expon * (1.0 / jnp.sum(expon, axis=-1, keepdims=True))).astype(BF16)
            r.soft[index, here, :] = soft
            r.o_heads[index, here, :] = dot(soft, values).astype(BF16)
            return carry

        return lax.fori_loop(0, 2, rows, carry)

    mixed_moves = []
    for latent in range(count):
        lax.fori_loop(latent * heads, (latent + 1) * heads, attend, 0)

        def assemble(block, carry, latent=latent):
            row = pl.multiple_of(block * tokens, tokens)
            pieces = [
                r.o_heads[latent * heads + head, pl.ds(row, tokens), :][:, :HEAD_DIM]
                for head in range(heads)
            ]
            r.mixed_send[block, latent] = jnp.concatenate(pieces, axis=1)
            return carry

        lax.fori_loop(0, seq, assemble, 0)
        own = local(r.mixed_send.at[s_me, latent], r.mixed_recv.at[s_me, latent])
        mixed_moves.append(
            (
                own,
                exchange(
                    lambda peer, latent=latent: r.mixed_send.at[peer, latent],
                    lambda me, latent=latent: r.mixed_recv.at[me, latent],
                ),
            )
        )
        if latent == 0:
            gather_fc1.forward()
            out_chip.wait_recv()
            other = rows_of(r.out_blocks, seq_peer(2) * out_wide, out_wide)
            out_last = send(other, other, device_seq(1))
    og_moves[0].forward()
    gather_fc2.forward(1)

    out_core.wait_recv()
    out_last.wait_recv()
    pending.extend([out_core, out_chip, out_last])

    def tighten_out(step, carry):
        blocks = [
            r.out_blocks[pl.ds(pl.multiple_of(block * out_wide + step * pad, 16), pad), :]
            for block in range(seq)
        ]
        start = pl.multiple_of(step * sz.chunk, 16)
        packed = dot(tighten, jnp.concatenate(blocks, axis=0))
        r.out[pl.ds(start, sz.chunk), :] = packed.astype(BF16)
        return carry

    lax.fori_loop(0, sz.dp, tighten_out, 0)

    m2_moves = []
    for latent in range(count):
        own, moves = mixed_moves[latent]
        own.wait()
        settle(moves)
        pieces = [r.mixed_recv[block, latent] for block in range(seq)]
        mixed = jnp.concatenate(pieces, axis=1)
        here = pl.ds(latent * tokens, tokens)
        r.mixed[here, :] = mixed
        r.attended[here, :] = dot(mixed, r.out[...]) + r.bias_out[...]

        def second_norm(step, carry, latent=latent):
            start = pl.multiple_of(step * ROWS, ROWS)
            here = pl.ds(latent * tokens + start, ROWS)
            tokens_in = r.latents[latent, pl.ds(start, ROWS), :].astype(F32)
            middle = tokens_in + mod[latent, 2:3, :] * r.attended[here, :]
            r.middle[here, :] = middle
            normed, _ = layer_norm(middle)
            modded = normed * (1.0 + mod[latent, 4:5, :]) + mod[latent, 3:4, :]
            place = pl.multiple_of((latent * seq + s_me) * tokens + start, ROWS)
            r.modded_two[pl.ds(place, ROWS), :] = modded.astype(BF16)
            return carry

        lax.fori_loop(0, tokens // ROWS, second_norm, 0)
        m2_moves.append(GatherTokens(r.modded_two, latent))

    for latent in range(1, count):
        og_moves.append(GatherTokens(r.grad_branch, latent, r.out_grad.at[latent]))
    gather_fc2.forward(1)
    for copy in og_local:
        copy.wait()
    for move in lat_moves:
        release(move.last)

    def gate_grads(step, carry):
        here = pl.ds(pl.multiple_of(step * ROWS, ROWS), ROWS)
        gate = mod[step // (length // ROWS), 5:6, :]
        r.grad_branch[here, :] = (r.grad_branch[here, :].astype(F32) * gate).astype(BF16)
        return carry

    def gate_latent(latent):
        og_moves[latent].finish()
        release(og_moves[latent].last)
        steps = length // ROWS
        lax.fori_loop(latent * steps, (latent + 1) * steps, gate_grads, 0)

    gate_latent(0)
    m2_moves[0].forward()
    gather_fc2.forward()

    cuts = column_cuts(sz.hidden, 256)
    gather_fc1.finish()
    for latent in range(count):
        m2_moves[latent].finish()

        def mlp(step, carry, latent=latent):
            start = pl.multiple_of(latent * length + step * tile, tile)
            rows = r.modded_two[pl.ds(start, tile), :]
            for column, size in cuts:
                here = slice(column, column + size)
                hidden = dot(rows, r.fc1[:, here]) + r.bias_fc1[:, here]
                square = hidden * hidden
                inner = 0.7978845608028654 * (hidden + 0.044715 * square * hidden)
                bent = jnp.tanh(inner)
                r.lat_all[pl.ds(start, tile), here] = (0.5 * hidden * (1.0 + bent)).astype(BF16)
                slope = 0.5 * (1.0 + bent) + 0.5 * hidden * (1.0 - bent * bent) * (
                    0.7978845608028654 * (1.0 + 3 * 0.044715 * square)
                )
                r.part_a[pl.ds(start, tile), here] = slope.astype(BF16)
            return carry

        lax.fori_loop(0, per_latent, mlp, 0)
        if latent + 1 < count:
            m2_moves[latent + 1].forward()

    for copy in (out_core, out_chip, out_last):
        release(copy)
    gather_out.drain()

    def weight_grad(left, right, target):
        size = 384 if width % 384 == 0 else LANES

        def tiles(step, carry):
            start = pl.multiple_of(step * size, LANES)
            sums = dot_left_t(left[:, pl.ds(start, size)], right[...])
            target[pl.ds(start, size), :] = sums.astype(BF16)
            return carry

        lax.fori_loop(0, left.shape[1] // size, tiles, 0)

    for latent in range(1, count):
        og_moves[latent].forward()
        gate_latent(latent)
    weight_grad(r.lat_all, r.grad_branch, r.out_blocks)
    sum_fc2 = SumWeights(r.out_blocks, sz.units, r.across_b, r.along_b, width)
    sum_fc2.push()

    gather_fc2.finish()
    r.fc1_sums[...] = jnp.zeros_like(r.fc1_sums)
    grad_moves = []
    for latent in range(count):

        def mlp_back(step, carry, latent=latent):
            start = pl.multiple_of(latent * length + step * tile, tile)
            incoming = r.grad_branch[pl.ds(start, tile), :]
            for column, size in cuts:
                here = slice(column, column + size)
                slope = r.part_a[pl.ds(start, tile), here].astype(F32)
                grads = (dot_right_t(incoming, r.fc2[here, :]) * slope).astype(BF16)
                r.grad_hidden[pl.ds(start, tile), here] = grads
                r.fc1_sums[:, here] += jnp.sum(grads.astype(F32), axis=0, keepdims=True)
            return carry

        lax.fori_loop(0, per_latent, mlp_back, 0)
        if latent:
            grad_moves[latent - 1].forward()

        def back_fc1(step, carry, latent=latent):
            start = pl.multiple_of(latent * length + step * tile, tile)
            rows = r.grad_hidden[pl.ds(start, tile), :]
            for column, size in column_cuts(width):
                here = slice(column, column + size)
                sums = dot_right_t(rows, r.fc1[here, :])
                r.part_a[pl.ds(start, tile), here] = sums.astype(BF16)
            return carry

        lax.fori_loop(0, per_latent, back_fc1, 0)
        grad_moves.append(SumTokens(r.part_a, 0, latent))

    for move in m2_moves:
        for copy in (move.core, move.chip, move.last):
            release(copy)
    gather_fc1.drain()
    grad_moves[-1].forward()
    weight_grad(r.modded_two, r.grad_hidden, r.fc1)
    sum_fc1 = SumWeights(r.fc1, sz.chunk, r.across_a, r.along_a, sz.hidden)
    sum_fc1.push()

    grad_mod = r.grad_mod
    grad_mod[...] = jnp.zeros_like(grad_mod)

    def total_rows(values):
        return jnp.sum(values, axis=0, keepdims=True)

    r.bias_sums[...] = jnp.zeros_like(r.bias_sums)
    mix_moves = []
    for latent in range(count):
        grad_moves[latent].finish()

        def second_back(step, carry, latent=latent):
            start = pl.multiple_of(step * ROWS, ROWS)
            here = pl.ds(latent * tokens + start, ROWS)
            incoming = grad_moves[latent].rows(start)
            normed, inverse = layer_norm(r.middle[here, :])
            grad_mod[latent, 3:4, :] += total_rows(incoming)
            grad_mod[latent, 4:5, :] += total_rows(incoming * normed)
            grad_middle = r.out_grad[latent, pl.ds(start, ROWS), :].astype(F32) + norm_back(
                incoming * (1.0 + mod[latent, 4:5, :]), normed, inverse
            )
            r.grad_middle[here, :] = grad_middle
            grad_mod[latent, 2:3, :] += total_rows(grad_middle * r.attended[here, :])
            grad_attended = (mod[latent, 2:3, :] * grad_middle).astype(BF16)
            r.grad_attended[here, :] = grad_attended
            r.bias_sums[0:1, :] += total_rows(grad_attended.astype(F32))
            return carry

        lax.fori_loop(0, tokens // ROWS, second_back, 0)
        sum_fc2.forward(1)
        here = pl.ds(latent * tokens, tokens)
        grad_mixed = dot_right_t(r.grad_attended[here, :], r.out[...])
        for copy in mixed_moves[latent][1]:
            release(copy)
        for block in range(seq):
            piece = grad_mixed[:, block * part : (block + 1) * part].astype(BF16)
            r.mixed_send[block, latent] = piece
        own = local(r.mixed_send.at[s_me, latent], r.mixed_recv.at[s_me, latent])
        mix_moves.append(
            (
                own,
                exchange(
                    lambda peer, latent=latent: r.mixed_send.at[peer, latent],
                    lambda me, latent=latent: r.mixed_recv.at[me, latent],
                ),
            )
        )

    gather_fc2.drain()
    branch_moves = []
    for latent in range(count):

        def branch_out(step, carry, latent=latent):
            start = pl.multiple_of(latent * length + step * tile, tile)
            sums = dot(r.lat_all[pl.ds(start, tile), :], r.fc2[...])
            r.lat_all[pl.ds(start, tile), :] = sums.astype(BF16)
            return carry

        lax.fori_loop(0, per_latent, branch_out, 0)
        branch_moves.append(SumTokens(r.lat_all, 1, latent))
    sum_fc2.forward()

    for move in branch_moves:
        move.forward()

    def attend_back(index, carry):
        queries, keys, values = r.q_heads[index], r.k_heads[index], r.v_heads[index]
        incoming = r.o_heads[index]
        r.v_heads[index] = dot_left_t(r.soft[index], incoming).astype(BF16)

        def rows(step, carry):
            here = pl.ds(pl.multiple_of(step * half, half), half)
            soft = r.soft[index, here, :].astype(F32)
            grad_soft = dot_right_t(r.o_heads[index, here, :], values)
            delta = jnp.sum(soft * grad_soft, axis=-1, keepdims=True)
            r.soft[index, here, :] = (soft * (grad_soft - delta)).astype(BF16)
            return carry

        lax.fori_loop(0, 2, rows, 0)
        r.q_heads[index] = (dot(r.soft[index], keys) * ROOT).astype(BF16)
        r.k_heads[index] = (dot_left_t(r.soft[index], queries) * ROOT).astype(BF16)
        return carry

    fc_rows = rows_of(r.attended, 0, sz.units)
    joined_sums = r.joined_sums
    grad_joined = r.grad_hidden.at[:, pl.ds(0, sz.joined)]
    joined_sums[...] = jnp.zeros_like(joined_sums)
    token_moves = []
    for latent in range(count):
        own, moves = mix_moves[latent]
        own.wait()
        settle(moves)

        def unpack(block, carry, latent=latent):
            row = pl.multiple_of(block * tokens, tokens)
            values = r.mixed_recv[block, latent]
            for head in range(heads):
                piece = pad_head(values[:, head * HEAD_DIM : (head + 1) * HEAD_DIM])
                r.o_heads[latent * heads + head, pl.ds(row, tokens), :] = piece
            return carry

        lax.fori_loop(0, seq, unpack, 0)
        middle_head = latent * heads + heads // 2
        lax.fori_loop(latent * heads, middle_head, attend_back, 0)
        if latent == 0:
            sum_fc2.finish(fc_rows)
            fc2_move = local(fc_rows, r.fc2_out)
            pl.semaphore_signal(r.free_x, inc=1, device_id=device_x, device_id_type=MESH)
            for step in range(1, line):
                pl.semaphore_signal(
                    r.free_z, inc=1, device_id=device_z(step), device_id_type=MESH
                )
        else:
            token_moves[latent - 1].forward()
            sum_fc1.forward(1)
        lax.fori_loop(middle_head, (latent + 1) * heads, attend_back, 0)
        sum_fc1.forward(1)

        def join(block, carry, latent=latent):
            row = pl.multiple_of(block * tokens, tokens)
            start = pl.multiple_of(latent * length + block * tokens, tokens)
            pieces = [
                source[latent * heads + head, pl.ds(row, tokens), :][:, :HEAD_DIM]
                for source in (r.q_heads, r.k_heads, r.v_heads)
                for head in range(heads)
            ]
            if sz.joined > 3 * part:
                pieces.append(jnp.zeros((tokens, sz.joined - 3 * part), BF16))
            values = jnp.concatenate(pieces, axis=1)
            joined_sums[...] += total_rows(values.astype(F32))
            grad_joined[pl.ds(start, tokens), :] = values
            return carry

        lax.fori_loop(0, seq, join, 0)

        def back_qkv(step, carry, latent=latent):
            start = pl.multiple_of(latent * length + step * tile, tile)
            rows = grad_joined[pl.ds(start, tile), :]
            for column, size in column_cuts(width):
                here = slice(column, column + size)
                sums = dot_right_t(rows, r.qkv[here, :])
                r.part_a[pl.ds(start, tile), here] = sums.astype(BF16)
            return carry

        lax.fori_loop(0, per_latent, back_qkv, 0)
        token_moves.append(SumTokens(r.part_a, 0, latent))

    token_moves[-1].forward()
    gather_qkv.drain()
    weight_grad(r.modded, grad_joined, r.qkv)
    sum_qkv = SumWeights(r.qkv, sz.chunk, r.across_b, r.along_b, sz.joined)
    pl.semaphore_wait(r.free_x, 1)
    sum_qkv.push((3,))
    sum_fc1.forward()


    weight_grad(r.mixed, r.grad_attended, r.out)

    def loosen_out(step, carry):
        start = pl.multiple_of(step * sz.chunk, 16)
        spread = dot(loosen, r.out[pl.ds(start, sz.chunk), :]).astype(BF16)
        for block in range(seq):
            place = pl.multiple_of(block * out_wide + step * pad, 16)
            r.out_blocks[pl.ds(place, pad), :] = spread[block * pad : (block + 1) * pad, :]
        return carry

    lax.fori_loop(0, sz.dp, loosen_out, 0)
    out_first = [
        send(
            rows_of(r.out_blocks, (y * 2 + 1 - c_me) * out_wide, out_wide),
            rows_of(r.grad_branch, y * out_wide, out_wide),
            device_seq(1),
        )
        for y in range(2)
    ]

    def out_from_core(y):
        return rows_of(r.grad_branch, y * out_wide, out_wide)[...].astype(F32)

    other = rows_of(r.out_blocks, ((1 - y_me) * 2 + c_me) * out_wide, out_wide)
    out_chip_sum = rows_of(r.modded_two, 2 * count * tokens, out_wide)

    def out_half(index):
        start, size = index * (out_wide // 2), out_wide // 2
        return send(rows_of(other, start, size), rows_of(out_chip_sum, start, size), device_seq(2))

    for latent in range(count):
        branch_moves[latent].finish()

        def final_output(step, carry, latent=latent):
            start = pl.multiple_of(step * ROWS, ROWS)
            here = pl.ds(latent * tokens + start, ROWS)
            branch = branch_moves[latent].rows(start) + r.bias_fc2[...]
            grad_output = r.out_grad[latent, pl.ds(start, ROWS), :].astype(F32)
            gate = mod[latent, 5:6, :]
            r.modded_two[here, :] = (r.middle[here, :] + gate * branch).astype(BF16)
            grad_mod[latent, 5:6, :] += total_rows(grad_output * branch)
            r.bias_sums[1:2, :] += total_rows((gate * grad_output).astype(BF16).astype(F32))
            return carry

        lax.fori_loop(0, tokens // ROWS, final_output, 0)
        slot = rows_of(r.modded_two, latent * tokens, tokens)
        far_moves.append(local(slot, r.output.at[latent]))
    for copy in out_first:
        copy.wait_recv()
    other[...] = (other[...].astype(F32) + out_from_core(1 - y_me)).astype(BF16)
    out_second = [out_half(0)]
    for latent in range(count):
        token_moves[latent].finish()

        def final_grads(step, carry, latent=latent):
            start = pl.multiple_of(step * ROWS, ROWS)
            here = pl.ds(latent * tokens + start, ROWS)
            incoming = token_moves[latent].rows(start)
            normed, inverse = layer_norm(r.latents[latent, pl.ds(start, ROWS), :].astype(F32))
            grad_mod[latent, 0:1, :] += total_rows(incoming)
            grad_mod[latent, 1:2, :] += total_rows(incoming * normed)
            grads = r.grad_middle[here, :] + norm_back(
                incoming * (1.0 + mod[latent, 1:2, :]), normed, inverse
            )
            place = pl.ds((count + latent) * tokens + start, ROWS)
            r.modded_two[place, :] = grads.astype(BF16)
            return carry

        lax.fori_loop(0, tokens // ROWS, final_grads, 0)
        slot = rows_of(r.modded_two, (count + latent) * tokens, tokens)
        far_moves.append(local(slot, r.latents_grad.at[latent]))

    def return_rows(total, send_ref, recv_ref):
        send_ref[...] = dot(loosen, total.astype(BF16)).astype(BF16)
        mine = rows_of(send_ref, s_me * pad, pad)
        own = local(mine, rows_of(recv_ref, s_me * pad, pad))
        moves = exchange(
            lambda peer: rows_of(send_ref, peer * pad, pad),
            lambda me: rows_of(recv_ref, me * pad, pad),
        )
        return own, moves

    def small(values):
        return values.reshape(count * 8, width)

    r.grad_core_send[...] = small(grad_mod[...])
    mod_core = send(r.grad_core_send, r.grad_core, device_seq(1))

    def own_place(sums, column):
        return place(sums[:, column : column + part], s_me * part, width)

    sums = joined_sums[...]
    r.bias_sums[2:3, :] = own_place(sums, 0)
    r.bias_sums[3:4, :] = own_place(sums, 2 * part)
    for position in range(seq):
        r.bias_sums[4 + position : 5 + position, :] = when(s_me == position, r.fc1_sums[...])
    bias_x = send(r.bias_sums, r.bias_x, device_x)
    sum_qkv.push((2,))
    mod_core.wait_recv()
    r.grad_chip_send[...] = r.grad_core_send[...] + r.grad_core[...]
    mod_chip = send(r.grad_chip_send, r.grad_chip, device_seq(2))
    out_second.append(out_half(1))
    for copy in fc1_moves:
        release(copy)
    fc2_move.wait()
    sum_fc1.finish(fc_rows)
    fc1_own, fc1_back = return_rows(fc_rows[...], r.fc1_blocks, r.fc1_rows)
    bias_x.wait_recv()
    r.bias_half[...] = r.bias_sums[...] + r.bias_x[...]
    mod_chip.wait_recv()
    rows_of(r.grad_all, dp_me * 16, 16)[...] = (r.grad_chip_send[...] + r.grad_chip[...]).astype(
        BF16
    )
    gather_grad = GatherWeights(r.grad_all, 16)
    gather_grad.push()
    bias_z = [send(r.bias_half, r.bias_z.at[step], device_z(step)) for step in range(1, line)]
    pl.semaphore_wait(r.free_z, line - 1)
    sum_qkv.forward(1)
    gather_grad.forward()
    sum_qkv.push((1,))
    pending.extend([mod_core, bias_x, mod_chip] + bias_z)
    bias_total = r.bias_half[...]
    for copy, step in zip(bias_z, range(1, line)):
        copy.wait_recv()
        bias_total = bias_total + r.bias_z[step]
    r.bias_line[...] = bias_total
    bias_core = send(r.bias_line, r.bias_core, device_seq(1))

    gather_grad.finish()
    all_grads = r.grad_all[...]
    rows = sz.dp * 16
    comp_of = iota((rows, rows), 0) & 7
    source = (iota((rows, rows), 0) & ~15) + ((iota((rows, rows), 0) >> 3) & 1)
    spread = jnp.where(iota((rows, rows), 1) == source, 1.0, 0.0).astype(BF16)
    cond_spread = dot(spread, r.cond_mine[...])
    comp_of = iota((rows, LANES), 0) & 7
    cond_grads = jnp.zeros((rows, sz.rows), F32)
    mod_rows = r.mod_out.shape[0]
    for comp in range(6):
        back = dot_right_t(all_grads, r.w_mod[:, comp * width : (comp + 1) * width])
        cond_grads = cond_grads + jnp.where(comp_of[:, : sz.rows] == comp, back, 0.0)
    cond_grads = jnp.sum(cond_grads.reshape(rows // 8, 8, sz.rows), axis=1)
    blank = jnp.zeros((16, width - sz.rows), F32)
    cond_grads = pltpu.roll(jnp.concatenate([cond_grads, blank], axis=1), me * sz.rows, 1)
    keep = iota((8, 16), 0)
    hits = []
    for side in range(2):
        hits.append(
            sum(
                when(
                    iota((8, width), 0) == along * count + latent,
                    jnp.broadcast_to(
                        cond_grads[
                            (along * 2 + side) * count + latent : (along * 2 + side) * count
                            + latent
                            + 1,
                            :,
                        ],
                        (8, width),
                    ),
                )
                for along in range(line)
                for latent in range(count)
            )
        )
    r.cond_sides[0] = hits[0]
    r.cond_sides[1] = hits[1]
    cond_x = send(r.cond_sides.at[1 - x_me], r.cond_x, device_x)
    sum_qkv.push((0,))
    bias_core.wait_recv()
    r.bias_pair[...] = r.bias_line[...] + r.bias_core[...]
    bias_chip = send(r.bias_pair, r.bias_chip, device_seq(2))
    comp_rows = iota((8, rows), 0) == (iota((8, rows), 1) & 7)
    mod_bias = dot(jnp.where(comp_rows, 1.0, 0.0).astype(BF16), all_grads)
    cond_x.wait_recv()
    r.cond_half[...] = r.cond_sides[x_me] + r.cond_x[...]
    cond_z = [send(r.cond_half, r.cond_z.at[step], device_z(step)) for step in range(1, line)]
    sum_qkv.forward(1)
    for copy in out_second:
        copy.wait_recv()
    mine = out_mine[...].astype(F32) + out_from_core(y_me)
    out_mine[...] = (mine + out_chip_sum[...].astype(F32)).astype(BF16)
    pending.extend(out_first + out_second)
    sum_out = SumWeights(out_mine, pad, r.across_out, r.along_out, width)
    sum_out.push()
    cond_total = r.cond_half[...]
    for copy, step in zip(cond_z, range(1, line)):
        copy.wait_recv()
        cond_total = cond_total + r.cond_z[step]
    r.cond_line[...] = cond_total
    cond_core = send(r.cond_line, r.cond_core, device_seq(1))
    sum_qkv.forward()
    cond_core.wait_recv()
    r.cond_pair[...] = r.cond_line[...] + r.cond_core[...]
    cond_chip = send(r.cond_pair, r.cond_chip, device_seq(2))
    for comp in range(6):
        chosen = jnp.where(comp_of == comp, cond_spread, 0.0).astype(BF16)
        place_rows = rows_of(r.grad_middle, comp * mod_rows, mod_rows)
        place_rows[...] = dot_left_t(chosen, all_grads)[:mod_rows, :]
        far_moves.append(local(place_rows, r.mod_out.at[:, pl.ds(comp * width, width)]))
    sum_out.forward(1)
    bias_chip.wait_recv()
    bias_full = r.bias_pair[...] + r.bias_chip[...]

    def own_lanes(row, start):
        size = row.shape[1]
        turned = pltpu.roll(jnp.broadcast_to(row, (8, size)), lax.rem(size - start, size), 1)
        return turned[0:1, : 2 * LANES]

    qv_total = when(me < half_way, bias_full[2:3, :]) + when(me >= half_way, bias_full[3:4, :])
    fc1_total = sum(
        when(s_me == position, bias_full[4 + position : 5 + position, :])
        for position in range(seq)
    )
    first = me * (6 * sz.rows) // width
    comp_row = iota((8, width), 0)
    pair = [
        jnp.sum(jnp.where(comp_row == first + more, mod_bias, 0.0), axis=0, keepdims=True)
        for more in range(2)
    ]
    r.small_out[...] = jnp.concatenate(
        [
            own_lanes(bias_full[0:1, :], me * sz.rows),
            own_lanes(bias_full[1:2, :], me * sz.rows),
            own_lanes(qv_total, lax.rem(me, half_way) * (2 * sz.rows)),
            own_lanes(fc1_total, dp_me * sz.units),
            own_lanes(jnp.concatenate(pair, axis=1), me * (6 * sz.rows) - first * width),
            jnp.zeros((3, 2 * LANES), F32),
        ],
        axis=0,
    )
    for copy in qkv_moves:
        release(copy)
    qkv_total = fc_rows.at[:, pl.ds(0, sz.joined)]
    sum_qkv.finish(qkv_total)
    qkv_own, qkv_back = return_rows(qkv_total[...], r.qkv_blocks, r.qkv_rows)
    sum_out.forward()
    sum_out.finish(r.out_out)
    gather_grad.drain()
    gather_bias.drain()
    gather_cond.drain()
    cond_chip.wait_recv()
    cond_full = r.cond_pair[...] + r.cond_chip[...]
    picked = [
        jnp.sum(
            jnp.where(comp_row == z_me * count + latent, cond_full, 0.0), axis=0, keepdims=True
        )
        for latent in range(count)
    ]
    slope = gate_cond * (1.0 + cond * (1.0 - gate_cond))
    r.cond_grad[...] = (jnp.concatenate(picked, axis=0) * slope).astype(BF16)
    pending.extend([bias_core, bias_chip, cond_x, cond_core, cond_chip] + cond_z)
    for own, moves in ((fc1_own, fc1_back), (qkv_own, qkv_back)):
        own.wait()
        settle(moves)
    far_moves.append(local(r.fc1_rows, r.fc1_out))
    far_moves.append(local(r.qkv_rows, r.qkv_out))
    for copy in far_moves:
        copy.wait()
    for copy in pending:
        copy.wait_send()


class Inputs(NamedTuple):
    latents: object
    out_grad: object
    conditioning: object
    bias: object
    w_mod: object
    qkv_src: object
    fc1_src: object
    out_src: object
    fc2_src: object


class Outputs(NamedTuple):
    output: object
    latents_grad: object
    cond_grad: object
    mod_out: object
    small_out: object
    qkv_out: object
    out_out: object
    fc1_out: object
    fc2_out: object


def kernel_scratch(sz):
    low = lambda *shape: pltpu.VMEM(shape, BF16)
    full = lambda *shape: pltpu.VMEM(shape, F32)
    count, tokens, width, seq = sz.count, sz.tokens, sz.width, sz.seq
    pad, groups = sz.padded_rows, sz.count * sz.heads
    tall = sz.chunk if sz.chunk > sz.units else sz.units
    wide = max(sz.joined, sz.hidden, width)
    return dict(
        lat_all=low(sz.total, max(width, sz.hidden)),
        grad_branch=low(sz.total, width),
        modded=low(sz.total, width),
        q_heads=low(groups, sz.length, LANES),
        k_heads=low(groups, sz.length, LANES),
        v_heads=low(groups, sz.length, LANES),
        o_heads=low(groups, sz.length, LANES),
        soft=low(groups, sz.length, sz.length),
        mixed_send=low(seq, count, tokens, sz.part),
        mixed_recv=low(seq, count, tokens, sz.part),
        mixed=low(sz.own, width),
        attended=full(sz.own, width),
        middle=full(sz.own, width),
        grad_middle=full(sz.own, width),
        grad_attended=low(sz.own, width),
        modded_two=low(sz.total, width),
        grad_hidden=low(sz.total, sz.hidden),
        part_a=low(sz.total, width),
        sum_core=low(2, 2, count, tokens, width),
        sum_send=low(2, count, tokens, width),
        sum_chip=low(2, count, tokens, width),
        qkv_blocks=low(seq * pad, sz.joined),
        fc1_blocks=low(seq * pad, sz.hidden),
        qkv_rows=low(seq * pad, sz.joined),
        fc1_rows=low(seq * pad, sz.hidden),
        out_blocks=low(seq * sz.dp * pad, width),
        qkv=low(width, sz.joined),
        fc1=low(width, sz.hidden),
        fc2=low(sz.hidden, width),
        out=low(width, width),
        across_a=low(sz.line, sz.chunk, wide),
        along_a=low(sz.line, sz.chunk, wide),
        across_b=low(sz.line, tall, wide),
        along_b=low(sz.line, tall, wide),
        across_out=low(sz.line, pad, width),
        along_out=low(sz.line, pad, width),
        cond_all=low(sz.dp * 16, width),
        cond_mine=low(sz.dp * 16, LANES),
        bias_blocks=low(seq * 16, width),
        bias_all=low(sz.dp * 16, width),
        mod_sums=full(16, sz.mod_part * seq),
        mod_core=full(2, 16, sz.mod_part),
        mod_send=full(16, sz.mod_part),
        mod_chip=full(16, sz.mod_part),
        mod_sum=full(16, sz.mod_part),
        mod_x=full(8, sz.mod_part),
        mod_half=full(8, sz.mod_part),
        mod_z=full(sz.line, 8, sz.mod_part),
        mod_all=full(seq, 8, sz.mod_part),
        modulation=full(count, 8, width),
        bias_joined=full(1, sz.joined),
        bias_out=full(1, width),
        bias_fc1=full(1, width),
        bias_fc2=full(1, width),
        joined_sums=full(1, sz.joined),
        fc1_sums=full(1, sz.hidden),
        grad_mod=full(count, 8, width),
        grad_core_send=full(16, width),
        grad_core=full(16, width),
        grad_chip_send=full(16, width),
        grad_chip=full(16, width),
        grad_all=low(sz.dp * 16, width),
        bias_sums=full(8, width),
        bias_x=full(8, width),
        bias_half=full(8, width),
        bias_z=full(sz.line, 8, width),
        bias_line=full(8, width),
        bias_core=full(8, width),
        bias_pair=full(8, width),
        bias_chip=full(8, width),
        cond_sides=full(2, 8, width),
        cond_x=full(8, width),
        cond_half=full(8, width),
        cond_z=full(sz.line, 8, width),
        cond_line=full(8, width),
        cond_core=full(8, width),
        cond_pair=full(8, width),
        cond_chip=full(8, width),
        send_sems=pltpu.SemaphoreType.DMA((200,)),
        recv_sems=pltpu.SemaphoreType.DMA((200,)),
        free_x=pltpu.SemaphoreType.REGULAR,
        free_z=pltpu.SemaphoreType.REGULAR,
        local_sems=pltpu.SemaphoreType.DMA((40,)),
    )


def kernel_outputs(sz):
    low = lambda *shape: jax.ShapeDtypeStruct(shape, BF16)
    full = lambda *shape: jax.ShapeDtypeStruct(shape, F32)
    count, tokens, width, pad = sz.count, sz.tokens, sz.width, sz.padded_rows
    return [
        low(count, tokens, width),
        low(count, tokens, width),
        low(count, width),
        full(-(-sz.rows // 8) * 8, 6 * width),
        full(8, 2 * LANES),
        low(sz.seq * pad, sz.joined),
        full(pad, width),
        low(sz.seq * pad, sz.hidden),
        full(sz.units, width),
    ]


def run_kernel(sz, *operands):
    vmem = pl.BlockSpec(memory_space=pltpu.VMEM)
    far = pl.BlockSpec(memory_space=pl.ANY)
    outputs = kernel_outputs(sz)
    return pl.pallas_call(
        partial(block_kernel, sz),
        out_shape=outputs,
        in_specs=[vmem] * 5 + [far] * 4,
        out_specs=[far, far, vmem, far, vmem, far, vmem, far, far],
        scratch_shapes=list(kernel_scratch(sz).values()),
        compiler_params=pltpu.CompilerParams(
            collective_id=0, has_side_effects=True, vmem_limit_bytes=66584576
        ),
    )(*operands)


def general_path(
    latents, out_grad, modulation, blocks, w_out, w_fc2, bias_qv, bias_out, bias_fc1, bias_fc2
):
    count, tokens, width = latents.shape
    dp, seq = lax.axis_size("dp"), lax.axis_size("seq")
    both = ("dp", "seq")
    qkv_blocks, fc1_blocks = blocks
    rows = qkv_blocks.shape[1]
    part, heads, length = width // seq, HEADS // seq, seq * tokens
    shift_att, scale_att, gate_att, shift_mlp, scale_mlp, gate_mlp = [
        modulation[:, index : index + 1] for index in range(6)
    ]

    def to_columns(blocks):
        mine = lax.all_to_all(blocks, "seq", 0, 0, tiled=True).reshape(seq * rows, -1)
        return lax.all_gather(mine, "dp", axis=0, tiled=True)

    full_qkv = to_columns(qkv_blocks)
    full_out = lax.all_gather(w_out, both, axis=0, tiled=True)
    full_fc1 = to_columns(fc1_blocks)
    full_fc2 = lax.all_gather(w_fc2, "dp", axis=0, tiled=True)

    def gather_tokens(values):
        return lax.all_gather(values, "seq", axis=1, tiled=True)

    def flat(values):
        return values.reshape(-1, values.shape[-1])

    tokens_f = latents.astype(F32)
    normed, inverse = layer_norm(tokens_f)
    modded = (normed * (1.0 + scale_att) + shift_att).astype(BF16)
    modded_all = flat(gather_tokens(modded))
    joined = dot(modded_all, full_qkv).reshape(count, length, 3, heads, HEAD_DIM)
    bias_q = bias_qv[0].reshape(heads, HEAD_DIM)
    bias_v = bias_qv[1].reshape(heads, HEAD_DIM)
    queries = (joined[:, :, 0] + bias_q).astype(BF16)
    keys = joined[:, :, 1].astype(BF16)
    values = (joined[:, :, 2] + bias_v).astype(BF16)
    scores = jnp.einsum("bqhd,bkhd->bhqk", queries, keys, preferred_element_type=F32) * (
        HEAD_DIM ** (-0.5)
    )
    soft = jax.nn.softmax(scores, axis=-1)
    soft_low = soft.astype(BF16)
    mixed = jnp.einsum("bhqk,bkhd->bqhd", soft_low, values, preferred_element_type=F32)
    mixed = mixed.astype(BF16).reshape(count, length, part)
    mixed_mine = lax.all_to_all(mixed, "seq", 1, 2, tiled=True)
    attended = dot(mixed_mine, full_out) + bias_out
    middle = tokens_f + gate_att * attended
    normed_two, inverse_two = layer_norm(middle)
    modded_two = (normed_two * (1.0 + scale_mlp) + shift_mlp).astype(BF16)
    modded_two_all = flat(gather_tokens(modded_two))
    hidden = dot(modded_two_all, full_fc1) + bias_fc1
    active, gelu_back = jax.vjp(partial(jax.nn.gelu, approximate=True), hidden)
    active = active.astype(BF16)

    def sum_tokens(partial_sums):
        parts = partial_sums.astype(BF16).reshape(count, length, width)
        return lax.psum_scatter(parts, "seq", scatter_dimension=1, tiled=True).astype(F32)

    branch = sum_tokens(dot(active, full_fc2)) + bias_fc2
    output = middle + gate_mlp * branch

    grad_output = out_grad.astype(F32)
    grad_gate_mlp = jnp.sum(grad_output * branch, axis=1)
    grad_branch = (gate_mlp * grad_output).astype(BF16)
    grad_branch_all = flat(gather_tokens(grad_branch))
    grad_hidden = gelu_back(dot_right_t(grad_branch_all, full_fc2))[0].astype(BF16)
    grad_modded_two = sum_tokens(dot_right_t(grad_hidden, full_fc1))
    grad_shift_mlp = jnp.sum(grad_modded_two, axis=1)
    grad_scale_mlp = jnp.sum(grad_modded_two * normed_two, axis=1)
    grad_middle = grad_output + norm_back(
        grad_modded_two * (1.0 + scale_mlp), normed_two, inverse_two
    )
    grad_gate_att = jnp.sum(grad_middle * attended, axis=1)
    grad_attended = (gate_att * grad_middle).astype(BF16)
    grad_mixed = dot_right_t(flat(grad_attended), full_out).astype(BF16)
    grad_mixed = lax.all_to_all(grad_mixed.reshape(latents.shape), "seq", 2, 1, tiled=True)
    grad_mixed = grad_mixed.reshape(count, length, heads, HEAD_DIM)
    grad_soft = jnp.einsum("bqhd,bkhd->bhqk", grad_mixed, values, preferred_element_type=F32)
    delta = jnp.sum(soft * grad_soft, axis=-1, keepdims=True)
    grad_scores = (soft * (grad_soft - delta)).astype(BF16)
    scale = HEAD_DIM ** (-0.5)
    grad_q = jnp.einsum("bhqk,bkhd->bqhd", grad_scores, keys, preferred_element_type=F32) * scale
    grad_k = jnp.einsum("bhqk,bqhd->bkhd", grad_scores, queries, preferred_element_type=F32) * scale
    grad_v = jnp.einsum("bhqk,bqhd->bkhd", soft_low, grad_mixed, preferred_element_type=F32)
    grad_joined = jnp.concatenate(
        [item.astype(BF16).reshape(count * length, part) for item in (grad_q, grad_k, grad_v)],
        axis=1,
    )
    grad_modded = sum_tokens(dot_right_t(grad_joined, full_qkv))
    grad_shift_att = jnp.sum(grad_modded, axis=1)
    grad_scale_att = jnp.sum(grad_modded * normed, axis=1)
    grad_tokens = grad_middle + norm_back(grad_modded * (1.0 + scale_att), normed, inverse)

    def from_columns(sums, groups):
        mine = lax.psum_scatter(sums.astype(BF16), "dp", scatter_dimension=0, tiled=True)
        blocks = lax.all_to_all(mine.reshape(seq, rows, -1), "seq", 0, 0, tiled=True)
        blocks = blocks.astype(F32).reshape(seq, rows, groups, -1)
        return blocks.transpose(1, 2, 0, 3).reshape(rows, -1)

    sums_fc2 = lax.psum_scatter(
        dot_left_t(active, grad_branch_all).astype(BF16), "dp", scatter_dimension=0, tiled=True
    ).astype(F32)
    sums_fc1 = from_columns(dot_left_t(modded_two_all, grad_hidden), dp)
    sums_out = lax.psum_scatter(
        dot_left_t(flat(mixed_mine), flat(grad_attended)).astype(BF16),
        both,
        scatter_dimension=0,
        tiled=True,
    ).astype(F32)
    sums_qkv = from_columns(dot_left_t(modded_all, grad_joined), 3)

    grad_mod = jnp.stack(
        [
            grad_shift_att,
            grad_scale_att,
            grad_gate_att,
            grad_shift_mlp,
            grad_scale_mlp,
            grad_gate_mlp,
        ],
        axis=1,
    )
    bias_sums = [
        jnp.sum(item.astype(F32), axis=0)
        for item in (grad_joined, flat(grad_attended), grad_hidden, flat(grad_branch))
    ]
    weight_sums = [sums_qkv, sums_out, sums_fc1, sums_fc2]
    return output.astype(BF16), grad_tokens.astype(BF16), grad_mod, bias_sums, weight_sums


def kernel_path(sz, latents, conditioning, w_mod, w_qkv, w_out, w_fc1, w_fc2, biases, out_grad):
    more = sz.padded_rows - sz.rows
    gap = sz.joined - 3 * sz.part
    part, seq, pad, rows = sz.part, sz.seq, sz.padded_rows, sz.rows
    qkv_blocks, fc1_blocks = column_blocks(seq, sz.dp, w_qkv, w_fc1, sz.units)
    output, grad_tokens, grad_cond, sums_mod, small, sums_qkv, sums_out, sums_fc1, sums_fc2 = (
        run_kernel(
            sz,
            latents,
            out_grad,
            conditioning,
            jnp.concatenate(biases).reshape(1, -1),
            w_mod,
            jnp.pad(qkv_blocks, ((0, 0), (0, more), (0, gap))),
            jnp.pad(fc1_blocks, ((0, 0), (0, more), (0, 0))),
            jnp.pad(w_out, ((0, more), (0, 0))),
            w_fc2,
        )
    )

    def spread(sums, columns, groups):
        sums = sums.reshape(seq, pad, -1)[:, :rows, :columns].astype(F32)
        return sums.reshape(seq, rows, groups, -1).transpose(1, 2, 0, 3).reshape(rows, -1)

    return (
        output,
        grad_tokens,
        grad_cond,
        sums_mod[:rows],
        small[4, : 6 * rows],
        spread(sums_qkv, 3 * part, 3),
        small[2, : 2 * rows],
        sums_out[:rows],
        small[0, :rows],
        spread(sums_fc1, sz.hidden, sz.dp),
        small[3, : sz.units],
        sums_fc2,
        small[1, :rows],
    )


def column_blocks(seq, dp, w_qkv, w_fc1, units):
    rows = w_qkv.shape[0]
    qkv_blocks = w_qkv.reshape(rows, 3, seq, -1).transpose(2, 0, 1, 3).reshape(seq, rows, -1)
    fc1_blocks = w_fc1.reshape(rows, dp, seq, units).transpose(2, 0, 1, 3).reshape(seq, rows, -1)
    return qkv_blocks, fc1_blocks


def body(
    latents,
    conditioning,
    w_mod,
    b_mod,
    w_qkv,
    b_qv,
    w_out,
    b_out,
    w_fc1,
    b_fc1,
    w_fc2,
    b_fc2,
    out_grad,
):
    count, tokens, width = latents.shape
    dp, seq = lax.axis_size("dp"), lax.axis_size("seq")
    sz = Sizes(dp, seq, latents, w_qkv, w_fc2)
    if sz.fits():
        biases = (b_mod, b_qv, b_out, b_fc1, b_fc2)
        return kernel_path(
            sz, latents, conditioning, w_mod, w_qkv, w_out, w_fc1, w_fc2, biases, out_grad
        )
    both = ("dp", "seq")
    my_dp, my_seq = lax.axis_index("dp"), lax.axis_index("seq")
    me = my_dp * seq + my_seq
    rows, units = w_qkv.shape[0], w_fc2.shape[0]
    part = width // seq

    cond = conditioning.astype(F32)
    cond_act, silu_back = jax.vjp(jax.nn.silu, cond)
    cond_low = lax.all_gather(cond_act.astype(BF16), "dp", axis=0, tiled=True)
    cond_mine = lax.dynamic_slice_in_dim(cond_low, me * rows, rows, axis=1)
    mod_part = dot(cond_mine, w_mod)
    mod_sum = lax.psum(lax.psum_scatter(mod_part, "dp", scatter_dimension=0, tiled=True), "seq")
    biases = lax.all_gather(jnp.concatenate([b_mod, b_qv, b_out, b_fc1, b_fc2]), both, axis=0)
    pieces, start = [], 0
    for item in (b_mod, b_qv, b_out, b_fc1, b_fc2):
        pieces.append(biases[:, start : start + item.shape[0]].reshape(-1).astype(F32))
        start += item.shape[0]
    bias_mod, bias_qv, bias_out, bias_fc1, bias_fc2 = pieces
    bias_qv = lax.dynamic_index_in_dim(bias_qv.reshape(2, seq, part), my_seq, 1, keepdims=False)
    bias_fc1 = lax.dynamic_index_in_dim(
        bias_fc1.reshape(dp, seq, units), my_seq, 1, keepdims=False
    ).reshape(-1)
    modulation = (mod_sum + bias_mod).reshape(count, 6, width)

    blocks = column_blocks(seq, dp, w_qkv, w_fc1, units)
    output, grad_tokens, grad_mod, bias_sums, weight_sums = general_path(
        latents,
        out_grad,
        modulation,
        blocks,
        w_out,
        w_fc2,
        bias_qv,
        bias_out,
        bias_fc1,
        bias_fc2,
    )
    sums_qkv, sums_out, sums_fc1, sums_fc2 = weight_sums

    grad_mod = grad_mod.reshape(count, -1)
    grad_mod = lax.psum(grad_mod, "seq").astype(BF16)
    grad_mod = lax.all_gather(grad_mod, "dp", axis=0, tiled=True)
    sums_mod = dot_left_t(cond_mine, grad_mod)
    own = b_mod.shape[0]
    sums_bias_mod = jnp.sum(
        lax.dynamic_slice_in_dim(grad_mod, me * own, own, axis=1).astype(F32), axis=0
    )
    grad_cond_act = lax.all_gather(dot_right_t(grad_mod, w_mod), both, axis=0)
    grad_cond_act = lax.dynamic_slice_in_dim(grad_cond_act, my_dp * count, count, axis=1)
    grad_cond = silu_back(grad_cond_act.transpose(1, 0, 2).reshape(count, width))[0]

    def spread(values, shape):
        blank = jnp.zeros(shape, F32)
        return lax.dynamic_update_slice_in_dim(blank, values, my_seq, 1).reshape(-1)

    joined_sums, out_sums, fc1_sums, fc2_sums = bias_sums
    qv_sums = jnp.stack([joined_sums[:part], joined_sums[2 * part : 3 * part]])
    bias_sums = [
        spread(qv_sums.reshape(2, 1, part), (2, seq, part)),
        out_sums,
        spread(fc1_sums.reshape(dp, 1, units), (dp, seq, units)),
        fc2_sums,
    ]
    joint = jnp.concatenate([item.reshape(dp * seq, -1) for item in bias_sums], axis=1)
    joint = lax.psum_scatter(joint, both, scatter_dimension=0, tiled=True).reshape(-1)
    cuts = [b_qv.shape[0], b_out.shape[0], b_fc1.shape[0]]
    sums_bias_qv, sums_bias_out, sums_bias_fc1, sums_bias_fc2 = jnp.split(
        joint, [cuts[0], cuts[0] + cuts[1], sum(cuts)]
    )
    return (
        output,
        grad_tokens,
        grad_cond.astype(BF16),
        sums_mod,
        sums_bias_mod,
        sums_qkv,
        sums_bias_qv,
        sums_out,
        sums_bias_out,
        sums_fc1,
        sums_bias_fc1,
        sums_fc2,
        sums_bias_fc2,
    )


def solution(mesh):
    both = P(("dp", "seq"))
    wide = P(("dp", "seq"), None)
    tokens = P("dp", "seq", None)
    in_specs = (
        tokens,
        P("dp", None),
        wide,
        both,
        wide,
        both,
        wide,
        both,
        wide,
        both,
        wide,
        both,
        tokens,
    )
    out_specs = (tokens, tokens, P("dp", None)) + (wide, both) * 5
    return jax.shard_map(body, mesh=mesh, in_specs=in_specs, out_specs=out_specs, check_vma=False)
```

```python
from functools import partial
from types import SimpleNamespace
from typing import NamedTuple

import jax
import jax.numpy as jnp
from jax import lax
from jax.experimental import pallas as pl
from jax.experimental.pallas import tpu as pltpu
from jax.sharding import PartitionSpec as P

HEADS = 16
HEAD_DIM = 72
EPSILON = 1e-06
BF16 = jnp.bfloat16
F32 = jnp.float32


def layer_norm(values):
    center = values - jnp.mean(values, axis=-1, keepdims=True)
    inverse = lax.rsqrt(jnp.mean(center * center, axis=-1, keepdims=True) + EPSILON)
    return (center * inverse, inverse)


def norm_back(incoming, normed, inverse):
    return inverse * (
        incoming
        - jnp.mean(incoming, axis=-1, keepdims=True)
        - normed * jnp.mean(incoming * normed, axis=-1, keepdims=True)
    )


def dot(left, right):
    return jnp.dot(left, right, preferred_element_type=F32)


def dot_right_t(left, right):
    return lax.dot_general(left, right, (((1,), (1,)), ((), ())), preferred_element_type=F32)


def dot_left_t(left, right):
    return lax.dot_general(left, right, (((0,), (0,)), ((), ())), preferred_element_type=F32)


MESH = pl.DeviceIdType.MESH
ROOT = HEAD_DIM ** (-0.5)
LANES = 128
ROWS = 32


class Sizes:
    def __init__(self, dp, seq, latents, w_qkv, w_fc2):
        self.dp, self.seq, self.line = dp, seq, dp // 2
        self.count, self.tokens, self.width = latents.shape
        self.rows, self.units = w_qkv.shape[0], w_fc2.shape[0]
        self.chunk = seq * self.rows
        self.hidden = dp * self.units
        self.heads = HEADS // seq
        self.part = self.width // seq
        self.length = seq * self.tokens
        self.total = self.count * self.length
        self.own = self.count * self.tokens
        self.padded_rows = -(-self.rows // 16) * 16
        self.joined = -(-3 * self.part // LANES) * LANES
        self.mod_part = -(-6 * self.width // (seq * LANES)) * LANES

    def fits(self):
        return (
            self.seq == 4
            and self.dp % 2 == 0
            and self.dp == 8
            and self.count == 2
            and self.width == self.dp * self.chunk
            and self.chunk % 16 == 0
            and self.units % 16 == 0
            and self.tokens % 128 == 0
            and self.width % LANES == 0
            and self.hidden == self.width
            and self.chunk == self.units
        )


def column_cuts(width, most=512):
    cuts, start = [], 0
    while start < width:
        size = min(most, width - start)
        cuts.append((start, size))
        start += size
    return cuts


def one_hot(rows, columns, group, padded, flip):
    shape = (columns, rows) if flip else (rows, columns)
    tight = lax.broadcasted_iota(jnp.int32, shape, 1 if flip else 0)
    loose = lax.broadcasted_iota(jnp.int32, shape, 0 if flip else 1)
    hit = jnp.zeros(shape, F32)
    for index in range(rows // group):
        inside = (tight >= index * group) & (tight < (index + 1) * group)
        match = loose == tight + index * (padded - group)
        hit = jnp.where(inside & match, 1.0, hit)
    return hit.astype(BF16)


def block_kernel(sz, *refs):
    names = Inputs._fields + Outputs._fields + tuple(kernel_scratch(sz))
    r = SimpleNamespace(**dict(zip(names, refs)))
    dp_me, s_me = lax.axis_index("dp"), lax.axis_index("seq")
    z_me, x_me = dp_me // 2, dp_me % 2
    y_me, c_me = s_me // 2, s_me % 2
    count, tokens, width = sz.count, sz.tokens, sz.width
    line, seq = sz.line, sz.seq

    def seq_peer(mask):
        flip_y, flip_c = mask // 2, mask % 2
        y = 1 - y_me if flip_y else y_me
        c = 1 - c_me if flip_c else c_me
        return y * 2 + c

    def z_peer(step):
        return lax.rem(z_me + step, line)

    def device_seq(mask):
        return (dp_me, seq_peer(mask))

    def device_z(step):
        return (z_peer(step) * 2 + x_me, s_me)

    inner = z_me % 3 != 0
    outer = z_me % 3 == 0

    def z_flip(mask):
        return (z_me, z_me + 1 - 2 * (z_me % 2), lax.rem(z_me + 2, line), line - 1 - z_me)[mask]

    def device_flip(mask):
        return (z_flip(mask) * 2 + x_me, s_me)

    device_x = (z_me * 2 + (1 - x_me), s_me)
    used = [0, 0]

    def copy_to(src, dst, device, arrival=None):
        index = used[0]
        used[0] += 1
        return pltpu.make_async_remote_copy(
            src_ref=src,
            dst_ref=dst,
            send_sem=r.send_sems.at[index],
            recv_sem=r.recv_sems.at[index] if arrival is None else arrival,
            device_id=device,
            device_id_type=MESH,
        )

    def send(src, dst, device, arrival=None):
        copy = copy_to(src, dst, device, arrival)
        copy.start()
        return copy

    def local(src, dst):
        index = used[1]
        used[1] += 1
        copy = pltpu.make_async_copy(src, dst, r.local_sems.at[index])
        copy.start()
        return copy

    def rows_of(ref, start, size):
        return ref.at[pl.ds(start, size)]

    raw_moves = [
        local(source, target)
        for source, target in (
            (r.qkv_src, r.qkv_raw),
            (r.fc1_src, r.fc1_raw),
            (r.out_src, r.out_raw),
        )
    ]

    peers = [device_seq(mask) for mask in (1, 2, 3)]
    peers += [device_z(step) for step in range(1, line)] + [device_x]
    barrier = pltpu.get_barrier_semaphore()
    for peer in peers:
        pl.semaphore_signal(barrier, inc=1, device_id=peer, device_id_type=MESH)
    pl.semaphore_wait(barrier, len(peers))

    pending = []
    far_moves = []

    def release(copy):
        copy.wait_send()
        pending[:] = [item for item in pending if item is not copy]

    def token_rows(ref, latent, position):
        return rows_of(ref, (latent * seq + position) * tokens, tokens)

    class GatherTokens:
        def __init__(self, ref, latent, source=None):
            self.ref, self.latent = ref, latent
            slot = token_rows(ref, latent, s_me)
            mine = slot if source is None else source
            self.core = send(mine, slot, device_seq(1))
            self.chip = send(mine, slot, device_seq(2))

        def forward(self):
            self.chip.wait_recv()
            slot = token_rows(self.ref, self.latent, seq_peer(2))
            self.last = send(slot, slot, device_seq(1))

        def finish(self):
            self.core.wait_recv()
            self.last.wait_recv()
            for copy in (self.core, self.chip, self.last):
                pending.append(copy)

    class SumTokens:
        def __init__(self, part, slot, latent):
            self.part, self.slot, self.latent = part, slot, latent
            self.first = [
                send(
                    token_rows(part, latent, y * 2 + 1 - c_me),
                    r.sum_core.at[slot, y, latent],
                    device_seq(1),
                )
                for y in range(2)
            ]

        def forward(self):
            for copy in self.first:
                copy.wait_recv()
            other = 1 - y_me
            total = token_rows(self.part, self.latent, other * 2 + c_me)[...].astype(F32)
            total = total + r.sum_core[self.slot, other, self.latent].astype(F32)
            r.sum_send[self.slot, self.latent] = total.astype(BF16)
            self.last = send(
                r.sum_send.at[self.slot, self.latent],
                r.sum_chip.at[self.slot, self.latent],
                device_seq(2),
            )

        def finish(self):
            self.last.wait_recv()
            for copy in self.first + [self.last]:
                copy.wait_send()

        def rows(self, start):
            place = pl.ds((self.latent * seq + s_me) * tokens + start, ROWS)
            here = pl.ds(start, ROWS)
            total = self.part[place, :].astype(F32)
            total = total + r.sum_core[self.slot, y_me, self.latent, here, :].astype(F32)
            return total + r.sum_chip[self.slot, self.latent, here, :].astype(F32)

    def exchange(pick, place):
        return [send(pick(seq_peer(mask)), place(s_me), device_seq(mask)) for mask in (1, 2, 3)]

    def settle(copies):
        for copy in copies:
            copy.wait_recv()
        pending.extend(copies)

    class GatherWeights:
        def __init__(self, ref, chunk):
            self.ref, self.chunk = ref, chunk

        def slot(self, dp):
            return rows_of(self.ref, dp * self.chunk, self.chunk)

        def push_along(self, source=None):
            own = self.slot(dp_me)
            mine = own if source is None else source
            self.along = [send(mine, own, device_flip(mask)) for mask in (2, 1)]
            self.arrival = r.recv_sems.at[used[0]]
            self.last = copy_to(mine, own, device_flip(3))
            pl.when(inner)(self.last.start)
            self.across, self.passed = [], 0

        def push_across(self, source=None):
            own = self.slot(dp_me)
            mine = own if source is None else source
            self.across.append(send(mine, own, device_x))

        def push(self, source=None):
            self.push_along(source)
            self.push_across(source)

        def forward(self, limit=3):
            for mask in (2, 1, 3)[self.passed :][:limit]:
                (self.along + [self.last])[self.passed].wait_recv()
                self.passed += 1
                came = self.slot(z_flip(mask) * 2 + x_me)
                if mask == 2:
                    self.relay = copy_to(came, came, device_flip(1), self.arrival)
                    pl.when(inner)(self.relay.start)
                self.across.append(send(came, came, device_x))

        def finish(self):
            for copy in self.across:
                copy.wait_recv()

        def drain(self):
            for copy in self.along + self.across:
                copy.wait_send()

            @pl.when(inner)
            def _():
                self.last.wait_send()
                self.relay.wait_send()

    class SumWeights:
        def __init__(self, ref, chunk, across_ref, along_ref, columns):
            self.ref, self.chunk, self.columns = ref, chunk, columns
            self.across_ref, self.along_ref = across_ref, along_ref
            self.across = {}

        def view(self, ref, index):
            return ref.at[index, :, pl.ds(0, self.columns)]

        def slot(self, dp):
            return rows_of(self.ref, dp * self.chunk, self.chunk)

        def push(self, masks=(3, 2, 1, 0)):
            if not self.across:
                self.across, self.passed = {}, []
            for mask in masks:
                self.across[mask] = send(
                    self.slot(z_flip(mask) * 2 + 1 - x_me),
                    self.view(self.across_ref, mask),
                    device_x,
                )

        def forward(self, limit=3):
            for mask in (3, 2, 1)[len(self.passed) :][:limit]:
                self.passed.append(mask)
                self.across[mask].wait_recv()
                slot = self.slot(z_flip(mask) * 2 + x_me)
                came = self.view(self.across_ref, mask)

                def total():
                    return slot[...].astype(F32) + came[...].astype(F32)

                extra = self.view(self.along_ref, 0)
                if mask == 3:
                    slot[...] = total().astype(BF16)
                    self.direct = copy_to(slot, self.view(self.along_ref, 3), device_flip(3))
                    self.relay = copy_to(slot, extra, device_flip(1))
                    pl.when(inner)(self.direct.start)
                    pl.when(outer)(self.relay.start)
                elif mask == 2:

                    @pl.when(inner)
                    def _():
                        self.relay.wait_recv()
                        slot[...] = (total() + extra[...].astype(F32)).astype(BF16)

                    @pl.when(outer)
                    def _():
                        slot[...] = total().astype(BF16)

                    self.two = send(slot, self.view(self.along_ref, 2), device_flip(2))
                else:
                    slot[...] = total().astype(BF16)
                    self.one = send(slot, self.view(self.along_ref, 1), device_flip(1))

        def finish(self, target):
            self.across[0].wait_recv()
            total = self.slot(dp_me)[...].astype(F32)
            total = total + self.view(self.across_ref, 0)[...].astype(F32)
            for copy, mask in ((self.one, 1), (self.two, 2)):
                copy.wait_recv()
                total = total + self.view(self.along_ref, mask)[...].astype(F32)
            target[...] = total

            @pl.when(inner)
            def _():
                self.direct.wait_recv()
                target[...] += self.view(self.along_ref, 3)[...].astype(F32)
                self.direct.wait_send()

            @pl.when(outer)
            def _():
                self.relay.wait_send()

            for copy in [self.one, self.two] + list(self.across.values()):
                copy.wait_send()

    pad = sz.padded_rows
    qkv_blocks, fc1_blocks = r.qkv_blocks, r.fc1_blocks
    out_wide = sz.dp * pad
    out_mine = rows_of(r.out_blocks, s_me * out_wide, out_wide)

    cond = r.conditioning[...].astype(F32)
    gate_cond = 1.0 / (1.0 + jnp.exp(-cond))
    low_rows = jnp.concatenate([cond * gate_cond, jnp.zeros((16 - count, width), F32)], axis=0)
    rows_of(r.cond_all, dp_me * 16, 16)[...] = low_rows.astype(BF16)
    gather_cond = GatherWeights(r.cond_all, 16)
    gather_cond.push()
    for move in raw_moves:
        move.wait()
    own_out = jnp.concatenate(
        [r.out_raw[...].astype(F32), jnp.zeros((pad - sz.rows, width), F32)], axis=0
    )
    rows_of(out_mine, dp_me * pad, pad)[...] = own_out.astype(BF16)
    gather_out = GatherWeights(out_mine, pad)
    gather_out.push()
    qkv_send, fc1_send = r.qkv_rows, r.fc1_rows
    qkv_send[...] = jnp.zeros_like(qkv_send)
    fc1_send[...] = jnp.zeros_like(fc1_send)
    for position in range(seq):
        here = slice(position * pad, position * pad + sz.rows)
        pieces = [
            r.qkv_raw[:, kind * width + position * sz.part :][:, : sz.part] for kind in range(3)
        ]
        qkv_send[here, : 3 * sz.part] = jnp.concatenate(pieces, axis=1)
        pieces = [
            r.fc1_raw[:, (group * seq + position) * sz.units :][:, : sz.units]
            for group in range(sz.dp)
        ]
        fc1_send[here, :] = jnp.concatenate(pieces, axis=1)
    qkv_local, fc1_local = [
        local(rows_of(source, s_me * pad, pad), rows_of(target, s_me * pad, pad))
        for source, target in ((qkv_send, qkv_blocks), (fc1_send, fc1_blocks))
    ]
    lat_local, og_local = [
        [local(source.at[latent], token_rows(target, latent, s_me)) for latent in range(count)]
        for source, target in ((r.latents, r.lat_all), (r.out_grad, r.grad_branch))
    ]
    fc2_local = local(r.fc2_src, rows_of(r.fc2, dp_me * sz.units, sz.units))

    def place(values, start, size):
        blank = jnp.zeros((1, size - values.shape[1]), F32)
        row = jnp.concatenate([values.astype(F32), blank], axis=1)
        return pltpu.roll(jnp.broadcast_to(row, (8, size)), start, 1)[0:1, :]

    def when(hit, values):
        return jnp.where(hit, values, jnp.zeros_like(values))

    me = dp_me * seq + s_me
    lengths = (6 * sz.rows, 2 * sz.rows, sz.rows, sz.units, sz.rows)
    starts = [sum(lengths[:index]) for index in range(len(lengths))]
    own_mod, own_qv, own_out, own_fc1, own_fc2 = [
        r.bias[:, start : start + size] for start, size in zip(starts, lengths)
    ]
    devices = sz.dp * seq
    half_way = devices // 2
    qv_row = place(own_qv, lax.rem(me, half_way) * (2 * sz.rows), width)
    fc1_row = place(own_fc1, dp_me * sz.units, width)
    bias_rows = [
        place(own_out, me * sz.rows, width),
        place(own_fc2, me * sz.rows, width),
        when(me < half_way, qv_row),
        when(me >= half_way, qv_row),
    ] + [when(s_me == position, fc1_row) for position in range(seq)]
    bias_rows.append(jnp.zeros((16 - len(bias_rows), width), F32))
    bias_mine = rows_of(r.bias_blocks, s_me * 16, 16)
    bias_mine[...] = jnp.concatenate(bias_rows, axis=0).astype(BF16)
    bias_moves = exchange(lambda peer: bias_mine, lambda me: rows_of(r.bias_blocks, me * 16, 16))
    qkv_moves = exchange(
        lambda peer: rows_of(qkv_send, peer * pad, pad),
        lambda me: rows_of(qkv_blocks, me * pad, pad),
    )
    fc1_moves = exchange(
        lambda peer: rows_of(fc1_send, peer * pad, pad),
        lambda me: rows_of(fc1_blocks, me * pad, pad),
    )
    lat_moves = [GatherTokens(r.lat_all, 0, r.latents.at[0])]

    tighten = one_hot(sz.chunk, seq * pad, sz.rows, pad, False)
    loosen = one_hot(sz.chunk, seq * pad, sz.rows, pad, True)
    gather_qkv = GatherWeights(r.qkv, sz.chunk)
    gather_fc1 = GatherWeights(r.fc1, sz.chunk)
    gather_fc2 = GatherWeights(r.fc2, sz.units)
    settle(bias_moves)
    bias_sum = sum(
        r.bias_blocks[position * 16 : (position + 1) * 16, :].astype(F32) for position in range(seq)
    )
    rows_of(r.bias_all, dp_me * 16, 16)[...] = bias_sum.astype(BF16)
    gather_bias = GatherWeights(r.bias_all, 16)
    gather_bias.push()
    gather_cond.forward()
    gather_out.forward(1)
    qkv_local.wait()
    settle(qkv_moves)
    rows_of(r.qkv, dp_me * sz.chunk, sz.chunk)[...] = dot(tighten, qkv_blocks[...]).astype(BF16)
    gather_qkv.push_along()

    gather_cond.finish()
    gather_qkv.push_across()
    iota = partial(lax.broadcasted_iota, jnp.int32)
    hit = iota((width, LANES), 0) == iota((width, LANES), 1) + me * sz.rows
    hit = hit & (iota((width, LANES), 1) < sz.rows)
    cond_mine = dot(r.cond_all[...], jnp.where(hit, 1.0, 0.0).astype(BF16)).astype(BF16)
    r.cond_mine[...] = cond_mine
    order = iota((16, sz.dp * 16), 0)
    across, along, which = order >> 3, (order >> 1) & (line - 1), order & 1
    hit = iota((16, sz.dp * 16), 1) == (along * 2 + across) * 16 + which
    cond_rows = dot(jnp.where(hit, 1.0, 0.0).astype(BF16), cond_mine).astype(BF16)
    cond_rows = cond_rows[:, : sz.rows]
    mod_wide = sz.mod_part * seq
    own_row = place(own_mod, me * (6 * sz.rows), mod_wide)
    for comp in range(6):
        here = slice(comp * width, (comp + 1) * width)
        r.mod_sums[:, here] = dot(cond_rows, r.w_mod[:, here]) + own_row[:, here]
    r.mod_sums[:, 6 * width :] = jnp.zeros((16, mod_wide - 6 * width), F32)

    def mod_part(position):
        return r.mod_sums.at[:, pl.ds(pl.multiple_of(position * sz.mod_part, LANES), sz.mod_part)]

    mod_core = [
        send(mod_part(y * 2 + 1 - c_me), r.mod_core.at[y], device_seq(1)) for y in range(2)
    ]
    gather_out.forward()
    fc1_local.wait()
    settle(fc1_moves)
    rows_of(r.fc1, dp_me * sz.chunk, sz.chunk)[...] = dot(tighten, fc1_blocks[...]).astype(BF16)
    for copy in mod_core:
        copy.wait_recv()
    r.mod_send[...] = mod_part((1 - y_me) * 2 + c_me)[...] + r.mod_core[1 - y_me]
    mod_chip = send(r.mod_send, r.mod_chip, device_seq(2))
    for latent in range(1, count):
        lat_moves.append(GatherTokens(r.lat_all, latent, r.latents.at[latent]))
    mod_chip.wait_recv()
    r.mod_sum[...] = mod_part(s_me)[...] + r.mod_core[y_me] + r.mod_chip[...]
    mod_x = send(rows_of(r.mod_sum, (1 - x_me) * 8, 8), r.mod_x, device_x)
    lat_moves[0].forward()
    gather_bias.forward(1)
    gather_qkv.forward(1)
    mod_x.wait_recv()
    r.mod_half[...] = rows_of(r.mod_sum, x_me * 8, 8)[...] + r.mod_x[...]
    mod_z = [send(r.mod_half, r.mod_z.at[step], device_z(step)) for step in range(1, line)]
    gather_fc1.push_along()
    gather_bias.forward()
    og_moves = [GatherTokens(r.grad_branch, 0, r.out_grad.at[0])]
    gather_fc1.push_across()
    gather_qkv.forward()
    for move in lat_moves[1:]:
        move.forward()
    gather_out.finish()
    mod_total = r.mod_half[...]
    for copy, step in zip(mod_z, range(1, line)):
        copy.wait_recv()
        mod_total = mod_total + r.mod_z[step]
    hit = iota((8, sz.mod_part), 0)
    picked = [
        jnp.sum(jnp.where(hit == z_me * count + latent, mod_total, 0.0), axis=0, keepdims=True)
        for latent in range(count)
    ]
    picked.append(jnp.zeros((8 - count, sz.mod_part), F32))
    mod_slot = r.mod_all.at[s_me]
    mod_slot[...] = jnp.concatenate(picked, axis=0)
    mod_moves = [send(mod_slot, mod_slot, device_seq(mask)) for mask in (1, 2)]
    out_core = send(out_mine, out_mine, device_seq(1))
    out_chip = send(out_mine, out_mine, device_seq(2))
    mod_moves[1].wait_recv()
    mod_slot = r.mod_all.at[seq_peer(2)]
    mod_moves.append(send(mod_slot, mod_slot, device_seq(1)))
    gather_bias.finish()
    bias = jnp.sum(r.bias_all[...].astype(F32).reshape(sz.dp, 16, width), axis=0)
    bias_out, bias_fc2 = bias[0:1, :], bias[1:2, :]
    part = sz.part

    def own_part(row):
        return sum(
            when(s_me == position, row[:, position * part : (position + 1) * part])
            for position in range(seq)
        )

    r.bias_joined[...] = jnp.concatenate(
        [
            own_part(bias[2:3, :]),
            jnp.zeros((1, part), F32),
            own_part(bias[3:4, :]),
            jnp.zeros((1, sz.joined - 3 * part), F32),
        ],
        axis=1,
    )
    r.bias_fc1[...] = sum(
        when(s_me == position, bias[4 + position : 5 + position, :]) for position in range(seq)
    )
    r.bias_out[...] = bias_out
    r.bias_fc2[...] = bias_fc2
    mod_moves[0].wait_recv()
    mod_moves[2].wait_recv()
    wide = jnp.concatenate([r.mod_all[position] for position in range(seq)], axis=1)
    mod = r.modulation
    for latent in range(count):
        for comp in range(6):
            mod[latent, comp : comp + 1, :] = wide[
                latent : latent + 1, comp * width : (comp + 1) * width
            ]
    pending.extend(mod_core + [mod_chip, mod_x] + mod_z + mod_moves)
    gather_fc1.forward(1)
    for copy in qkv_moves + fc1_moves:
        release(copy)
    gather_bias.drain()
    gather_cond.drain()
    fc2_local.wait()
    gather_fc2.push()

    for copy in lat_local:
        copy.wait()
    for move in lat_moves:
        move.finish()

    heads, length = sz.heads, sz.length

    def modulate_tokens(step, carry):
        latent = step // (length // ROWS)
        here = pl.ds(pl.multiple_of(step * ROWS, ROWS), ROWS)
        normed, _ = layer_norm(r.lat_all[here, :].astype(F32))
        shift, scale = mod[latent, 0:1, :], mod[latent, 1:2, :]
        r.modded[here, :] = (normed * (1.0 + scale) + shift).astype(BF16)
        return carry

    lax.fori_loop(0, count * length // ROWS, modulate_tokens, 0)

    gather_qkv.finish()
    tile = 2 * tokens
    per_latent = length // tile

    def pad_head(values):
        return jnp.concatenate(
            [values, jnp.zeros((values.shape[0], LANES - HEAD_DIM), values.dtype)], axis=1
        )

    def project(step, carry):
        start = pl.multiple_of(step * tile, tile)
        latent = step // per_latent
        row = pl.multiple_of((step % per_latent) * tile, tile)
        joined = dot(r.modded[pl.ds(start, tile), :], r.qkv[...]) + r.bias_joined[...]
        for kind, target in enumerate((r.q_heads, r.k_heads, r.v_heads)):
            for head in range(heads):
                column = kind * part + head * HEAD_DIM
                piece = pad_head(joined[:, column : column + HEAD_DIM]).astype(BF16)
                target[latent * heads + head, pl.ds(row, tile), :] = piece
        return carry

    lax.fori_loop(0, count * per_latent, project, 0)
    gather_fc1.forward(1)

    half = length // 2

    def attend(index, carry):
        keys, values = r.k_heads[index], r.v_heads[index]

        def rows(step, carry):
            here = pl.ds(pl.multiple_of(step * half, half), half)
            scores = dot_right_t(r.q_heads[index, here, :], keys) * ROOT
            expon = jnp.exp(scores - jnp.max(scores, axis=-1, keepdims=True))
            soft = (expon * (1.0 / jnp.sum(expon, axis=-1, keepdims=True))).astype(BF16)
            r.soft[index, here, :] = soft
            r.o_heads[index, here, :] = dot(soft, values).astype(BF16)
            return carry

        return lax.fori_loop(0, 2, rows, carry)

    mixed_moves = []
    for latent in range(count):
        lax.fori_loop(latent * heads, (latent + 1) * heads, attend, 0)

        def assemble(block, carry, latent=latent):
            row = pl.multiple_of(block * tokens, tokens)
            pieces = [
                r.o_heads[latent * heads + head, pl.ds(row, tokens), :][:, :HEAD_DIM]
                for head in range(heads)
            ]
            r.mixed_send[block, latent] = jnp.concatenate(pieces, axis=1)
            return carry

        lax.fori_loop(0, seq, assemble, 0)
        own = local(r.mixed_send.at[s_me, latent], r.mixed_recv.at[s_me, latent])
        mixed_moves.append(
            (
                own,
                exchange(
                    lambda peer, latent=latent: r.mixed_send.at[peer, latent],
                    lambda me, latent=latent: r.mixed_recv.at[me, latent],
                ),
            )
        )
        if latent == 0:
            gather_fc1.forward()
            out_chip.wait_recv()
            other = rows_of(r.out_blocks, seq_peer(2) * out_wide, out_wide)
            out_last = send(other, other, device_seq(1))
    og_moves[0].forward()
    gather_fc2.forward(1)

    out_core.wait_recv()
    out_last.wait_recv()
    pending.extend([out_core, out_chip, out_last])

    def tighten_out(step, carry):
        blocks = [
            r.out_blocks[pl.ds(pl.multiple_of(block * out_wide + step * pad, 16), pad), :]
            for block in range(seq)
        ]
        start = pl.multiple_of(step * sz.chunk, 16)
        packed = dot(tighten, jnp.concatenate(blocks, axis=0))
        r.out[pl.ds(start, sz.chunk), :] = packed.astype(BF16)
        return carry

    lax.fori_loop(0, sz.dp, tighten_out, 0)

    m2_moves = []
    for latent in range(count):
        own, moves = mixed_moves[latent]
        own.wait()
        settle(moves)
        pieces = [r.mixed_recv[block, latent] for block in range(seq)]
        mixed = jnp.concatenate(pieces, axis=1)
        here = pl.ds(latent * tokens, tokens)
        r.mixed[here, :] = mixed
        r.attended[here, :] = dot(mixed, r.out[...]) + r.bias_out[...]

        def second_norm(step, carry, latent=latent):
            start = pl.multiple_of(step * ROWS, ROWS)
            here = pl.ds(latent * tokens + start, ROWS)
            tokens_in = r.latents[latent, pl.ds(start, ROWS), :].astype(F32)
            middle = tokens_in + mod[latent, 2:3, :] * r.attended[here, :]
            r.middle[here, :] = middle
            normed, _ = layer_norm(middle)
            modded = normed * (1.0 + mod[latent, 4:5, :]) + mod[latent, 3:4, :]
            place = pl.multiple_of((latent * seq + s_me) * tokens + start, ROWS)
            r.modded_two[pl.ds(place, ROWS), :] = modded.astype(BF16)
            return carry

        lax.fori_loop(0, tokens // ROWS, second_norm, 0)
        m2_moves.append(GatherTokens(r.modded_two, latent))

    for latent in range(1, count):
        og_moves.append(GatherTokens(r.grad_branch, latent, r.out_grad.at[latent]))
    gather_fc2.forward(1)
    for copy in og_local:
        copy.wait()
    for move in lat_moves:
        release(move.last)

    def gate_grads(step, carry):
        here = pl.ds(pl.multiple_of(step * ROWS, ROWS), ROWS)
        gate = mod[step // (length // ROWS), 5:6, :]
        r.grad_branch[here, :] = (r.grad_branch[here, :].astype(F32) * gate).astype(BF16)
        return carry

    def gate_latent(latent):
        og_moves[latent].finish()
        release(og_moves[latent].last)
        steps = length // ROWS
        lax.fori_loop(latent * steps, (latent + 1) * steps, gate_grads, 0)

    gate_latent(0)
    m2_moves[0].forward()
    gather_fc2.forward()

    cuts = column_cuts(sz.hidden, 256)
    gather_fc1.finish()
    for latent in range(count):
        m2_moves[latent].finish()

        def mlp(step, carry, latent=latent):
            start = pl.multiple_of(latent * length + step * tile, tile)
            rows = r.modded_two[pl.ds(start, tile), :]
            for column, size in cuts:
                here = slice(column, column + size)
                hidden = dot(rows, r.fc1[:, here]) + r.bias_fc1[:, here]
                square = hidden * hidden
                inner = 0.7978845608028654 * (hidden + 0.044715 * square * hidden)
                bent = jnp.tanh(inner)
                r.lat_all[pl.ds(start, tile), here] = (0.5 * hidden * (1.0 + bent)).astype(BF16)
                slope = 0.5 * (1.0 + bent) + 0.5 * hidden * (1.0 - bent * bent) * (
                    0.7978845608028654 * (1.0 + 3 * 0.044715 * square)
                )
                r.part_a[pl.ds(start, tile), here] = slope.astype(BF16)
            return carry

        lax.fori_loop(0, per_latent, mlp, 0)
        if latent + 1 < count:
            m2_moves[latent + 1].forward()

    for copy in (out_core, out_chip, out_last):
        release(copy)
    gather_out.drain()

    def weight_grad(left, right, target):
        size = 384 if width % 384 == 0 else LANES

        def tiles(step, carry):
            start = pl.multiple_of(step * size, LANES)
            sums = dot_left_t(left[:, pl.ds(start, size)], right[...])
            target[pl.ds(start, size), :] = sums.astype(BF16)
            return carry

        lax.fori_loop(0, left.shape[1] // size, tiles, 0)

    for latent in range(1, count):
        og_moves[latent].forward()
        gate_latent(latent)
    weight_grad(r.lat_all, r.grad_branch, r.out_blocks)
    sum_fc2 = SumWeights(r.out_blocks, sz.units, r.across_b, r.along_b, width)
    sum_fc2.push()

    gather_fc2.finish()
    r.fc1_sums[...] = jnp.zeros_like(r.fc1_sums)
    grad_moves = []
    for latent in range(count):

        def mlp_back(step, carry, latent=latent):
            start = pl.multiple_of(latent * length + step * tile, tile)
            incoming = r.grad_branch[pl.ds(start, tile), :]
            for column, size in cuts:
                here = slice(column, column + size)
                slope = r.part_a[pl.ds(start, tile), here].astype(F32)
                grads = (dot_right_t(incoming, r.fc2[here, :]) * slope).astype(BF16)
                r.grad_hidden[pl.ds(start, tile), here] = grads
                r.fc1_sums[:, here] += jnp.sum(grads.astype(F32), axis=0, keepdims=True)
            return carry

        lax.fori_loop(0, per_latent, mlp_back, 0)
        if latent:
            grad_moves[latent - 1].forward()

        def back_fc1(step, carry, latent=latent):
            start = pl.multiple_of(latent * length + step * tile, tile)
            rows = r.grad_hidden[pl.ds(start, tile), :]
            for column, size in column_cuts(width):
                here = slice(column, column + size)
                sums = dot_right_t(rows, r.fc1[here, :])
                r.part_a[pl.ds(start, tile), here] = sums.astype(BF16)
            return carry

        lax.fori_loop(0, per_latent, back_fc1, 0)
        grad_moves.append(SumTokens(r.part_a, 0, latent))

    for move in m2_moves:
        for copy in (move.core, move.chip, move.last):
            release(copy)
    gather_fc1.drain()
    grad_moves[-1].forward()
    weight_grad(r.modded_two, r.grad_hidden, r.fc1)
    sum_fc1 = SumWeights(r.fc1, sz.chunk, r.across_a, r.along_a, sz.hidden)
    sum_fc1.push()

    grad_mod = r.grad_mod
    grad_mod[...] = jnp.zeros_like(grad_mod)

    def total_rows(values):
        return jnp.sum(values, axis=0, keepdims=True)

    r.bias_sums[...] = jnp.zeros_like(r.bias_sums)
    mix_moves = []
    for latent in range(count):
        grad_moves[latent].finish()

        def second_back(step, carry, latent=latent):
            start = pl.multiple_of(step * ROWS, ROWS)
            here = pl.ds(latent * tokens + start, ROWS)
            incoming = grad_moves[latent].rows(start)
            normed, inverse = layer_norm(r.middle[here, :])
            grad_mod[latent, 3:4, :] += total_rows(incoming)
            grad_mod[latent, 4:5, :] += total_rows(incoming * normed)
            grad_middle = r.out_grad[latent, pl.ds(start, ROWS), :].astype(F32) + norm_back(
                incoming * (1.0 + mod[latent, 4:5, :]), normed, inverse
            )
            r.grad_middle[here, :] = grad_middle
            grad_mod[latent, 2:3, :] += total_rows(grad_middle * r.attended[here, :])
            grad_attended = (mod[latent, 2:3, :] * grad_middle).astype(BF16)
            r.grad_attended[here, :] = grad_attended
            r.bias_sums[0:1, :] += total_rows(grad_attended.astype(F32))
            return carry

        lax.fori_loop(0, tokens // ROWS, second_back, 0)
        sum_fc2.forward(1)
        here = pl.ds(latent * tokens, tokens)
        grad_mixed = dot_right_t(r.grad_attended[here, :], r.out[...])
        for copy in mixed_moves[latent][1]:
            release(copy)
        for block in range(seq):
            piece = grad_mixed[:, block * part : (block + 1) * part].astype(BF16)
            r.mixed_send[block, latent] = piece
        own = local(r.mixed_send.at[s_me, latent], r.mixed_recv.at[s_me, latent])
        mix_moves.append(
            (
                own,
                exchange(
                    lambda peer, latent=latent: r.mixed_send.at[peer, latent],
                    lambda me, latent=latent: r.mixed_recv.at[me, latent],
                ),
            )
        )

    gather_fc2.drain()
    branch_moves = []
    for latent in range(count):

        def branch_out(step, carry, latent=latent):
            start = pl.multiple_of(latent * length + step * tile, tile)
            sums = dot(r.lat_all[pl.ds(start, tile), :], r.fc2[...])
            r.lat_all[pl.ds(start, tile), :] = sums.astype(BF16)
            return carry

        lax.fori_loop(0, per_latent, branch_out, 0)
        branch_moves.append(SumTokens(r.lat_all, 1, latent))
    sum_fc2.forward()

    for move in branch_moves:
        move.forward()

    def attend_back(index, carry):
        queries, keys, values = r.q_heads[index], r.k_heads[index], r.v_heads[index]
        incoming = r.o_heads[index]
        r.v_heads[index] = dot_left_t(r.soft[index], incoming).astype(BF16)

        def rows(step, carry):
            here = pl.ds(pl.multiple_of(step * half, half), half)
            soft = r.soft[index, here, :].astype(F32)
            grad_soft = dot_right_t(r.o_heads[index, here, :], values)
            delta = jnp.sum(soft * grad_soft, axis=-1, keepdims=True)
            r.soft[index, here, :] = (soft * (grad_soft - delta)).astype(BF16)
            return carry

        lax.fori_loop(0, 2, rows, 0)
        r.q_heads[index] = (dot(r.soft[index], keys) * ROOT).astype(BF16)
        r.k_heads[index] = (dot_left_t(r.soft[index], queries) * ROOT).astype(BF16)
        return carry

    fc_rows = rows_of(r.attended, 0, sz.units)
    joined_sums = r.joined_sums
    grad_joined = r.grad_hidden.at[:, pl.ds(0, sz.joined)]
    joined_sums[...] = jnp.zeros_like(joined_sums)
    token_moves = []
    for latent in range(count):
        own, moves = mix_moves[latent]
        own.wait()
        settle(moves)

        def unpack(block, carry, latent=latent):
            row = pl.multiple_of(block * tokens, tokens)
            values = r.mixed_recv[block, latent]
            for head in range(heads):
                piece = pad_head(values[:, head * HEAD_DIM : (head + 1) * HEAD_DIM])
                r.o_heads[latent * heads + head, pl.ds(row, tokens), :] = piece
            return carry

        lax.fori_loop(0, seq, unpack, 0)
        middle_head = latent * heads + heads // 2
        lax.fori_loop(latent * heads, middle_head, attend_back, 0)
        if latent:
            token_moves[latent - 1].forward()
            sum_fc1.forward(1)
        lax.fori_loop(middle_head, (latent + 1) * heads, attend_back, 0)
        sum_fc1.forward(1)

        def join(block, carry, latent=latent):
            row = pl.multiple_of(block * tokens, tokens)
            start = pl.multiple_of(latent * length + block * tokens, tokens)
            pieces = [
                source[latent * heads + head, pl.ds(row, tokens), :][:, :HEAD_DIM]
                for source in (r.q_heads, r.k_heads, r.v_heads)
                for head in range(heads)
            ]
            if sz.joined > 3 * part:
                pieces.append(jnp.zeros((tokens, sz.joined - 3 * part), BF16))
            values = jnp.concatenate(pieces, axis=1)
            joined_sums[...] += total_rows(values.astype(F32))
            grad_joined[pl.ds(start, tokens), :] = values
            return carry

        lax.fori_loop(0, seq, join, 0)

        def back_qkv(step, carry, latent=latent):
            start = pl.multiple_of(latent * length + step * tile, tile)
            rows = grad_joined[pl.ds(start, tile), :]
            for column, size in column_cuts(width):
                here = slice(column, column + size)
                sums = dot_right_t(rows, r.qkv[here, :])
                r.part_a[pl.ds(start, tile), here] = sums.astype(BF16)
            return carry

        lax.fori_loop(0, per_latent, back_qkv, 0)
        token_moves.append(SumTokens(r.part_a, 0, latent))

    token_moves[-1].forward()
    sum_fc2.finish(fc_rows)
    fc2_move = local(fc_rows, r.fc2_out)
    pl.semaphore_signal(r.free_x, inc=1, device_id=device_x, device_id_type=MESH)
    for step in range(1, line):
        pl.semaphore_signal(
            r.free_z, inc=1, device_id=device_z(step), device_id_type=MESH
        )
    gather_qkv.drain()
    weight_grad(r.modded, grad_joined, r.qkv)
    sum_qkv = SumWeights(r.qkv, sz.chunk, r.across_b, r.along_b, sz.joined)
    pl.semaphore_wait(r.free_x, 1)
    sum_qkv.push()
    sum_fc1.forward()


    weight_grad(r.mixed, r.grad_attended, r.out)

    def loosen_out(step, carry):
        start = pl.multiple_of(step * sz.chunk, 16)
        spread = dot(loosen, r.out[pl.ds(start, sz.chunk), :]).astype(BF16)
        for block in range(seq):
            place = pl.multiple_of(block * out_wide + step * pad, 16)
            r.out_blocks[pl.ds(place, pad), :] = spread[block * pad : (block + 1) * pad, :]
        return carry

    lax.fori_loop(0, sz.dp, loosen_out, 0)
    out_first = [
        send(
            rows_of(r.out_blocks, (y * 2 + 1 - c_me) * out_wide, out_wide),
            rows_of(r.grad_branch, y * out_wide, out_wide),
            device_seq(1),
        )
        for y in range(2)
    ]

    def out_from_core(y):
        return rows_of(r.grad_branch, y * out_wide, out_wide)[...].astype(F32)

    other = rows_of(r.out_blocks, ((1 - y_me) * 2 + c_me) * out_wide, out_wide)
    out_chip_sum = rows_of(r.modded_two, 2 * count * tokens, out_wide)

    def out_half(index):
        start, size = index * (out_wide // 2), out_wide // 2
        return send(rows_of(other, start, size), rows_of(out_chip_sum, start, size), device_seq(2))

    for latent in range(count):
        branch_moves[latent].finish()

        def final_output(step, carry, latent=latent):
            start = pl.multiple_of(step * ROWS, ROWS)
            here = pl.ds(latent * tokens + start, ROWS)
            branch = branch_moves[latent].rows(start) + r.bias_fc2[...]
            grad_output = r.out_grad[latent, pl.ds(start, ROWS), :].astype(F32)
            gate = mod[latent, 5:6, :]
            r.modded_two[here, :] = (r.middle[here, :] + gate * branch).astype(BF16)
            grad_mod[latent, 5:6, :] += total_rows(grad_output * branch)
            r.bias_sums[1:2, :] += total_rows((gate * grad_output).astype(BF16).astype(F32))
            return carry

        lax.fori_loop(0, tokens // ROWS, final_output, 0)
        slot = rows_of(r.modded_two, latent * tokens, tokens)
        far_moves.append(local(slot, r.output.at[latent]))
    for copy in out_first:
        copy.wait_recv()
    other[...] = (other[...].astype(F32) + out_from_core(1 - y_me)).astype(BF16)
    out_second = [out_half(0)]
    pl.semaphore_wait(r.free_z, line - 1)
    sum_qkv.forward(1)
    for latent in range(count):
        token_moves[latent].finish()

        def final_grads(step, carry, latent=latent):
            start = pl.multiple_of(step * ROWS, ROWS)
            here = pl.ds(latent * tokens + start, ROWS)
            incoming = token_moves[latent].rows(start)
            normed, inverse = layer_norm(r.latents[latent, pl.ds(start, ROWS), :].astype(F32))
            grad_mod[latent, 0:1, :] += total_rows(incoming)
            grad_mod[latent, 1:2, :] += total_rows(incoming * normed)
            grads = r.grad_middle[here, :] + norm_back(
                incoming * (1.0 + mod[latent, 1:2, :]), normed, inverse
            )
            place = pl.ds((count + latent) * tokens + start, ROWS)
            r.modded_two[place, :] = grads.astype(BF16)
            return carry

        lax.fori_loop(0, tokens // ROWS, final_grads, 0)
        slot = rows_of(r.modded_two, (count + latent) * tokens, tokens)
        far_moves.append(local(slot, r.latents_grad.at[latent]))

    def return_rows(total, send_ref, recv_ref):
        send_ref[...] = dot(loosen, total.astype(BF16)).astype(BF16)
        mine = rows_of(send_ref, s_me * pad, pad)
        own = local(mine, rows_of(recv_ref, s_me * pad, pad))
        moves = exchange(
            lambda peer: rows_of(send_ref, peer * pad, pad),
            lambda me: rows_of(recv_ref, me * pad, pad),
        )
        return own, moves

    def small(values):
        return values.reshape(count * 8, width)

    r.grad_core_send[...] = small(grad_mod[...])
    mod_core = send(r.grad_core_send, r.grad_core, device_seq(1))

    def own_place(sums, column):
        return place(sums[:, column : column + part], s_me * part, width)

    sums = joined_sums[...]
    r.bias_sums[2:3, :] = own_place(sums, 0)
    r.bias_sums[3:4, :] = own_place(sums, 2 * part)
    for position in range(seq):
        r.bias_sums[4 + position : 5 + position, :] = when(s_me == position, r.fc1_sums[...])
    bias_x = send(r.bias_sums, r.bias_x, device_x)
    mod_core.wait_recv()
    r.grad_chip_send[...] = r.grad_core_send[...] + r.grad_core[...]
    mod_chip = send(r.grad_chip_send, r.grad_chip, device_seq(2))
    out_second.append(out_half(1))
    fc2_move.wait()
    sum_fc1.finish(fc_rows)
    fc1_own, fc1_back = return_rows(fc_rows[...], r.fc1_blocks, r.fc1_rows)
    bias_x.wait_recv()
    r.bias_half[...] = r.bias_sums[...] + r.bias_x[...]
    mod_chip.wait_recv()
    rows_of(r.bias_all, dp_me * 16, 16)[...] = (r.grad_chip_send[...] + r.grad_chip[...]).astype(
        BF16
    )
    gather_grad = GatherWeights(r.bias_all, 16)
    gather_grad.push()
    room_z = r.mod_z.at[:, :, pl.ds(0, width)]
    bias_z = [send(r.bias_half, room_z.at[step], device_z(step)) for step in range(1, line)]
    gather_grad.forward()
    sum_qkv.forward(1)
    pending.extend([mod_core, bias_x, mod_chip] + bias_z)
    bias_total = r.bias_half[...]
    for copy, step in zip(bias_z, range(1, line)):
        copy.wait_recv()
        bias_total = bias_total + room_z[step]
    r.bias_line[...] = bias_total
    bias_core = send(r.bias_line, r.bias_core, device_seq(1))

    gather_grad.finish()
    all_grads = r.bias_all[...]
    rows = sz.dp * 16
    comp_of = iota((rows, rows), 0) & 7
    source = (iota((rows, rows), 0) & ~15) + ((iota((rows, rows), 0) >> 3) & 1)
    spread = jnp.where(iota((rows, rows), 1) == source, 1.0, 0.0).astype(BF16)
    cond_spread = dot(spread, r.cond_mine[...])
    comp_of = iota((rows, LANES), 0) & 7
    cond_grads = jnp.zeros((rows, sz.rows), F32)
    mod_rows = r.mod_out.shape[0]
    for comp in range(6):
        back = dot_right_t(all_grads, r.w_mod[:, comp * width : (comp + 1) * width])
        cond_grads = cond_grads + jnp.where(comp_of[:, : sz.rows] == comp, back, 0.0)
    cond_grads = jnp.sum(cond_grads.reshape(rows // 8, 8, sz.rows), axis=1)
    blank = jnp.zeros((16, width - sz.rows), F32)
    cond_grads = pltpu.roll(jnp.concatenate([cond_grads, blank], axis=1), me * sz.rows, 1)
    keep = iota((8, 16), 0)
    hits = []
    for side in range(2):
        hits.append(
            sum(
                when(
                    iota((8, width), 0) == along * count + latent,
                    jnp.broadcast_to(
                        cond_grads[
                            (along * 2 + side) * count + latent : (along * 2 + side) * count
                            + latent
                            + 1,
                            :,
                        ],
                        (8, width),
                    ),
                )
                for along in range(line)
                for latent in range(count)
            )
        )
    r.cond_sides[0] = hits[0]
    r.cond_sides[1] = hits[1]
    cond_x = send(r.cond_sides.at[1 - x_me], r.cond_x, device_x)
    bias_core.wait_recv()
    r.bias_pair[...] = r.bias_line[...] + r.bias_core[...]
    bias_chip = send(r.bias_pair, r.bias_chip, device_seq(2))
    comp_rows = iota((8, rows), 0) == (iota((8, rows), 1) & 7)
    mod_bias = dot(jnp.where(comp_rows, 1.0, 0.0).astype(BF16), all_grads)
    cond_x.wait_recv()
    r.cond_half[...] = r.cond_sides[x_me] + r.cond_x[...]
    cond_z = [send(r.cond_half, r.cond_z.at[step], device_z(step)) for step in range(1, line)]
    sum_qkv.forward(1)
    for copy in out_second:
        copy.wait_recv()
    mine = out_mine[...].astype(F32) + out_from_core(y_me)
    out_mine[...] = (mine + out_chip_sum[...].astype(F32)).astype(BF16)
    pending.extend(out_first + out_second)
    sum_out = SumWeights(out_mine, pad, r.across_out, r.along_out, width)
    sum_out.push()
    cond_total = r.cond_half[...]
    for copy, step in zip(cond_z, range(1, line)):
        copy.wait_recv()
        cond_total = cond_total + r.cond_z[step]
    r.cond_line[...] = cond_total
    cond_core = send(r.cond_line, r.cond_core, device_seq(1))
    sum_qkv.forward()
    cond_core.wait_recv()
    r.cond_pair[...] = r.cond_line[...] + r.cond_core[...]
    cond_chip = send(r.cond_pair, r.cond_chip, device_seq(2))
    for comp in range(6):
        chosen = jnp.where(comp_of == comp, cond_spread, 0.0).astype(BF16)
        place_rows = rows_of(r.grad_middle, comp * mod_rows, mod_rows)
        place_rows[...] = dot_left_t(chosen, all_grads)[:mod_rows, :]
        far_moves.append(local(place_rows, r.mod_out.at[:, pl.ds(comp * width, width)]))
    sum_out.forward(1)
    bias_chip.wait_recv()
    bias_full = r.bias_pair[...] + r.bias_chip[...]

    def own_lanes(row, start):
        size = row.shape[1]
        turned = pltpu.roll(jnp.broadcast_to(row, (8, size)), lax.rem(size - start, size), 1)
        return turned[0:1, : 2 * LANES]

    qv_total = when(me < half_way, bias_full[2:3, :]) + when(me >= half_way, bias_full[3:4, :])
    fc1_total = sum(
        when(s_me == position, bias_full[4 + position : 5 + position, :])
        for position in range(seq)
    )
    first = me * (6 * sz.rows) // width
    comp_row = iota((8, width), 0)
    pair = [
        jnp.sum(jnp.where(comp_row == first + more, mod_bias, 0.0), axis=0, keepdims=True)
        for more in range(2)
    ]
    r.small_out[...] = jnp.concatenate(
        [
            own_lanes(bias_full[0:1, :], me * sz.rows),
            own_lanes(bias_full[1:2, :], me * sz.rows),
            own_lanes(qv_total, lax.rem(me, half_way) * (2 * sz.rows)),
            own_lanes(fc1_total, dp_me * sz.units),
            own_lanes(jnp.concatenate(pair, axis=1), me * (6 * sz.rows) - first * width),
            jnp.zeros((3, 2 * LANES), F32),
        ],
        axis=0,
    )
    qkv_total = fc_rows.at[:, pl.ds(0, sz.joined)]
    sum_qkv.finish(qkv_total)
    qkv_own, qkv_back = return_rows(qkv_total[...], r.qkv_blocks, r.qkv_rows)
    sum_out.forward()
    out_rows = rows_of(r.middle, 0, pad)
    sum_out.finish(out_rows)
    far_moves.append(local(out_rows, r.out_out))
    gather_grad.drain()
    cond_chip.wait_recv()
    cond_full = r.cond_pair[...] + r.cond_chip[...]
    picked = [
        jnp.sum(
            jnp.where(comp_row == z_me * count + latent, cond_full, 0.0), axis=0, keepdims=True
        )
        for latent in range(count)
    ]
    slope = gate_cond * (1.0 + cond * (1.0 - gate_cond))
    r.cond_grad[...] = (jnp.concatenate(picked, axis=0) * slope).astype(BF16)
    pending.extend([bias_core, bias_chip, cond_x, cond_core, cond_chip] + cond_z)
    for own, moves in ((fc1_own, fc1_back), (qkv_own, qkv_back)):
        own.wait()
        settle(moves)
    far_moves.append(local(r.fc1_rows, r.fc1_out))
    far_moves.append(local(r.qkv_rows, r.qkv_out))
    for copy in far_moves:
        copy.wait()
    for copy in pending:
        copy.wait_send()


class Inputs(NamedTuple):
    latents: object
    out_grad: object
    conditioning: object
    bias: object
    w_mod: object
    qkv_src: object
    fc1_src: object
    out_src: object
    fc2_src: object


class Outputs(NamedTuple):
    output: object
    latents_grad: object
    cond_grad: object
    mod_out: object
    small_out: object
    qkv_out: object
    out_out: object
    fc1_out: object
    fc2_out: object


def kernel_scratch(sz):
    low = lambda *shape: pltpu.VMEM(shape, BF16)
    full = lambda *shape: pltpu.VMEM(shape, F32)
    count, tokens, width, seq = sz.count, sz.tokens, sz.width, sz.seq
    pad, groups = sz.padded_rows, sz.count * sz.heads
    tall = sz.chunk if sz.chunk > sz.units else sz.units
    wide = max(sz.joined, sz.hidden, width)
    return dict(
        lat_all=low(sz.total, max(width, sz.hidden)),
        grad_branch=low(sz.total, width),
        modded=low(sz.total, width),
        q_heads=low(groups, sz.length, LANES),
        k_heads=low(groups, sz.length, LANES),
        v_heads=low(groups, sz.length, LANES),
        o_heads=low(groups, sz.length, LANES),
        soft=low(groups, sz.length, sz.length),
        mixed_send=low(seq, count, tokens, sz.part),
        mixed_recv=low(seq, count, tokens, sz.part),
        mixed=low(sz.own, width),
        attended=full(sz.own, width),
        middle=full(sz.own, width),
        grad_middle=full(sz.own, width),
        grad_attended=low(sz.own, width),
        modded_two=low(sz.total, width),
        grad_hidden=low(sz.total, sz.hidden),
        part_a=low(sz.total, width),
        sum_core=low(2, 2, count, tokens, width),
        sum_send=low(2, count, tokens, width),
        sum_chip=low(2, count, tokens, width),
        qkv_raw=low(sz.rows, 3 * width),
        fc1_raw=low(sz.rows, seq * sz.hidden),
        out_raw=low(sz.rows, width),
        qkv_blocks=low(seq * pad, sz.joined),
        fc1_blocks=low(seq * pad, sz.hidden),
        qkv_rows=low(seq * pad, sz.joined),
        fc1_rows=low(seq * pad, sz.hidden),
        out_blocks=low(seq * sz.dp * pad, width),
        qkv=low(width, sz.joined),
        fc1=low(width, sz.hidden),
        fc2=low(sz.hidden, width),
        out=low(width, width),
        across_a=low(sz.line, sz.chunk, wide),
        along_a=low(sz.line, sz.chunk, wide),
        across_b=low(sz.line, tall, wide),
        along_b=low(sz.line, tall, wide),
        across_out=low(sz.line, pad, width),
        along_out=low(sz.line, pad, width),
        cond_all=low(sz.dp * 16, width),
        cond_mine=low(sz.dp * 16, LANES),
        bias_blocks=low(seq * 16, width),
        bias_all=low(sz.dp * 16, width),
        mod_sums=full(16, sz.mod_part * seq),
        mod_core=full(2, 16, sz.mod_part),
        mod_send=full(16, sz.mod_part),
        mod_chip=full(16, sz.mod_part),
        mod_sum=full(16, sz.mod_part),
        mod_x=full(8, sz.mod_part),
        mod_half=full(8, sz.mod_part),
        mod_z=full(sz.line, 8, sz.mod_part),
        mod_all=full(seq, 8, sz.mod_part),
        modulation=full(count, 8, width),
        bias_joined=full(1, sz.joined),
        bias_out=full(1, width),
        bias_fc1=full(1, width),
        bias_fc2=full(1, width),
        joined_sums=full(1, sz.joined),
        fc1_sums=full(1, sz.hidden),
        grad_mod=full(count, 8, width),
        grad_core_send=full(16, width),
        grad_core=full(16, width),
        grad_chip_send=full(16, width),
        grad_chip=full(16, width),
        bias_sums=full(8, width),
        bias_x=full(8, width),
        bias_half=full(8, width),
        bias_line=full(8, width),
        bias_core=full(8, width),
        bias_pair=full(8, width),
        bias_chip=full(8, width),
        cond_sides=full(2, 8, width),
        cond_x=full(8, width),
        cond_half=full(8, width),
        cond_z=full(sz.line, 8, width),
        cond_line=full(8, width),
        cond_core=full(8, width),
        cond_pair=full(8, width),
        cond_chip=full(8, width),
        send_sems=pltpu.SemaphoreType.DMA((200,)),
        recv_sems=pltpu.SemaphoreType.DMA((200,)),
        free_x=pltpu.SemaphoreType.REGULAR,
        free_z=pltpu.SemaphoreType.REGULAR,
        local_sems=pltpu.SemaphoreType.DMA((40,)),
    )


def kernel_outputs(sz):
    low = lambda *shape: jax.ShapeDtypeStruct(shape, BF16)
    full = lambda *shape: jax.ShapeDtypeStruct(shape, F32)
    count, tokens, width, pad = sz.count, sz.tokens, sz.width, sz.padded_rows
    return [
        low(count, tokens, width),
        low(count, tokens, width),
        low(count, width),
        full(-(-sz.rows // 8) * 8, 6 * width),
        full(8, 2 * LANES),
        low(sz.seq * pad, sz.joined),
        full(pad, width),
        low(sz.seq * pad, sz.hidden),
        full(sz.units, width),
    ]


def run_kernel(sz, *operands):
    vmem = pl.BlockSpec(memory_space=pltpu.VMEM)
    far = pl.BlockSpec(memory_space=pl.ANY)
    outputs = kernel_outputs(sz)
    return pl.pallas_call(
        partial(block_kernel, sz),
        out_shape=outputs,
        in_specs=[vmem] * 5 + [far] * 4,
        out_specs=[far, far, vmem, far, vmem, far, far, far, far],
        scratch_shapes=list(kernel_scratch(sz).values()),
        compiler_params=pltpu.CompilerParams(
            collective_id=0, has_side_effects=True, vmem_limit_bytes=66584576
        ),
    )(*operands)


def general_path(
    latents, out_grad, modulation, blocks, w_out, w_fc2, bias_qv, bias_out, bias_fc1, bias_fc2
):
    count, tokens, width = latents.shape
    dp, seq = lax.axis_size("dp"), lax.axis_size("seq")
    both = ("dp", "seq")
    qkv_blocks, fc1_blocks = blocks
    rows = qkv_blocks.shape[1]
    part, heads, length = width // seq, HEADS // seq, seq * tokens
    shift_att, scale_att, gate_att, shift_mlp, scale_mlp, gate_mlp = [
        modulation[:, index : index + 1] for index in range(6)
    ]

    def to_columns(blocks):
        mine = lax.all_to_all(blocks, "seq", 0, 0, tiled=True).reshape(seq * rows, -1)
        return lax.all_gather(mine, "dp", axis=0, tiled=True)

    full_qkv = to_columns(qkv_blocks)
    full_out = lax.all_gather(w_out, both, axis=0, tiled=True)
    full_fc1 = to_columns(fc1_blocks)
    full_fc2 = lax.all_gather(w_fc2, "dp", axis=0, tiled=True)

    def gather_tokens(values):
        return lax.all_gather(values, "seq", axis=1, tiled=True)

    def flat(values):
        return values.reshape(-1, values.shape[-1])

    tokens_f = latents.astype(F32)
    normed, inverse = layer_norm(tokens_f)
    modded = (normed * (1.0 + scale_att) + shift_att).astype(BF16)
    modded_all = flat(gather_tokens(modded))
    joined = dot(modded_all, full_qkv).reshape(count, length, 3, heads, HEAD_DIM)
    bias_q = bias_qv[0].reshape(heads, HEAD_DIM)
    bias_v = bias_qv[1].reshape(heads, HEAD_DIM)
    queries = (joined[:, :, 0] + bias_q).astype(BF16)
    keys = joined[:, :, 1].astype(BF16)
    values = (joined[:, :, 2] + bias_v).astype(BF16)
    scores = jnp.einsum("bqhd,bkhd->bhqk", queries, keys, preferred_element_type=F32) * (
        HEAD_DIM ** (-0.5)
    )
    soft = jax.nn.softmax(scores, axis=-1)
    soft_low = soft.astype(BF16)
    mixed = jnp.einsum("bhqk,bkhd->bqhd", soft_low, values, preferred_element_type=F32)
    mixed = mixed.astype(BF16).reshape(count, length, part)
    mixed_mine = lax.all_to_all(mixed, "seq", 1, 2, tiled=True)
    attended = dot(mixed_mine, full_out) + bias_out
    middle = tokens_f + gate_att * attended
    normed_two, inverse_two = layer_norm(middle)
    modded_two = (normed_two * (1.0 + scale_mlp) + shift_mlp).astype(BF16)
    modded_two_all = flat(gather_tokens(modded_two))
    hidden = dot(modded_two_all, full_fc1) + bias_fc1
    active, gelu_back = jax.vjp(partial(jax.nn.gelu, approximate=True), hidden)
    active = active.astype(BF16)

    def sum_tokens(partial_sums):
        parts = partial_sums.astype(BF16).reshape(count, length, width)
        return lax.psum_scatter(parts, "seq", scatter_dimension=1, tiled=True).astype(F32)

    branch = sum_tokens(dot(active, full_fc2)) + bias_fc2
    output = middle + gate_mlp * branch

    grad_output = out_grad.astype(F32)
    grad_gate_mlp = jnp.sum(grad_output * branch, axis=1)
    grad_branch = (gate_mlp * grad_output).astype(BF16)
    grad_branch_all = flat(gather_tokens(grad_branch))
    grad_hidden = gelu_back(dot_right_t(grad_branch_all, full_fc2))[0].astype(BF16)
    grad_modded_two = sum_tokens(dot_right_t(grad_hidden, full_fc1))
    grad_shift_mlp = jnp.sum(grad_modded_two, axis=1)
    grad_scale_mlp = jnp.sum(grad_modded_two * normed_two, axis=1)
    grad_middle = grad_output + norm_back(
        grad_modded_two * (1.0 + scale_mlp), normed_two, inverse_two
    )
    grad_gate_att = jnp.sum(grad_middle * attended, axis=1)
    grad_attended = (gate_att * grad_middle).astype(BF16)
    grad_mixed = dot_right_t(flat(grad_attended), full_out).astype(BF16)
    grad_mixed = lax.all_to_all(grad_mixed.reshape(latents.shape), "seq", 2, 1, tiled=True)
    grad_mixed = grad_mixed.reshape(count, length, heads, HEAD_DIM)
    grad_soft = jnp.einsum("bqhd,bkhd->bhqk", grad_mixed, values, preferred_element_type=F32)
    delta = jnp.sum(soft * grad_soft, axis=-1, keepdims=True)
    grad_scores = (soft * (grad_soft - delta)).astype(BF16)
    scale = HEAD_DIM ** (-0.5)
    grad_q = jnp.einsum("bhqk,bkhd->bqhd", grad_scores, keys, preferred_element_type=F32) * scale
    grad_k = jnp.einsum("bhqk,bqhd->bkhd", grad_scores, queries, preferred_element_type=F32) * scale
    grad_v = jnp.einsum("bhqk,bqhd->bkhd", soft_low, grad_mixed, preferred_element_type=F32)
    grad_joined = jnp.concatenate(
        [item.astype(BF16).reshape(count * length, part) for item in (grad_q, grad_k, grad_v)],
        axis=1,
    )
    grad_modded = sum_tokens(dot_right_t(grad_joined, full_qkv))
    grad_shift_att = jnp.sum(grad_modded, axis=1)
    grad_scale_att = jnp.sum(grad_modded * normed, axis=1)
    grad_tokens = grad_middle + norm_back(grad_modded * (1.0 + scale_att), normed, inverse)

    def from_columns(sums, groups):
        mine = lax.psum_scatter(sums.astype(BF16), "dp", scatter_dimension=0, tiled=True)
        blocks = lax.all_to_all(mine.reshape(seq, rows, -1), "seq", 0, 0, tiled=True)
        blocks = blocks.astype(F32).reshape(seq, rows, groups, -1)
        return blocks.transpose(1, 2, 0, 3).reshape(rows, -1)

    sums_fc2 = lax.psum_scatter(
        dot_left_t(active, grad_branch_all).astype(BF16), "dp", scatter_dimension=0, tiled=True
    ).astype(F32)
    sums_fc1 = from_columns(dot_left_t(modded_two_all, grad_hidden), dp)
    sums_out = lax.psum_scatter(
        dot_left_t(flat(mixed_mine), flat(grad_attended)).astype(BF16),
        both,
        scatter_dimension=0,
        tiled=True,
    ).astype(F32)
    sums_qkv = from_columns(dot_left_t(modded_all, grad_joined), 3)

    grad_mod = jnp.stack(
        [
            grad_shift_att,
            grad_scale_att,
            grad_gate_att,
            grad_shift_mlp,
            grad_scale_mlp,
            grad_gate_mlp,
        ],
        axis=1,
    )
    bias_sums = [
        jnp.sum(item.astype(F32), axis=0)
        for item in (grad_joined, flat(grad_attended), grad_hidden, flat(grad_branch))
    ]
    weight_sums = [sums_qkv, sums_out, sums_fc1, sums_fc2]
    return output.astype(BF16), grad_tokens.astype(BF16), grad_mod, bias_sums, weight_sums


def kernel_path(sz, latents, conditioning, w_mod, w_qkv, w_out, w_fc1, w_fc2, biases, out_grad):
    output, grad_tokens, grad_cond, sums_mod, small, sums_qkv, sums_out, sums_fc1, sums_fc2 = (
        run_kernel(
            sz,
            latents,
            out_grad,
            conditioning,
            jnp.concatenate(biases).reshape(1, -1),
            w_mod,
            w_qkv,
            w_fc1,
            w_out,
            w_fc2,
        )
    )

    return arrange(
        sz, output, grad_tokens, sums_fc2, grad_cond, sums_mod, sums_qkv, sums_out, sums_fc1, small
    )


def arrange_kernel(sz, *refs):
    output, grad_tokens, fc2, cond, mod, qkv, out, fc1, small = refs[:9]
    (to_output, to_tokens, to_cond, to_mod, to_b_mod, to_qkv, to_b_qv) = refs[9:16]
    (to_out, to_b_out, to_fc1, to_b_fc1, to_fc2, to_b_fc2, sems) = refs[16:23]
    near = refs[23:]
    pairs = list(zip((cond, mod, qkv, out, fc1, small), near))
    pairs += [(output, to_output), (grad_tokens, to_tokens), (fc2, to_fc2)]
    moves = [
        pltpu.make_async_copy(source, target, sems.at[index])
        for index, (source, target) in enumerate(pairs)
    ]
    for move in moves:
        move.start()
    for move in moves[: len(near)]:
        move.wait()
    cond, mod, qkv, out, fc1, small = near
    rows, pad, seq = sz.rows, sz.padded_rows, sz.seq

    def join(source, groups, size):
        pieces = [
            source[position * pad : (position + 1) * pad, group * size : (group + 1) * size]
            for group in range(groups)
            for position in range(seq)
        ]
        return jnp.concatenate([piece.astype(F32) for piece in pieces], axis=1)[:rows, :]

    to_cond[...] = cond[...]
    to_mod[...] = mod[:rows, :]
    to_out[...] = out[:rows, :]
    to_qkv[...] = join(qkv, 3, sz.part)
    to_fc1[...] = join(fc1, sz.dp, sz.units)
    for index, target in enumerate((to_b_out, to_b_fc2, to_b_qv, to_b_fc1, to_b_mod)):
        target[...] = small[index : index + 1, : target.shape[1]]
    for move in moves[len(near) :]:
        move.wait()


def arrange(sz, output, grad_tokens, fc2, cond, mod, qkv, out, fc1, small):
    vmem = pl.BlockSpec(memory_space=pltpu.VMEM)
    far = pl.BlockSpec(memory_space=pl.ANY)
    low = lambda *shape: jax.ShapeDtypeStruct(shape, BF16)
    full = lambda *shape: jax.ShapeDtypeStruct(shape, F32)
    rows, width, hidden = sz.rows, sz.width, sz.hidden * sz.seq
    results = pl.pallas_call(
        partial(arrange_kernel, sz),
        out_shape=[
            low(*output.shape),
            low(*output.shape),
            low(sz.count, width),
            full(rows, 6 * width),
            full(1, 6 * rows),
            full(rows, 3 * width),
            full(1, 2 * rows),
            full(rows, width),
            full(1, rows),
            full(rows, hidden),
            full(1, sz.units),
            full(sz.units, width),
            full(1, rows),
        ],
        in_specs=[far] * 9,
        out_specs=[far, far] + [vmem] * 9 + [far, vmem],
        scratch_shapes=[pltpu.SemaphoreType.DMA((9,))]
        + [pltpu.VMEM(item.shape, item.dtype) for item in (cond, mod, qkv, out, fc1, small)],
        compiler_params=pltpu.CompilerParams(vmem_limit_bytes=33554432),
    )(output, grad_tokens, fc2, cond, mod, qkv, out, fc1, small)
    return tuple(item.reshape(-1) if item.shape[0] == 1 else item for item in results)


def column_blocks(seq, dp, w_qkv, w_fc1, units):
    rows = w_qkv.shape[0]
    qkv_blocks = w_qkv.reshape(rows, 3, seq, -1).transpose(2, 0, 1, 3).reshape(seq, rows, -1)
    fc1_blocks = w_fc1.reshape(rows, dp, seq, units).transpose(2, 0, 1, 3).reshape(seq, rows, -1)
    return qkv_blocks, fc1_blocks


def body(
    latents,
    conditioning,
    w_mod,
    b_mod,
    w_qkv,
    b_qv,
    w_out,
    b_out,
    w_fc1,
    b_fc1,
    w_fc2,
    b_fc2,
    out_grad,
):
    count, tokens, width = latents.shape
    dp, seq = lax.axis_size("dp"), lax.axis_size("seq")
    sz = Sizes(dp, seq, latents, w_qkv, w_fc2)
    if sz.fits():
        biases = (b_mod, b_qv, b_out, b_fc1, b_fc2)
        return kernel_path(
            sz, latents, conditioning, w_mod, w_qkv, w_out, w_fc1, w_fc2, biases, out_grad
        )
    both = ("dp", "seq")
    my_dp, my_seq = lax.axis_index("dp"), lax.axis_index("seq")
    me = my_dp * seq + my_seq
    rows, units = w_qkv.shape[0], w_fc2.shape[0]
    part = width // seq

    cond = conditioning.astype(F32)
    cond_act, silu_back = jax.vjp(jax.nn.silu, cond)
    cond_low = lax.all_gather(cond_act.astype(BF16), "dp", axis=0, tiled=True)
    cond_mine = lax.dynamic_slice_in_dim(cond_low, me * rows, rows, axis=1)
    mod_part = dot(cond_mine, w_mod)
    mod_sum = lax.psum(lax.psum_scatter(mod_part, "dp", scatter_dimension=0, tiled=True), "seq")
    biases = lax.all_gather(jnp.concatenate([b_mod, b_qv, b_out, b_fc1, b_fc2]), both, axis=0)
    pieces, start = [], 0
    for item in (b_mod, b_qv, b_out, b_fc1, b_fc2):
        pieces.append(biases[:, start : start + item.shape[0]].reshape(-1).astype(F32))
        start += item.shape[0]
    bias_mod, bias_qv, bias_out, bias_fc1, bias_fc2 = pieces
    bias_qv = lax.dynamic_index_in_dim(bias_qv.reshape(2, seq, part), my_seq, 1, keepdims=False)
    bias_fc1 = lax.dynamic_index_in_dim(
        bias_fc1.reshape(dp, seq, units), my_seq, 1, keepdims=False
    ).reshape(-1)
    modulation = (mod_sum + bias_mod).reshape(count, 6, width)

    blocks = column_blocks(seq, dp, w_qkv, w_fc1, units)
    output, grad_tokens, grad_mod, bias_sums, weight_sums = general_path(
        latents,
        out_grad,
        modulation,
        blocks,
        w_out,
        w_fc2,
        bias_qv,
        bias_out,
        bias_fc1,
        bias_fc2,
    )
    sums_qkv, sums_out, sums_fc1, sums_fc2 = weight_sums

    grad_mod = grad_mod.reshape(count, -1)
    grad_mod = lax.psum(grad_mod, "seq").astype(BF16)
    grad_mod = lax.all_gather(grad_mod, "dp", axis=0, tiled=True)
    sums_mod = dot_left_t(cond_mine, grad_mod)
    own = b_mod.shape[0]
    sums_bias_mod = jnp.sum(
        lax.dynamic_slice_in_dim(grad_mod, me * own, own, axis=1).astype(F32), axis=0
    )
    grad_cond_act = lax.all_gather(dot_right_t(grad_mod, w_mod), both, axis=0)
    grad_cond_act = lax.dynamic_slice_in_dim(grad_cond_act, my_dp * count, count, axis=1)
    grad_cond = silu_back(grad_cond_act.transpose(1, 0, 2).reshape(count, width))[0]

    def spread(values, shape):
        blank = jnp.zeros(shape, F32)
        return lax.dynamic_update_slice_in_dim(blank, values, my_seq, 1).reshape(-1)

    joined_sums, out_sums, fc1_sums, fc2_sums = bias_sums
    qv_sums = jnp.stack([joined_sums[:part], joined_sums[2 * part : 3 * part]])
    bias_sums = [
        spread(qv_sums.reshape(2, 1, part), (2, seq, part)),
        out_sums,
        spread(fc1_sums.reshape(dp, 1, units), (dp, seq, units)),
        fc2_sums,
    ]
    joint = jnp.concatenate([item.reshape(dp * seq, -1) for item in bias_sums], axis=1)
    joint = lax.psum_scatter(joint, both, scatter_dimension=0, tiled=True).reshape(-1)
    cuts = [b_qv.shape[0], b_out.shape[0], b_fc1.shape[0]]
    sums_bias_qv, sums_bias_out, sums_bias_fc1, sums_bias_fc2 = jnp.split(
        joint, [cuts[0], cuts[0] + cuts[1], sum(cuts)]
    )
    return (
        output,
        grad_tokens,
        grad_cond.astype(BF16),
        sums_mod,
        sums_bias_mod,
        sums_qkv,
        sums_bias_qv,
        sums_out,
        sums_bias_out,
        sums_fc1,
        sums_bias_fc1,
        sums_fc2,
        sums_bias_fc2,
    )


def solution(mesh):
    both = P(("dp", "seq"))
    wide = P(("dp", "seq"), None)
    tokens = P("dp", "seq", None)
    in_specs = (
        tokens,
        P("dp", None),
        wide,
        both,
        wide,
        both,
        wide,
        both,
        wide,
        both,
        wide,
        both,
        tokens,
    )
    out_specs = (tokens, tokens, P("dp", None)) + (wide, both) * 5
    return jax.shard_map(body, mesh=mesh, in_specs=in_specs, out_specs=out_specs, check_vma=False)
```

```python
from functools import partial
from types import SimpleNamespace
from typing import NamedTuple

import jax
import jax.numpy as jnp
from jax import lax
from jax.experimental import pallas as pl
from jax.experimental.pallas import tpu as pltpu
from jax.sharding import PartitionSpec as P

HEADS = 16
HEAD_DIM = 72
EPSILON = 1e-06
BF16 = jnp.bfloat16
F32 = jnp.float32


def layer_norm(values):
    center = values - jnp.mean(values, axis=-1, keepdims=True)
    inverse = lax.rsqrt(jnp.mean(center * center, axis=-1, keepdims=True) + EPSILON)
    return (center * inverse, inverse)


def norm_back(incoming, normed, inverse):
    return inverse * (
        incoming
        - jnp.mean(incoming, axis=-1, keepdims=True)
        - normed * jnp.mean(incoming * normed, axis=-1, keepdims=True)
    )


def dot(left, right):
    return jnp.dot(left, right, preferred_element_type=F32)


def dot_right_t(left, right):
    return lax.dot_general(left, right, (((1,), (1,)), ((), ())), preferred_element_type=F32)


def dot_left_t(left, right):
    return lax.dot_general(left, right, (((0,), (0,)), ((), ())), preferred_element_type=F32)


MESH = pl.DeviceIdType.MESH
ROOT = HEAD_DIM ** (-0.5)
LANES = 128
ROWS = 32


class Sizes:
    def __init__(self, dp, seq, latents, w_qkv, w_fc2):
        self.dp, self.seq, self.line = dp, seq, dp // 2
        self.count, self.tokens, self.width = latents.shape
        self.rows, self.units = w_qkv.shape[0], w_fc2.shape[0]
        self.chunk = seq * self.rows
        self.hidden = dp * self.units
        self.heads = HEADS // seq
        self.part = self.width // seq
        self.length = seq * self.tokens
        self.total = self.count * self.length
        self.own = self.count * self.tokens
        self.padded_rows = -(-self.rows // 16) * 16
        self.joined = -(-3 * self.part // LANES) * LANES
        self.mod_part = -(-6 * self.width // (seq * LANES)) * LANES

    def fits(self):
        return (
            self.seq == 4
            and self.dp % 2 == 0
            and self.dp == 8
            and self.count == 2
            and self.width == self.dp * self.chunk
            and self.chunk % 16 == 0
            and self.units % 16 == 0
            and self.tokens % 128 == 0
            and self.width % LANES == 0
            and self.hidden == self.width
            and self.chunk == self.units
        )


def column_cuts(width, most=512):
    cuts, start = [], 0
    while start < width:
        size = min(most, width - start)
        cuts.append((start, size))
        start += size
    return cuts


def one_hot(rows, columns, group, padded, flip):
    shape = (columns, rows) if flip else (rows, columns)
    tight = lax.broadcasted_iota(jnp.int32, shape, 1 if flip else 0)
    loose = lax.broadcasted_iota(jnp.int32, shape, 0 if flip else 1)
    hit = jnp.zeros(shape, F32)
    for index in range(rows // group):
        inside = (tight >= index * group) & (tight < (index + 1) * group)
        match = loose == tight + index * (padded - group)
        hit = jnp.where(inside & match, 1.0, hit)
    return hit.astype(BF16)


def block_kernel(sz, *refs):
    names = Inputs._fields + Outputs._fields + tuple(kernel_scratch(sz))
    r = SimpleNamespace(**dict(zip(names, refs)))
    dp_me, s_me = lax.axis_index("dp"), lax.axis_index("seq")
    z_me, x_me = dp_me // 2, dp_me % 2
    y_me, c_me = s_me // 2, s_me % 2
    count, tokens, width = sz.count, sz.tokens, sz.width
    line, seq = sz.line, sz.seq

    def seq_peer(mask):
        flip_y, flip_c = mask // 2, mask % 2
        y = 1 - y_me if flip_y else y_me
        c = 1 - c_me if flip_c else c_me
        return y * 2 + c

    def z_peer(step):
        return lax.rem(z_me + step, line)

    def device_seq(mask):
        return (dp_me, seq_peer(mask))

    def device_z(step):
        return (z_peer(step) * 2 + x_me, s_me)

    inner = z_me % 3 != 0
    outer = z_me % 3 == 0

    def z_flip(mask):
        return (z_me, z_me + 1 - 2 * (z_me % 2), lax.rem(z_me + 2, line), line - 1 - z_me)[mask]

    def device_flip(mask):
        return (z_flip(mask) * 2 + x_me, s_me)

    device_x = (z_me * 2 + (1 - x_me), s_me)
    used = [0, 0]

    def copy_to(src, dst, device, arrival=None):
        index = used[0]
        used[0] += 1
        return pltpu.make_async_remote_copy(
            src_ref=src,
            dst_ref=dst,
            send_sem=r.send_sems.at[index],
            recv_sem=r.recv_sems.at[index] if arrival is None else arrival,
            device_id=device,
            device_id_type=MESH,
        )

    def send(src, dst, device, arrival=None):
        copy = copy_to(src, dst, device, arrival)
        copy.start()
        return copy

    def local(src, dst):
        index = used[1]
        used[1] += 1
        copy = pltpu.make_async_copy(src, dst, r.local_sems.at[index])
        copy.start()
        return copy

    def rows_of(ref, start, size):
        return ref.at[pl.ds(start, size)]

    raw_moves = [
        local(source, target)
        for source, target in (
            (r.qkv_src, r.qkv_raw),
            (r.fc1_src, r.fc1_raw),
            (r.out_src, r.out_raw),
        )
    ]

    peers = [device_seq(mask) for mask in (1, 2, 3)]
    peers += [device_z(step) for step in range(1, line)] + [device_x]
    barrier = pltpu.get_barrier_semaphore()
    for peer in peers:
        pl.semaphore_signal(barrier, inc=1, device_id=peer, device_id_type=MESH)
    pl.semaphore_wait(barrier, len(peers))

    pending = []
    far_moves = []

    def release(copy):
        copy.wait_send()
        pending[:] = [item for item in pending if item is not copy]

    def token_rows(ref, latent, position):
        return rows_of(ref, (latent * seq + position) * tokens, tokens)

    class GatherTokens:
        def __init__(self, ref, latent, source=None):
            self.ref, self.latent = ref, latent
            slot = token_rows(ref, latent, s_me)
            mine = slot if source is None else source
            self.core = send(mine, slot, device_seq(1))
            self.chip = send(mine, slot, device_seq(2))

        def forward(self):
            self.chip.wait_recv()
            slot = token_rows(self.ref, self.latent, seq_peer(2))
            self.last = send(slot, slot, device_seq(1))

        def finish(self):
            self.core.wait_recv()
            self.last.wait_recv()
            for copy in (self.core, self.chip, self.last):
                pending.append(copy)

    class SumTokens:
        def __init__(self, part, slot, latent):
            self.part, self.slot, self.latent = part, slot, latent
            self.first = [
                send(
                    token_rows(part, latent, y * 2 + 1 - c_me),
                    r.sum_core.at[slot, y, latent],
                    device_seq(1),
                )
                for y in range(2)
            ]

        def forward(self):
            for copy in self.first:
                copy.wait_recv()
            other = 1 - y_me
            total = token_rows(self.part, self.latent, other * 2 + c_me)[...].astype(F32)
            total = total + r.sum_core[self.slot, other, self.latent].astype(F32)
            r.sum_send[self.slot, self.latent] = total.astype(BF16)
            self.last = send(
                r.sum_send.at[self.slot, self.latent],
                r.sum_chip.at[self.slot, self.latent],
                device_seq(2),
            )

        def finish(self):
            self.last.wait_recv()
            for copy in self.first + [self.last]:
                copy.wait_send()

        def rows(self, start):
            place = pl.ds((self.latent * seq + s_me) * tokens + start, ROWS)
            here = pl.ds(start, ROWS)
            total = self.part[place, :].astype(F32)
            total = total + r.sum_core[self.slot, y_me, self.latent, here, :].astype(F32)
            return total + r.sum_chip[self.slot, self.latent, here, :].astype(F32)

    def exchange(pick, place):
        return [send(pick(seq_peer(mask)), place(s_me), device_seq(mask)) for mask in (1, 2, 3)]

    def settle(copies):
        for copy in copies:
            copy.wait_recv()
        pending.extend(copies)

    class GatherWeights:
        def __init__(self, ref, chunk, direct=False):
            self.ref, self.chunk, self.direct = ref, chunk, direct

        def slot(self, dp):
            return rows_of(self.ref, dp * self.chunk, self.chunk)

        def push_along(self, source=None):
            own = self.slot(dp_me)
            mine = own if source is None else source
            self.along = [send(mine, own, device_flip(mask)) for mask in (2, 1)]
            self.arrival = r.recv_sems.at[used[0]]
            self.last = copy_to(mine, own, device_flip(3))
            if self.direct:
                self.last.start()
            else:
                pl.when(inner)(self.last.start)
            self.across, self.passed = [], 0

        def push_across(self, source=None):
            own = self.slot(dp_me)
            mine = own if source is None else source
            self.across.append(send(mine, own, device_x))

        def push(self, source=None):
            self.push_along(source)
            self.push_across(source)

        def forward(self, limit=3):
            for mask in (2, 1, 3)[self.passed :][:limit]:
                (self.along + [self.last])[self.passed].wait_recv()
                self.passed += 1
                came = self.slot(z_flip(mask) * 2 + x_me)
                if mask == 2 and not self.direct:
                    self.relay = copy_to(came, came, device_flip(1), self.arrival)
                    pl.when(inner)(self.relay.start)
                self.across.append(send(came, came, device_x))

        def finish(self):
            for copy in self.across:
                copy.wait_recv()

        def drain(self):
            for copy in self.along + self.across:
                copy.wait_send()
            if self.direct:
                self.last.wait_send()
                return

            @pl.when(inner)
            def _():
                self.last.wait_send()
                self.relay.wait_send()

    class SumWeights:
        def __init__(self, ref, chunk, across_ref, along_ref, columns):
            self.ref, self.chunk, self.columns = ref, chunk, columns
            self.across_ref, self.along_ref = across_ref, along_ref
            self.across = {}

        def view(self, ref, index):
            return ref.at[index, :, pl.ds(0, self.columns)]

        def slot(self, dp):
            return rows_of(self.ref, dp * self.chunk, self.chunk)

        def push(self, masks=(3, 2, 1, 0)):
            if not self.across:
                self.across, self.passed = {}, []
            for mask in masks:
                self.across[mask] = send(
                    self.slot(z_flip(mask) * 2 + 1 - x_me),
                    self.view(self.across_ref, mask),
                    device_x,
                )

        def forward(self, limit=3):
            for mask in (3, 2, 1)[len(self.passed) :][:limit]:
                self.passed.append(mask)
                self.across[mask].wait_recv()
                slot = self.slot(z_flip(mask) * 2 + x_me)
                came = self.view(self.across_ref, mask)

                def total():
                    return slot[...].astype(F32) + came[...].astype(F32)

                extra = self.view(self.along_ref, 0)
                if mask == 3:
                    slot[...] = total().astype(BF16)
                    self.direct = copy_to(slot, self.view(self.along_ref, 3), device_flip(3))
                    self.relay = copy_to(slot, extra, device_flip(1))
                    pl.when(inner)(self.direct.start)
                    pl.when(outer)(self.relay.start)
                elif mask == 2:

                    @pl.when(inner)
                    def _():
                        self.relay.wait_recv()
                        slot[...] = (total() + extra[...].astype(F32)).astype(BF16)

                    @pl.when(outer)
                    def _():
                        slot[...] = total().astype(BF16)

                    self.two = send(slot, self.view(self.along_ref, 2), device_flip(2))
                else:
                    slot[...] = total().astype(BF16)
                    self.one = send(slot, self.view(self.along_ref, 1), device_flip(1))

        def finish(self, target):
            self.across[0].wait_recv()
            total = self.slot(dp_me)[...].astype(F32)
            total = total + self.view(self.across_ref, 0)[...].astype(F32)
            for copy, mask in ((self.one, 1), (self.two, 2)):
                copy.wait_recv()
                total = total + self.view(self.along_ref, mask)[...].astype(F32)
            target[...] = total

            @pl.when(inner)
            def _():
                self.direct.wait_recv()
                target[...] += self.view(self.along_ref, 3)[...].astype(F32)
                self.direct.wait_send()

            @pl.when(outer)
            def _():
                self.relay.wait_send()

            for copy in [self.one, self.two] + list(self.across.values()):
                copy.wait_send()

    pad = sz.padded_rows
    qkv_blocks, fc1_blocks = r.qkv_blocks, r.fc1_blocks
    out_wide = sz.dp * pad
    out_mine = rows_of(r.out_blocks, s_me * out_wide, out_wide)

    cond = r.conditioning[...].astype(F32)
    gate_cond = 1.0 / (1.0 + jnp.exp(-cond))
    low_rows = jnp.concatenate([cond * gate_cond, jnp.zeros((16 - count, width), F32)], axis=0)
    rows_of(r.cond_all, dp_me * 16, 16)[...] = low_rows.astype(BF16)
    gather_cond = GatherWeights(r.cond_all, 16)
    gather_cond.push()
    for move in raw_moves:
        move.wait()
    own_out = jnp.concatenate(
        [r.out_raw[...].astype(F32), jnp.zeros((pad - sz.rows, width), F32)], axis=0
    )
    rows_of(out_mine, dp_me * pad, pad)[...] = own_out.astype(BF16)
    gather_out = GatherWeights(out_mine, pad)
    gather_out.push()
    qkv_send, fc1_send = r.qkv_rows, r.fc1_rows
    qkv_send[...] = jnp.zeros_like(qkv_send)
    fc1_send[...] = jnp.zeros_like(fc1_send)
    for position in range(seq):
        here = slice(position * pad, position * pad + sz.rows)
        pieces = [
            r.qkv_raw[:, kind * width + position * sz.part :][:, : sz.part] for kind in range(3)
        ]
        qkv_send[here, : 3 * sz.part] = jnp.concatenate(pieces, axis=1)
        pieces = [
            r.fc1_raw[:, (group * seq + position) * sz.units :][:, : sz.units]
            for group in range(sz.dp)
        ]
        fc1_send[here, :] = jnp.concatenate(pieces, axis=1)
    qkv_local, fc1_local = [
        local(rows_of(source, s_me * pad, pad), rows_of(target, s_me * pad, pad))
        for source, target in ((qkv_send, qkv_blocks), (fc1_send, fc1_blocks))
    ]
    lat_local, og_local = [
        [local(source.at[latent], token_rows(target, latent, s_me)) for latent in range(count)]
        for source, target in ((r.latents, r.lat_all), (r.out_grad, r.grad_branch))
    ]
    fc2_local = local(r.fc2_src, rows_of(r.fc2, dp_me * sz.units, sz.units))

    def place(values, start, size):
        blank = jnp.zeros((1, size - values.shape[1]), F32)
        row = jnp.concatenate([values.astype(F32), blank], axis=1)
        return pltpu.roll(jnp.broadcast_to(row, (8, size)), start, 1)[0:1, :]

    def when(hit, values):
        return jnp.where(hit, values, jnp.zeros_like(values))

    me = dp_me * seq + s_me
    own_mod, own_qv, own_out, own_fc1, own_fc2 = [
        ref[...].astype(F32).reshape(1, -1) for ref in (r.b_mod, r.b_qv, r.b_out, r.b_fc1, r.b_fc2)
    ]
    devices = sz.dp * seq
    half_way = devices // 2
    qv_row = place(own_qv, lax.rem(me, half_way) * (2 * sz.rows), width)
    fc1_row = place(own_fc1, dp_me * sz.units, width)
    bias_rows = [
        place(own_out, me * sz.rows, width),
        place(own_fc2, me * sz.rows, width),
        when(me < half_way, qv_row),
        when(me >= half_way, qv_row),
    ] + [when(s_me == position, fc1_row) for position in range(seq)]
    bias_rows.append(jnp.zeros((16 - len(bias_rows), width), F32))
    bias_mine = rows_of(r.bias_blocks, s_me * 16, 16)
    bias_mine[...] = jnp.concatenate(bias_rows, axis=0).astype(BF16)
    bias_moves = exchange(lambda peer: bias_mine, lambda me: rows_of(r.bias_blocks, me * 16, 16))
    qkv_moves = exchange(
        lambda peer: rows_of(qkv_send, peer * pad, pad),
        lambda me: rows_of(qkv_blocks, me * pad, pad),
    )
    fc1_moves = exchange(
        lambda peer: rows_of(fc1_send, peer * pad, pad),
        lambda me: rows_of(fc1_blocks, me * pad, pad),
    )

    tighten = one_hot(sz.chunk, seq * pad, sz.rows, pad, False)
    loosen = one_hot(sz.chunk, seq * pad, sz.rows, pad, True)
    gather_qkv = GatherWeights(r.qkv, sz.chunk)
    gather_fc1 = GatherWeights(r.fc1, sz.chunk)
    gather_fc2 = GatherWeights(r.fc2, sz.units)
    settle(bias_moves)
    bias_sum = sum(
        r.bias_blocks[position * 16 : (position + 1) * 16, :].astype(F32) for position in range(seq)
    )
    rows_of(r.bias_all, dp_me * 16, 16)[...] = bias_sum.astype(BF16)
    gather_bias = GatherWeights(r.bias_all, 16)
    gather_bias.push()
    gather_cond.forward()
    gather_out.forward(1)
    qkv_local.wait()
    settle(qkv_moves)
    rows_of(r.qkv, dp_me * sz.chunk, sz.chunk)[...] = dot(tighten, qkv_blocks[...]).astype(BF16)
    gather_qkv.push_along()

    gather_cond.finish()
    gather_qkv.push_across()
    iota = partial(lax.broadcasted_iota, jnp.int32)
    hit = iota((width, LANES), 0) == iota((width, LANES), 1) + me * sz.rows
    hit = hit & (iota((width, LANES), 1) < sz.rows)
    cond_mine = dot(r.cond_all[...], jnp.where(hit, 1.0, 0.0).astype(BF16)).astype(BF16)
    r.cond_mine[...] = cond_mine
    order = iota((16, sz.dp * 16), 0)
    across, along, which = order >> 3, (order >> 1) & (line - 1), order & 1
    hit = iota((16, sz.dp * 16), 1) == (along * 2 + across) * 16 + which
    cond_rows = dot(jnp.where(hit, 1.0, 0.0).astype(BF16), cond_mine).astype(BF16)
    cond_rows = cond_rows[:, : sz.rows]
    mod_wide = sz.mod_part * seq
    own_row = place(own_mod, me * (6 * sz.rows), mod_wide)
    for comp in range(6):
        here = slice(comp * width, (comp + 1) * width)
        r.mod_sums[:, here] = dot(cond_rows, r.w_mod[:, here]) + own_row[:, here]
    r.mod_sums[:, 6 * width :] = jnp.zeros((16, mod_wide - 6 * width), F32)

    def mod_part(position):
        return r.mod_sums.at[:, pl.ds(pl.multiple_of(position * sz.mod_part, LANES), sz.mod_part)]

    mod_core = [
        send(mod_part(y * 2 + 1 - c_me), r.mod_core.at[y], device_seq(1)) for y in range(2)
    ]
    gather_out.forward()
    fc1_local.wait()
    settle(fc1_moves)
    rows_of(r.fc1, dp_me * sz.chunk, sz.chunk)[...] = dot(tighten, fc1_blocks[...]).astype(BF16)
    for copy in mod_core:
        copy.wait_recv()
    r.mod_send[...] = mod_part((1 - y_me) * 2 + c_me)[...] + r.mod_core[1 - y_me]
    mod_chip = send(r.mod_send, r.mod_chip, device_seq(2))
    lat_moves = [
        GatherTokens(r.lat_all, latent, r.latents.at[latent]) for latent in range(count)
    ]
    mod_chip.wait_recv()
    r.mod_sum[...] = mod_part(s_me)[...] + r.mod_core[y_me] + r.mod_chip[...]
    mod_x = send(rows_of(r.mod_sum, (1 - x_me) * 8, 8), r.mod_x, device_x)
    gather_bias.forward(1)
    gather_qkv.forward(1)
    mod_x.wait_recv()
    r.mod_half[...] = rows_of(r.mod_sum, x_me * 8, 8)[...] + r.mod_x[...]
    mod_z = [send(r.mod_half, r.mod_z.at[step], device_z(step)) for step in range(1, line)]
    gather_fc1.push_along()
    gather_bias.forward()
    og_moves = [GatherTokens(r.grad_branch, 0, r.out_grad.at[0])]
    gather_fc1.push_across()
    gather_qkv.forward()
    for move in lat_moves:
        move.forward()
    gather_out.finish()
    mod_total = r.mod_half[...]
    for copy, step in zip(mod_z, range(1, line)):
        copy.wait_recv()
        mod_total = mod_total + r.mod_z[step]
    hit = iota((8, sz.mod_part), 0)
    picked = [
        jnp.sum(jnp.where(hit == z_me * count + latent, mod_total, 0.0), axis=0, keepdims=True)
        for latent in range(count)
    ]
    picked.append(jnp.zeros((8 - count, sz.mod_part), F32))
    mod_slot = r.mod_all.at[s_me]
    mod_slot[...] = jnp.concatenate(picked, axis=0)
    mod_moves = [send(mod_slot, mod_slot, device_seq(mask)) for mask in (1, 2)]
    out_core = send(out_mine, out_mine, device_seq(1))
    out_chip = send(out_mine, out_mine, device_seq(2))
    mod_moves[1].wait_recv()
    mod_slot = r.mod_all.at[seq_peer(2)]
    mod_moves.append(send(mod_slot, mod_slot, device_seq(1)))
    gather_bias.finish()
    bias = jnp.sum(r.bias_all[...].astype(F32).reshape(sz.dp, 16, width), axis=0)
    bias_out, bias_fc2 = bias[0:1, :], bias[1:2, :]
    part = sz.part

    def own_part(row):
        return sum(
            when(s_me == position, row[:, position * part : (position + 1) * part])
            for position in range(seq)
        )

    r.bias_joined[...] = jnp.concatenate(
        [
            own_part(bias[2:3, :]),
            jnp.zeros((1, part), F32),
            own_part(bias[3:4, :]),
            jnp.zeros((1, sz.joined - 3 * part), F32),
        ],
        axis=1,
    )
    r.bias_fc1[...] = sum(
        when(s_me == position, bias[4 + position : 5 + position, :]) for position in range(seq)
    )
    r.bias_out[...] = bias_out
    r.bias_fc2[...] = bias_fc2
    mod_moves[0].wait_recv()
    mod_moves[2].wait_recv()
    wide = jnp.concatenate([r.mod_all[position] for position in range(seq)], axis=1)
    mod = r.modulation
    for latent in range(count):
        for comp in range(6):
            mod[latent, comp : comp + 1, :] = wide[
                latent : latent + 1, comp * width : (comp + 1) * width
            ]
    pending.extend(mod_core + [mod_chip, mod_x] + mod_z + mod_moves)
    gather_fc1.forward(1)
    for copy in qkv_moves + fc1_moves:
        release(copy)
    gather_bias.drain()
    gather_cond.drain()
    fc2_local.wait()
    gather_fc2.push()

    for copy in lat_local:
        copy.wait()
    for move in lat_moves:
        move.finish()

    heads, length = sz.heads, sz.length

    def modulate_tokens(step, carry):
        latent = step // (length // ROWS)
        here = pl.ds(pl.multiple_of(step * ROWS, ROWS), ROWS)
        normed, _ = layer_norm(r.lat_all[here, :].astype(F32))
        shift, scale = mod[latent, 0:1, :], mod[latent, 1:2, :]
        r.modded[here, :] = (normed * (1.0 + scale) + shift).astype(BF16)
        return carry

    lax.fori_loop(0, count * length // ROWS, modulate_tokens, 0)

    gather_qkv.finish()
    tile = 2 * tokens
    per_latent = length // tile

    def pad_head(values):
        return jnp.concatenate(
            [values, jnp.zeros((values.shape[0], LANES - HEAD_DIM), values.dtype)], axis=1
        )

    def project(step, carry):
        start = pl.multiple_of(step * tile, tile)
        latent = step // per_latent
        row = pl.multiple_of((step % per_latent) * tile, tile)
        joined = dot(r.modded[pl.ds(start, tile), :], r.qkv[...]) + r.bias_joined[...]
        for kind, target in enumerate((r.q_heads, r.k_heads, r.v_heads)):
            for head in range(heads):
                column = kind * part + head * HEAD_DIM
                piece = pad_head(joined[:, column : column + HEAD_DIM]).astype(BF16)
                target[latent * heads + head, pl.ds(row, tile), :] = piece
        return carry

    lax.fori_loop(0, count * per_latent, project, 0)
    gather_fc1.forward(1)

    half = length // 2

    def attend(index, carry):
        keys, values = r.k_heads[index], r.v_heads[index]

        def rows(step, carry):
            here = pl.ds(pl.multiple_of(step * half, half), half)
            scores = dot_right_t(r.q_heads[index, here, :], keys) * ROOT
            expon = jnp.exp(scores - jnp.max(scores, axis=-1, keepdims=True))
            soft = (expon * (1.0 / jnp.sum(expon, axis=-1, keepdims=True))).astype(BF16)
            r.soft[index, here, :] = soft
            r.o_heads[index, here, :] = dot(soft, values).astype(BF16)
            return carry

        return lax.fori_loop(0, 2, rows, carry)

    mixed_moves = []
    for latent in range(count):
        lax.fori_loop(latent * heads, (latent + 1) * heads, attend, 0)

        def assemble(block, carry, latent=latent):
            row = pl.multiple_of(block * tokens, tokens)
            pieces = [
                r.o_heads[latent * heads + head, pl.ds(row, tokens), :][:, :HEAD_DIM]
                for head in range(heads)
            ]
            r.mixed_send[block, latent] = jnp.concatenate(pieces, axis=1)
            return carry

        lax.fori_loop(0, seq, assemble, 0)
        own = local(r.mixed_send.at[s_me, latent], r.mixed_recv.at[s_me, latent])
        mixed_moves.append(
            (
                own,
                exchange(
                    lambda peer, latent=latent: r.mixed_send.at[peer, latent],
                    lambda me, latent=latent: r.mixed_recv.at[me, latent],
                ),
            )
        )
        if latent == 0:
            gather_fc1.forward()
            out_chip.wait_recv()
            other = rows_of(r.out_blocks, seq_peer(2) * out_wide, out_wide)
            out_last = send(other, other, device_seq(1))
    og_moves[0].forward()
    gather_fc2.forward(1)

    out_core.wait_recv()
    out_last.wait_recv()
    pending.extend([out_core, out_chip, out_last])

    def tighten_out(step, carry):
        blocks = [
            r.out_blocks[pl.ds(pl.multiple_of(block * out_wide + step * pad, 16), pad), :]
            for block in range(seq)
        ]
        start = pl.multiple_of(step * sz.chunk, 16)
        packed = dot(tighten, jnp.concatenate(blocks, axis=0))
        r.out[pl.ds(start, sz.chunk), :] = packed.astype(BF16)
        return carry

    lax.fori_loop(0, sz.dp, tighten_out, 0)

    m2_moves = []
    for latent in range(count):
        own, moves = mixed_moves[latent]
        own.wait()
        settle(moves)
        pieces = [r.mixed_recv[block, latent] for block in range(seq)]
        mixed = jnp.concatenate(pieces, axis=1)
        here = pl.ds(latent * tokens, tokens)
        r.mixed[here, :] = mixed
        r.attended[here, :] = dot(mixed, r.out[...]) + r.bias_out[...]

        def second_norm(step, carry, latent=latent):
            start = pl.multiple_of(step * ROWS, ROWS)
            here = pl.ds(latent * tokens + start, ROWS)
            tokens_in = r.latents[latent, pl.ds(start, ROWS), :].astype(F32)
            middle = tokens_in + mod[latent, 2:3, :] * r.attended[here, :]
            r.middle[here, :] = middle
            normed, _ = layer_norm(middle)
            modded = normed * (1.0 + mod[latent, 4:5, :]) + mod[latent, 3:4, :]
            place = pl.multiple_of((latent * seq + s_me) * tokens + start, ROWS)
            r.modded_two[pl.ds(place, ROWS), :] = modded.astype(BF16)
            return carry

        lax.fori_loop(0, tokens // ROWS, second_norm, 0)
        m2_moves.append(GatherTokens(r.modded_two, latent))

    for latent in range(1, count):
        og_moves.append(GatherTokens(r.grad_branch, latent, r.out_grad.at[latent]))
    gather_fc2.forward(1)
    for copy in og_local:
        copy.wait()
    for move in lat_moves:
        release(move.last)

    def gate_grads(step, carry):
        here = pl.ds(pl.multiple_of(step * ROWS, ROWS), ROWS)
        gate = mod[step // (length // ROWS), 5:6, :]
        r.grad_branch[here, :] = (r.grad_branch[here, :].astype(F32) * gate).astype(BF16)
        return carry

    def gate_latent(latent):
        og_moves[latent].finish()
        release(og_moves[latent].last)
        steps = length // ROWS
        lax.fori_loop(latent * steps, (latent + 1) * steps, gate_grads, 0)

    gate_latent(0)
    m2_moves[0].forward()
    gather_fc2.forward()

    cuts = column_cuts(sz.hidden, 256)
    gather_fc1.finish()
    for latent in range(count):
        m2_moves[latent].finish()

        def mlp(step, carry, latent=latent):
            start = pl.multiple_of(latent * length + step * tile, tile)
            rows = r.modded_two[pl.ds(start, tile), :]
            for column, size in cuts:
                here = slice(column, column + size)
                hidden = dot(rows, r.fc1[:, here]) + r.bias_fc1[:, here]
                square = hidden * hidden
                inner = 0.7978845608028654 * (hidden + 0.044715 * square * hidden)
                bent = jnp.tanh(inner)
                r.lat_all[pl.ds(start, tile), here] = (0.5 * hidden * (1.0 + bent)).astype(BF16)
                slope = 0.5 * (1.0 + bent) + 0.5 * hidden * (1.0 - bent * bent) * (
                    0.7978845608028654 * (1.0 + 3 * 0.044715 * square)
                )
                r.part_a[pl.ds(start, tile), here] = slope.astype(BF16)
            return carry

        lax.fori_loop(0, per_latent, mlp, 0)
        if latent + 1 < count:
            m2_moves[latent + 1].forward()

    for copy in (out_core, out_chip, out_last):
        release(copy)
    gather_out.drain()

    def weight_grad(left, right, target):
        size = 384 if width % 384 == 0 else LANES

        def tiles(step, carry):
            start = pl.multiple_of(step * size, LANES)
            sums = dot_left_t(left[:, pl.ds(start, size)], right[...])
            target[pl.ds(start, size), :] = sums.astype(BF16)
            return carry

        lax.fori_loop(0, left.shape[1] // size, tiles, 0)

    for latent in range(1, count):
        og_moves[latent].forward()
        gate_latent(latent)
    weight_grad(r.lat_all, r.grad_branch, r.out_blocks)
    sum_fc2 = SumWeights(r.out_blocks, sz.units, r.across_b, r.along_b, width)
    sum_fc2.push()

    gather_fc2.finish()
    r.fc1_sums[...] = jnp.zeros_like(r.fc1_sums)
    grad_moves = []
    for latent in range(count):

        def mlp_back(step, carry, latent=latent):
            start = pl.multiple_of(latent * length + step * tile, tile)
            incoming = r.grad_branch[pl.ds(start, tile), :]
            for column, size in cuts:
                here = slice(column, column + size)
                slope = r.part_a[pl.ds(start, tile), here].astype(F32)
                grads = (dot_right_t(incoming, r.fc2[here, :]) * slope).astype(BF16)
                r.grad_hidden[pl.ds(start, tile), here] = grads
                r.fc1_sums[:, here] += jnp.sum(grads.astype(F32), axis=0, keepdims=True)
            return carry

        lax.fori_loop(0, per_latent, mlp_back, 0)
        if latent:
            grad_moves[latent - 1].forward()

        def back_fc1(step, carry, latent=latent):
            start = pl.multiple_of(latent * length + step * tile, tile)
            rows = r.grad_hidden[pl.ds(start, tile), :]
            for column, size in column_cuts(width):
                here = slice(column, column + size)
                sums = dot_right_t(rows, r.fc1[here, :])
                r.part_a[pl.ds(start, tile), here] = sums.astype(BF16)
            return carry

        lax.fori_loop(0, per_latent, back_fc1, 0)
        grad_moves.append(SumTokens(r.part_a, 0, latent))

    for move in m2_moves:
        for copy in (move.core, move.chip, move.last):
            release(copy)
    gather_fc1.drain()
    grad_moves[-1].forward()
    weight_grad(r.modded_two, r.grad_hidden, r.fc1)
    sum_fc1 = SumWeights(r.fc1, sz.chunk, r.across_a, r.along_a, sz.hidden)
    sum_fc1.push()

    grad_mod = r.grad_mod
    grad_mod[...] = jnp.zeros_like(grad_mod)

    def total_rows(values):
        return jnp.sum(values, axis=0, keepdims=True)

    r.bias_sums[...] = jnp.zeros_like(r.bias_sums)
    mix_moves = []
    for latent in range(count):
        grad_moves[latent].finish()

        def second_back(step, carry, latent=latent):
            start = pl.multiple_of(step * ROWS, ROWS)
            here = pl.ds(latent * tokens + start, ROWS)
            incoming = grad_moves[latent].rows(start)
            normed, inverse = layer_norm(r.middle[here, :])
            grad_mod[latent, 3:4, :] += total_rows(incoming)
            grad_mod[latent, 4:5, :] += total_rows(incoming * normed)
            grad_middle = r.out_grad[latent, pl.ds(start, ROWS), :].astype(F32) + norm_back(
                incoming * (1.0 + mod[latent, 4:5, :]), normed, inverse
            )
            r.grad_middle[here, :] = grad_middle
            grad_mod[latent, 2:3, :] += total_rows(grad_middle * r.attended[here, :])
            grad_attended = (mod[latent, 2:3, :] * grad_middle).astype(BF16)
            r.grad_attended[here, :] = grad_attended
            r.bias_sums[0:1, :] += total_rows(grad_attended.astype(F32))
            return carry

        lax.fori_loop(0, tokens // ROWS, second_back, 0)
        sum_fc2.forward(1)
        here = pl.ds(latent * tokens, tokens)
        grad_mixed = dot_right_t(r.grad_attended[here, :], r.out[...])
        for copy in mixed_moves[latent][1]:
            release(copy)
        for block in range(seq):
            piece = grad_mixed[:, block * part : (block + 1) * part].astype(BF16)
            r.mixed_send[block, latent] = piece
        own = local(r.mixed_send.at[s_me, latent], r.mixed_recv.at[s_me, latent])
        mix_moves.append(
            (
                own,
                exchange(
                    lambda peer, latent=latent: r.mixed_send.at[peer, latent],
                    lambda me, latent=latent: r.mixed_recv.at[me, latent],
                ),
            )
        )

    gather_fc2.drain()
    branch_moves = []
    for latent in range(count):

        def branch_out(step, carry, latent=latent):
            start = pl.multiple_of(latent * length + step * tile, tile)
            sums = dot(r.lat_all[pl.ds(start, tile), :], r.fc2[...])
            r.lat_all[pl.ds(start, tile), :] = sums.astype(BF16)
            return carry

        lax.fori_loop(0, per_latent, branch_out, 0)
        branch_moves.append(SumTokens(r.lat_all, 1, latent))
    sum_fc2.forward()

    for move in branch_moves:
        move.forward()

    def attend_back(index, carry):
        queries, keys, values = r.q_heads[index], r.k_heads[index], r.v_heads[index]
        incoming = r.o_heads[index]
        r.v_heads[index] = dot_left_t(r.soft[index], incoming).astype(BF16)

        def rows(step, carry):
            here = pl.ds(pl.multiple_of(step * half, half), half)
            soft = r.soft[index, here, :].astype(F32)
            grad_soft = dot_right_t(r.o_heads[index, here, :], values)
            delta = jnp.sum(soft * grad_soft, axis=-1, keepdims=True)
            r.soft[index, here, :] = (soft * (grad_soft - delta)).astype(BF16)
            return carry

        lax.fori_loop(0, 2, rows, 0)
        r.q_heads[index] = (dot(r.soft[index], keys) * ROOT).astype(BF16)
        r.k_heads[index] = (dot_left_t(r.soft[index], queries) * ROOT).astype(BF16)
        return carry

    fc_rows = rows_of(r.attended, 0, sz.units)
    joined_sums = r.joined_sums
    grad_joined = r.grad_hidden.at[:, pl.ds(0, sz.joined)]
    joined_sums[...] = jnp.zeros_like(joined_sums)
    token_moves = []
    for latent in range(count):
        own, moves = mix_moves[latent]
        own.wait()
        settle(moves)

        def unpack(block, carry, latent=latent):
            row = pl.multiple_of(block * tokens, tokens)
            values = r.mixed_recv[block, latent]
            for head in range(heads):
                piece = pad_head(values[:, head * HEAD_DIM : (head + 1) * HEAD_DIM])
                r.o_heads[latent * heads + head, pl.ds(row, tokens), :] = piece
            return carry

        lax.fori_loop(0, seq, unpack, 0)
        middle_head = latent * heads + heads // 2
        lax.fori_loop(latent * heads, middle_head, attend_back, 0)
        if latent:
            token_moves[latent - 1].forward()
            sum_fc1.forward(1)
        lax.fori_loop(middle_head, (latent + 1) * heads, attend_back, 0)
        sum_fc1.forward(1)

        def join(block, carry, latent=latent):
            row = pl.multiple_of(block * tokens, tokens)
            start = pl.multiple_of(latent * length + block * tokens, tokens)
            pieces = [
                source[latent * heads + head, pl.ds(row, tokens), :][:, :HEAD_DIM]
                for source in (r.q_heads, r.k_heads, r.v_heads)
                for head in range(heads)
            ]
            if sz.joined > 3 * part:
                pieces.append(jnp.zeros((tokens, sz.joined - 3 * part), BF16))
            values = jnp.concatenate(pieces, axis=1)
            joined_sums[...] += total_rows(values.astype(F32))
            grad_joined[pl.ds(start, tokens), :] = values
            return carry

        lax.fori_loop(0, seq, join, 0)

        def back_qkv(step, carry, latent=latent):
            start = pl.multiple_of(latent * length + step * tile, tile)
            rows = grad_joined[pl.ds(start, tile), :]
            for column, size in column_cuts(width):
                here = slice(column, column + size)
                sums = dot_right_t(rows, r.qkv[here, :])
                r.part_a[pl.ds(start, tile), here] = sums.astype(BF16)
            return carry

        lax.fori_loop(0, per_latent, back_qkv, 0)
        token_moves.append(SumTokens(r.part_a, 0, latent))

    token_moves[-1].forward()
    sum_fc2.finish(fc_rows)
    fc2_move = local(fc_rows, r.fc2_out)
    pl.semaphore_signal(r.free_x, inc=1, device_id=device_x, device_id_type=MESH)
    for step in range(1, line):
        pl.semaphore_signal(
            r.free_z, inc=1, device_id=device_z(step), device_id_type=MESH
        )
    gather_qkv.drain()
    weight_grad(r.modded, grad_joined, r.qkv)
    sum_qkv = SumWeights(r.qkv, sz.chunk, r.across_b, r.along_b, sz.joined)
    pl.semaphore_wait(r.free_x, 1)
    sum_qkv.push()
    sum_fc1.forward()
    pl.semaphore_wait(r.free_z, line - 1)


    for latent in range(count):
        branch_moves[latent].finish()

        def final_output(step, carry, latent=latent):
            start = pl.multiple_of(step * ROWS, ROWS)
            here = pl.ds(latent * tokens + start, ROWS)
            branch = branch_moves[latent].rows(start) + r.bias_fc2[...]
            grad_output = r.out_grad[latent, pl.ds(start, ROWS), :].astype(F32)
            gate = mod[latent, 5:6, :]
            r.modded_two[here, :] = (r.middle[here, :] + gate * branch).astype(BF16)
            grad_mod[latent, 5:6, :] += total_rows(grad_output * branch)
            r.bias_sums[1:2, :] += total_rows((gate * grad_output).astype(BF16).astype(F32))
            return carry

        lax.fori_loop(0, tokens // ROWS, final_output, 0)
        slot = rows_of(r.modded_two, latent * tokens, tokens)
        far_moves.append(local(slot, r.output.at[latent]))
    for latent in range(count):
        token_moves[latent].finish()

        def final_grads(step, carry, latent=latent):
            start = pl.multiple_of(step * ROWS, ROWS)
            here = pl.ds(latent * tokens + start, ROWS)
            incoming = token_moves[latent].rows(start)
            normed, inverse = layer_norm(r.latents[latent, pl.ds(start, ROWS), :].astype(F32))
            grad_mod[latent, 0:1, :] += total_rows(incoming)
            grad_mod[latent, 1:2, :] += total_rows(incoming * normed)
            grads = r.grad_middle[here, :] + norm_back(
                incoming * (1.0 + mod[latent, 1:2, :]), normed, inverse
            )
            place = pl.ds((count + latent) * tokens + start, ROWS)
            r.modded_two[place, :] = grads.astype(BF16)
            return carry

        lax.fori_loop(0, tokens // ROWS, final_grads, 0)
        slot = rows_of(r.modded_two, (count + latent) * tokens, tokens)
        far_moves.append(local(slot, r.latents_grad.at[latent]))

    def return_rows(total, send_ref, recv_ref):
        send_ref[...] = dot(loosen, total.astype(BF16)).astype(BF16)
        mine = rows_of(send_ref, s_me * pad, pad)
        own = local(mine, rows_of(recv_ref, s_me * pad, pad))
        moves = exchange(
            lambda peer: rows_of(send_ref, peer * pad, pad),
            lambda me: rows_of(recv_ref, me * pad, pad),
        )
        return own, moves

    def small(values):
        return values.reshape(count * 8, width)

    r.grad_core_send[...] = small(grad_mod[...])
    mod_core = send(r.grad_core_send, r.grad_core, device_seq(1))

    def own_place(sums, column):
        return place(sums[:, column : column + part], s_me * part, width)

    sums = joined_sums[...]
    r.bias_sums[2:3, :] = own_place(sums, 0)
    r.bias_sums[3:4, :] = own_place(sums, 2 * part)
    for position in range(seq):
        r.bias_sums[4 + position : 5 + position, :] = when(s_me == position, r.fc1_sums[...])
    bias_x = send(r.bias_sums, r.bias_x, device_x)
    mod_core.wait_recv()
    r.grad_chip_send[...] = r.grad_core_send[...] + r.grad_core[...]
    mod_chip = send(r.grad_chip_send, r.grad_chip, device_seq(2))
    weight_grad(r.mixed, r.grad_attended, r.out)

    def loosen_out(step, carry):
        start = pl.multiple_of(step * sz.chunk, 16)
        spread = dot(loosen, r.out[pl.ds(start, sz.chunk), :]).astype(BF16)
        for block in range(seq):
            place = pl.multiple_of(block * out_wide + step * pad, 16)
            r.out_blocks[pl.ds(place, pad), :] = spread[block * pad : (block + 1) * pad, :]
        return carry

    lax.fori_loop(0, sz.dp, loosen_out, 0)
    out_first = [
        send(
            rows_of(r.out_blocks, (y * 2 + 1 - c_me) * out_wide, out_wide),
            rows_of(r.grad_branch, y * out_wide, out_wide),
            device_seq(1),
        )
        for y in range(2)
    ]

    def out_from_core(y):
        return rows_of(r.grad_branch, y * out_wide, out_wide)[...].astype(F32)

    other = rows_of(r.out_blocks, ((1 - y_me) * 2 + c_me) * out_wide, out_wide)
    out_chip_sum = rows_of(r.modded_two, 2 * count * tokens, out_wide)

    def out_half(index):
        start, size = index * (out_wide // 2), out_wide // 2
        return send(rows_of(other, start, size), rows_of(out_chip_sum, start, size), device_seq(2))

    for copy in out_first:
        copy.wait_recv()
    other[...] = (other[...].astype(F32) + out_from_core(1 - y_me)).astype(BF16)
    out_second = [out_half(0), out_half(1)]
    mod_chip.wait_recv()
    rows_of(r.bias_all, dp_me * 16, 16)[...] = (r.grad_chip_send[...] + r.grad_chip[...]).astype(
        BF16
    )
    gather_grad = GatherWeights(r.bias_all, 16, direct=True)
    gather_grad.push()
    sum_qkv.forward(1)
    fc2_move.wait()
    sum_fc1.finish(fc_rows)
    fc1_own, fc1_back = return_rows(fc_rows[...], r.fc1_blocks, r.fc1_rows)
    gather_grad.forward()
    sum_qkv.forward(1)
    bias_x.wait_recv()
    r.bias_half[...] = r.bias_sums[...] + r.bias_x[...]
    room_z = r.mod_z.at[:, :, pl.ds(0, width)]
    bias_z = [send(r.bias_half, room_z.at[step], device_z(step)) for step in range(1, line)]
    pending.extend([mod_core, bias_x, mod_chip] + bias_z)
    sum_qkv.forward(1)

    gather_grad.finish()
    all_grads = r.bias_all[...]
    rows = sz.dp * 16
    comp_of = iota((rows, rows), 0) & 7
    source = (iota((rows, rows), 0) & ~15) + ((iota((rows, rows), 0) >> 3) & 1)
    spread = jnp.where(iota((rows, rows), 1) == source, 1.0, 0.0).astype(BF16)
    cond_spread = dot(spread, r.cond_mine[...])
    comp_of = iota((rows, LANES), 0) & 7
    cond_grads = jnp.zeros((rows, sz.rows), F32)
    mod_rows = r.mod_out.shape[0]
    for comp in range(6):
        back = dot_right_t(all_grads, r.w_mod[:, comp * width : (comp + 1) * width])
        cond_grads = cond_grads + jnp.where(comp_of[:, : sz.rows] == comp, back, 0.0)
    cond_grads = jnp.sum(cond_grads.reshape(rows // 8, 8, sz.rows), axis=1)
    blank = jnp.zeros((16, width - sz.rows), F32)
    cond_grads = pltpu.roll(jnp.concatenate([cond_grads, blank], axis=1), me * sz.rows, 1)
    keep = iota((8, 16), 0)
    hits = []
    for side in range(2):
        hits.append(
            sum(
                when(
                    iota((8, width), 0) == along * count + latent,
                    jnp.broadcast_to(
                        cond_grads[
                            (along * 2 + side) * count + latent : (along * 2 + side) * count
                            + latent
                            + 1,
                            :,
                        ],
                        (8, width),
                    ),
                )
                for along in range(line)
                for latent in range(count)
            )
        )
    r.cond_sides[0] = hits[0]
    r.cond_sides[1] = hits[1]
    cond_x = send(r.cond_sides.at[1 - x_me], r.cond_x, device_x)
    for copy in out_second:
        copy.wait_recv()
    mine = out_mine[...].astype(F32) + out_from_core(y_me)
    out_mine[...] = (mine + out_chip_sum[...].astype(F32)).astype(BF16)
    pending.extend(out_first + out_second)
    sum_out = SumWeights(out_mine, pad, r.across_out, r.along_out, width)
    sum_out.push()
    bias_total = r.bias_half[...]
    for copy, step in zip(bias_z, range(1, line)):
        copy.wait_recv()
        bias_total = bias_total + room_z[step]
    r.bias_line[...] = bias_total
    bias_core = send(r.bias_line, r.bias_core, device_seq(1))
    cond_x.wait_recv()
    r.cond_half[...] = r.cond_sides[x_me] + r.cond_x[...]
    cond_z = [send(r.cond_half, r.cond_z.at[step], device_z(step)) for step in range(1, line)]
    bias_core.wait_recv()
    r.bias_pair[...] = r.bias_line[...] + r.bias_core[...]
    bias_chip = send(r.bias_pair, r.bias_chip, device_seq(2))
    comp_rows = iota((8, rows), 0) == (iota((8, rows), 1) & 7)
    mod_bias = dot(jnp.where(comp_rows, 1.0, 0.0).astype(BF16), all_grads)
    cond_total = r.cond_half[...]
    for copy, step in zip(cond_z, range(1, line)):
        copy.wait_recv()
        cond_total = cond_total + r.cond_z[step]
    r.cond_line[...] = cond_total
    cond_seq = exchange(lambda peer: r.cond_line, lambda me: r.cond_seq.at[me])
    for comp in range(6):
        chosen = jnp.where(comp_of == comp, cond_spread, 0.0).astype(BF16)
        place_rows = rows_of(r.grad_middle, comp * mod_rows, mod_rows)
        place_rows[...] = dot_left_t(chosen, all_grads)[:mod_rows, :]
        far_moves.append(local(place_rows, r.mod_out.at[:, pl.ds(comp * width, width)]))
    sum_out.forward(1)
    bias_chip.wait_recv()
    bias_full = r.bias_pair[...] + r.bias_chip[...]

    def own_lanes(row, start):
        size = row.shape[1]
        turned = pltpu.roll(jnp.broadcast_to(row, (8, size)), lax.rem(size - start, size), 1)
        return turned[0:1, : 2 * LANES]

    qv_total = when(me < half_way, bias_full[2:3, :]) + when(me >= half_way, bias_full[3:4, :])
    fc1_total = sum(
        when(s_me == position, bias_full[4 + position : 5 + position, :])
        for position in range(seq)
    )
    first = me * (6 * sz.rows) // width
    comp_row = iota((8, width), 0)
    pair = [
        jnp.sum(jnp.where(comp_row == first + more, mod_bias, 0.0), axis=0, keepdims=True)
        for more in range(2)
    ]
    r.small_out[...] = jnp.concatenate(
        [
            own_lanes(bias_full[0:1, :], me * sz.rows),
            own_lanes(bias_full[1:2, :], me * sz.rows),
            own_lanes(qv_total, lax.rem(me, half_way) * (2 * sz.rows)),
            own_lanes(fc1_total, dp_me * sz.units),
            own_lanes(jnp.concatenate(pair, axis=1), me * (6 * sz.rows) - first * width),
            jnp.zeros((3, 2 * LANES), F32),
        ],
        axis=0,
    )
    qkv_total = fc_rows.at[:, pl.ds(0, sz.joined)]
    sum_qkv.finish(qkv_total)
    qkv_own, qkv_back = return_rows(qkv_total[...], r.qkv_blocks, r.qkv_rows)
    sum_out.forward()
    out_rows = rows_of(r.middle, 0, pad)
    sum_out.finish(out_rows)
    far_moves.append(local(out_rows, r.out_out))
    gather_grad.drain()
    cond_full = r.cond_line[...]
    for copy, mask in zip(cond_seq, (1, 2, 3)):
        copy.wait_recv()
        cond_full = cond_full + r.cond_seq[seq_peer(mask)]
    picked = [
        jnp.sum(
            jnp.where(comp_row == z_me * count + latent, cond_full, 0.0), axis=0, keepdims=True
        )
        for latent in range(count)
    ]
    slope = gate_cond * (1.0 + cond * (1.0 - gate_cond))
    r.cond_grad[...] = (jnp.concatenate(picked, axis=0) * slope).astype(BF16)
    pending.extend([bias_core, bias_chip, cond_x] + cond_seq + cond_z)
    for own, moves in ((fc1_own, fc1_back), (qkv_own, qkv_back)):
        own.wait()
        settle(moves)
    far_moves.append(local(r.fc1_rows, r.fc1_out))
    far_moves.append(local(r.qkv_rows, r.qkv_out))
    for copy in far_moves:
        copy.wait()
    for copy in pending:
        copy.wait_send()


class Inputs(NamedTuple):
    latents: object
    out_grad: object
    conditioning: object
    b_mod: object
    b_qv: object
    b_out: object
    b_fc1: object
    b_fc2: object
    w_mod: object
    qkv_src: object
    fc1_src: object
    out_src: object
    fc2_src: object


class Outputs(NamedTuple):
    output: object
    latents_grad: object
    cond_grad: object
    mod_out: object
    small_out: object
    qkv_out: object
    out_out: object
    fc1_out: object
    fc2_out: object


def kernel_scratch(sz):
    low = lambda *shape: pltpu.VMEM(shape, BF16)
    full = lambda *shape: pltpu.VMEM(shape, F32)
    count, tokens, width, seq = sz.count, sz.tokens, sz.width, sz.seq
    pad, groups = sz.padded_rows, sz.count * sz.heads
    tall = sz.chunk if sz.chunk > sz.units else sz.units
    wide = max(sz.joined, sz.hidden, width)
    return dict(
        lat_all=low(sz.total, max(width, sz.hidden)),
        grad_branch=low(sz.total, width),
        modded=low(sz.total, width),
        q_heads=low(groups, sz.length, LANES),
        k_heads=low(groups, sz.length, LANES),
        v_heads=low(groups, sz.length, LANES),
        o_heads=low(groups, sz.length, LANES),
        soft=low(groups, sz.length, sz.length),
        mixed_send=low(seq, count, tokens, sz.part),
        mixed_recv=low(seq, count, tokens, sz.part),
        mixed=low(sz.own, width),
        attended=full(sz.own, width),
        middle=full(sz.own, width),
        grad_middle=full(sz.own, width),
        grad_attended=low(sz.own, width),
        modded_two=low(sz.total, width),
        grad_hidden=low(sz.total, sz.hidden),
        part_a=low(sz.total, width),
        sum_core=low(2, 2, count, tokens, width),
        sum_send=low(2, count, tokens, width),
        sum_chip=low(2, count, tokens, width),
        qkv_raw=low(sz.rows, 3 * width),
        fc1_raw=low(sz.rows, seq * sz.hidden),
        out_raw=low(sz.rows, width),
        qkv_blocks=low(seq * pad, sz.joined),
        fc1_blocks=low(seq * pad, sz.hidden),
        qkv_rows=low(seq * pad, sz.joined),
        fc1_rows=low(seq * pad, sz.hidden),
        out_blocks=low(seq * sz.dp * pad, width),
        qkv=low(width, sz.joined),
        fc1=low(width, sz.hidden),
        fc2=low(sz.hidden, width),
        out=low(width, width),
        across_a=low(sz.line, sz.chunk, wide),
        along_a=low(sz.line, sz.chunk, wide),
        across_b=low(sz.line, tall, wide),
        along_b=low(sz.line, tall, wide),
        across_out=low(sz.line, pad, width),
        along_out=low(sz.line, pad, width),
        cond_all=low(sz.dp * 16, width),
        cond_mine=low(sz.dp * 16, LANES),
        bias_blocks=low(seq * 16, width),
        bias_all=low(sz.dp * 16, width),
        mod_sums=full(16, sz.mod_part * seq),
        mod_core=full(2, 16, sz.mod_part),
        mod_send=full(16, sz.mod_part),
        mod_chip=full(16, sz.mod_part),
        mod_sum=full(16, sz.mod_part),
        mod_x=full(8, sz.mod_part),
        mod_half=full(8, sz.mod_part),
        mod_z=full(sz.line, 8, sz.mod_part),
        mod_all=full(seq, 8, sz.mod_part),
        modulation=full(count, 8, width),
        bias_joined=full(1, sz.joined),
        bias_out=full(1, width),
        bias_fc1=full(1, width),
        bias_fc2=full(1, width),
        joined_sums=full(1, sz.joined),
        fc1_sums=full(1, sz.hidden),
        grad_mod=full(count, 8, width),
        grad_core_send=full(16, width),
        grad_core=full(16, width),
        grad_chip_send=full(16, width),
        grad_chip=full(16, width),
        bias_sums=full(8, width),
        bias_x=full(8, width),
        bias_half=full(8, width),
        bias_line=full(8, width),
        bias_core=full(8, width),
        bias_pair=full(8, width),
        bias_chip=full(8, width),
        cond_sides=full(2, 8, width),
        cond_x=full(8, width),
        cond_half=full(8, width),
        cond_z=full(sz.line, 8, width),
        cond_line=full(8, width),
        cond_seq=full(seq, 8, width),
        send_sems=pltpu.SemaphoreType.DMA((200,)),
        recv_sems=pltpu.SemaphoreType.DMA((200,)),
        free_x=pltpu.SemaphoreType.REGULAR,
        free_z=pltpu.SemaphoreType.REGULAR,
        local_sems=pltpu.SemaphoreType.DMA((40,)),
    )


def kernel_outputs(sz):
    low = lambda *shape: jax.ShapeDtypeStruct(shape, BF16)
    full = lambda *shape: jax.ShapeDtypeStruct(shape, F32)
    count, tokens, width, pad = sz.count, sz.tokens, sz.width, sz.padded_rows
    return [
        low(count, tokens, width),
        low(count, tokens, width),
        low(count, width),
        full(-(-sz.rows // 8) * 8, 6 * width),
        full(8, 2 * LANES),
        low(sz.seq * pad, sz.joined),
        full(pad, width),
        low(sz.seq * pad, sz.hidden),
        full(sz.units, width),
    ]


def run_kernel(sz, *operands):
    vmem = pl.BlockSpec(memory_space=pltpu.VMEM)
    far = pl.BlockSpec(memory_space=pl.ANY)
    outputs = kernel_outputs(sz)
    return pl.pallas_call(
        partial(block_kernel, sz),
        out_shape=outputs,
        in_specs=[vmem] * 9 + [far] * 4,
        out_specs=[far, far, vmem, far, vmem, far, far, far, far],
        scratch_shapes=list(kernel_scratch(sz).values()),
        compiler_params=pltpu.CompilerParams(
            collective_id=0, has_side_effects=True, vmem_limit_bytes=66584576
        ),
    )(*operands)


def general_path(
    latents, out_grad, modulation, blocks, w_out, w_fc2, bias_qv, bias_out, bias_fc1, bias_fc2
):
    count, tokens, width = latents.shape
    dp, seq = lax.axis_size("dp"), lax.axis_size("seq")
    both = ("dp", "seq")
    qkv_blocks, fc1_blocks = blocks
    rows = qkv_blocks.shape[1]
    part, heads, length = width // seq, HEADS // seq, seq * tokens
    shift_att, scale_att, gate_att, shift_mlp, scale_mlp, gate_mlp = [
        modulation[:, index : index + 1] for index in range(6)
    ]

    def to_columns(blocks):
        mine = lax.all_to_all(blocks, "seq", 0, 0, tiled=True).reshape(seq * rows, -1)
        return lax.all_gather(mine, "dp", axis=0, tiled=True)

    full_qkv = to_columns(qkv_blocks)
    full_out = lax.all_gather(w_out, both, axis=0, tiled=True)
    full_fc1 = to_columns(fc1_blocks)
    full_fc2 = lax.all_gather(w_fc2, "dp", axis=0, tiled=True)

    def gather_tokens(values):
        return lax.all_gather(values, "seq", axis=1, tiled=True)

    def flat(values):
        return values.reshape(-1, values.shape[-1])

    tokens_f = latents.astype(F32)
    normed, inverse = layer_norm(tokens_f)
    modded = (normed * (1.0 + scale_att) + shift_att).astype(BF16)
    modded_all = flat(gather_tokens(modded))
    joined = dot(modded_all, full_qkv).reshape(count, length, 3, heads, HEAD_DIM)
    bias_q = bias_qv[0].reshape(heads, HEAD_DIM)
    bias_v = bias_qv[1].reshape(heads, HEAD_DIM)
    queries = (joined[:, :, 0] + bias_q).astype(BF16)
    keys = joined[:, :, 1].astype(BF16)
    values = (joined[:, :, 2] + bias_v).astype(BF16)
    scores = jnp.einsum("bqhd,bkhd->bhqk", queries, keys, preferred_element_type=F32) * (
        HEAD_DIM ** (-0.5)
    )
    soft = jax.nn.softmax(scores, axis=-1)
    soft_low = soft.astype(BF16)
    mixed = jnp.einsum("bhqk,bkhd->bqhd", soft_low, values, preferred_element_type=F32)
    mixed = mixed.astype(BF16).reshape(count, length, part)
    mixed_mine = lax.all_to_all(mixed, "seq", 1, 2, tiled=True)
    attended = dot(mixed_mine, full_out) + bias_out
    middle = tokens_f + gate_att * attended
    normed_two, inverse_two = layer_norm(middle)
    modded_two = (normed_two * (1.0 + scale_mlp) + shift_mlp).astype(BF16)
    modded_two_all = flat(gather_tokens(modded_two))
    hidden = dot(modded_two_all, full_fc1) + bias_fc1
    active, gelu_back = jax.vjp(partial(jax.nn.gelu, approximate=True), hidden)
    active = active.astype(BF16)

    def sum_tokens(partial_sums):
        parts = partial_sums.astype(BF16).reshape(count, length, width)
        return lax.psum_scatter(parts, "seq", scatter_dimension=1, tiled=True).astype(F32)

    branch = sum_tokens(dot(active, full_fc2)) + bias_fc2
    output = middle + gate_mlp * branch

    grad_output = out_grad.astype(F32)
    grad_gate_mlp = jnp.sum(grad_output * branch, axis=1)
    grad_branch = (gate_mlp * grad_output).astype(BF16)
    grad_branch_all = flat(gather_tokens(grad_branch))
    grad_hidden = gelu_back(dot_right_t(grad_branch_all, full_fc2))[0].astype(BF16)
    grad_modded_two = sum_tokens(dot_right_t(grad_hidden, full_fc1))
    grad_shift_mlp = jnp.sum(grad_modded_two, axis=1)
    grad_scale_mlp = jnp.sum(grad_modded_two * normed_two, axis=1)
    grad_middle = grad_output + norm_back(
        grad_modded_two * (1.0 + scale_mlp), normed_two, inverse_two
    )
    grad_gate_att = jnp.sum(grad_middle * attended, axis=1)
    grad_attended = (gate_att * grad_middle).astype(BF16)
    grad_mixed = dot_right_t(flat(grad_attended), full_out).astype(BF16)
    grad_mixed = lax.all_to_all(grad_mixed.reshape(latents.shape), "seq", 2, 1, tiled=True)
    grad_mixed = grad_mixed.reshape(count, length, heads, HEAD_DIM)
    grad_soft = jnp.einsum("bqhd,bkhd->bhqk", grad_mixed, values, preferred_element_type=F32)
    delta = jnp.sum(soft * grad_soft, axis=-1, keepdims=True)
    grad_scores = (soft * (grad_soft - delta)).astype(BF16)
    scale = HEAD_DIM ** (-0.5)
    grad_q = jnp.einsum("bhqk,bkhd->bqhd", grad_scores, keys, preferred_element_type=F32) * scale
    grad_k = jnp.einsum("bhqk,bqhd->bkhd", grad_scores, queries, preferred_element_type=F32) * scale
    grad_v = jnp.einsum("bhqk,bqhd->bkhd", soft_low, grad_mixed, preferred_element_type=F32)
    grad_joined = jnp.concatenate(
        [item.astype(BF16).reshape(count * length, part) for item in (grad_q, grad_k, grad_v)],
        axis=1,
    )
    grad_modded = sum_tokens(dot_right_t(grad_joined, full_qkv))
    grad_shift_att = jnp.sum(grad_modded, axis=1)
    grad_scale_att = jnp.sum(grad_modded * normed, axis=1)
    grad_tokens = grad_middle + norm_back(grad_modded * (1.0 + scale_att), normed, inverse)

    def from_columns(sums, groups):
        mine = lax.psum_scatter(sums.astype(BF16), "dp", scatter_dimension=0, tiled=True)
        blocks = lax.all_to_all(mine.reshape(seq, rows, -1), "seq", 0, 0, tiled=True)
        blocks = blocks.astype(F32).reshape(seq, rows, groups, -1)
        return blocks.transpose(1, 2, 0, 3).reshape(rows, -1)

    sums_fc2 = lax.psum_scatter(
        dot_left_t(active, grad_branch_all).astype(BF16), "dp", scatter_dimension=0, tiled=True
    ).astype(F32)
    sums_fc1 = from_columns(dot_left_t(modded_two_all, grad_hidden), dp)
    sums_out = lax.psum_scatter(
        dot_left_t(flat(mixed_mine), flat(grad_attended)).astype(BF16),
        both,
        scatter_dimension=0,
        tiled=True,
    ).astype(F32)
    sums_qkv = from_columns(dot_left_t(modded_all, grad_joined), 3)

    grad_mod = jnp.stack(
        [
            grad_shift_att,
            grad_scale_att,
            grad_gate_att,
            grad_shift_mlp,
            grad_scale_mlp,
            grad_gate_mlp,
        ],
        axis=1,
    )
    bias_sums = [
        jnp.sum(item.astype(F32), axis=0)
        for item in (grad_joined, flat(grad_attended), grad_hidden, flat(grad_branch))
    ]
    weight_sums = [sums_qkv, sums_out, sums_fc1, sums_fc2]
    return output.astype(BF16), grad_tokens.astype(BF16), grad_mod, bias_sums, weight_sums


def kernel_path(sz, latents, conditioning, w_mod, w_qkv, w_out, w_fc1, w_fc2, biases, out_grad):
    output, grad_tokens, grad_cond, sums_mod, small, sums_qkv, sums_out, sums_fc1, sums_fc2 = (
        run_kernel(
            sz,
            latents,
            out_grad,
            conditioning,
            *biases,
            w_mod,
            w_qkv,
            w_fc1,
            w_out,
            w_fc2,
        )
    )

    return arrange(
        sz, output, grad_tokens, sums_fc2, grad_cond, sums_mod, sums_qkv, sums_out, sums_fc1, small
    )


def arrange_kernel(sz, *refs):
    output, grad_tokens, fc2, cond, mod, qkv, out, fc1, small = refs[:9]
    (to_output, to_tokens, to_cond, to_mod, to_b_mod, to_qkv, to_b_qv) = refs[9:16]
    (to_out, to_b_out, to_fc1, to_b_fc1, to_fc2, to_b_fc2, sems) = refs[16:23]
    near = refs[23:]
    moves = [
        pltpu.make_async_copy(source, target, sems.at[index])
        for index, (source, target) in enumerate(zip(refs[:9], near))
    ]
    for move in moves:
        move.start()
    for move in moves:
        move.wait()
    output, grad_tokens, fc2, cond, mod, qkv, out, fc1, small = near
    moves = [
        pltpu.make_async_copy(source, target, sems.at[index])
        for index, (source, target) in enumerate(
            ((output, to_output), (grad_tokens, to_tokens), (fc2, to_fc2))
        )
    ]
    for move in moves:
        move.start()
    rows, pad, seq = sz.rows, sz.padded_rows, sz.seq

    def join(source, groups, size):
        pieces = [
            source[position * pad : (position + 1) * pad, group * size : (group + 1) * size]
            for group in range(groups)
            for position in range(seq)
        ]
        return jnp.concatenate([piece.astype(F32) for piece in pieces], axis=1)[:rows, :]

    to_cond[...] = cond[...]
    to_mod[...] = mod[:rows, :]
    to_out[...] = out[:rows, :]
    to_qkv[...] = join(qkv, 3, sz.part)
    to_fc1[...] = join(fc1, sz.dp, sz.units)
    for index, target in enumerate((to_b_out, to_b_fc2, to_b_qv, to_b_fc1, to_b_mod)):
        target[...] = small[index : index + 1, : target.shape[1]]
    for move in moves:
        move.wait()


def arrange(sz, output, grad_tokens, fc2, cond, mod, qkv, out, fc1, small):
    vmem = pl.BlockSpec(memory_space=pltpu.VMEM)
    far = pl.BlockSpec(memory_space=pl.ANY)
    low = lambda *shape: jax.ShapeDtypeStruct(shape, BF16)
    full = lambda *shape: jax.ShapeDtypeStruct(shape, F32)
    rows, width, hidden = sz.rows, sz.width, sz.hidden * sz.seq
    results = pl.pallas_call(
        partial(arrange_kernel, sz),
        out_shape=[
            low(*output.shape),
            low(*output.shape),
            low(sz.count, width),
            full(rows, 6 * width),
            full(1, 6 * rows),
            full(rows, 3 * width),
            full(1, 2 * rows),
            full(rows, width),
            full(1, rows),
            full(rows, hidden),
            full(1, sz.units),
            full(sz.units, width),
            full(1, rows),
        ],
        in_specs=[far] * 9,
        out_specs=[far, far] + [vmem] * 9 + [far, vmem],
        scratch_shapes=[pltpu.SemaphoreType.DMA((9,))]
        + [
            pltpu.VMEM(item.shape, item.dtype)
            for item in (output, grad_tokens, fc2, cond, mod, qkv, out, fc1, small)
        ],
        compiler_params=pltpu.CompilerParams(vmem_limit_bytes=66584576),
    )(output, grad_tokens, fc2, cond, mod, qkv, out, fc1, small)
    return tuple(item.reshape(-1) if item.shape[0] == 1 else item for item in results)


def column_blocks(seq, dp, w_qkv, w_fc1, units):
    rows = w_qkv.shape[0]
    qkv_blocks = w_qkv.reshape(rows, 3, seq, -1).transpose(2, 0, 1, 3).reshape(seq, rows, -1)
    fc1_blocks = w_fc1.reshape(rows, dp, seq, units).transpose(2, 0, 1, 3).reshape(seq, rows, -1)
    return qkv_blocks, fc1_blocks


def body(
    latents,
    conditioning,
    w_mod,
    b_mod,
    w_qkv,
    b_qv,
    w_out,
    b_out,
    w_fc1,
    b_fc1,
    w_fc2,
    b_fc2,
    out_grad,
):
    count, tokens, width = latents.shape
    dp, seq = lax.axis_size("dp"), lax.axis_size("seq")
    sz = Sizes(dp, seq, latents, w_qkv, w_fc2)
    if sz.fits():
        biases = (b_mod, b_qv, b_out, b_fc1, b_fc2)
        return kernel_path(
            sz, latents, conditioning, w_mod, w_qkv, w_out, w_fc1, w_fc2, biases, out_grad
        )
    both = ("dp", "seq")
    my_dp, my_seq = lax.axis_index("dp"), lax.axis_index("seq")
    me = my_dp * seq + my_seq
    rows, units = w_qkv.shape[0], w_fc2.shape[0]
    part = width // seq

    cond = conditioning.astype(F32)
    cond_act, silu_back = jax.vjp(jax.nn.silu, cond)
    cond_low = lax.all_gather(cond_act.astype(BF16), "dp", axis=0, tiled=True)
    cond_mine = lax.dynamic_slice_in_dim(cond_low, me * rows, rows, axis=1)
    mod_part = dot(cond_mine, w_mod)
    mod_sum = lax.psum(lax.psum_scatter(mod_part, "dp", scatter_dimension=0, tiled=True), "seq")
    biases = lax.all_gather(jnp.concatenate([b_mod, b_qv, b_out, b_fc1, b_fc2]), both, axis=0)
    pieces, start = [], 0
    for item in (b_mod, b_qv, b_out, b_fc1, b_fc2):
        pieces.append(biases[:, start : start + item.shape[0]].reshape(-1).astype(F32))
        start += item.shape[0]
    bias_mod, bias_qv, bias_out, bias_fc1, bias_fc2 = pieces
    bias_qv = lax.dynamic_index_in_dim(bias_qv.reshape(2, seq, part), my_seq, 1, keepdims=False)
    bias_fc1 = lax.dynamic_index_in_dim(
        bias_fc1.reshape(dp, seq, units), my_seq, 1, keepdims=False
    ).reshape(-1)
    modulation = (mod_sum + bias_mod).reshape(count, 6, width)

    blocks = column_blocks(seq, dp, w_qkv, w_fc1, units)
    output, grad_tokens, grad_mod, bias_sums, weight_sums = general_path(
        latents,
        out_grad,
        modulation,
        blocks,
        w_out,
        w_fc2,
        bias_qv,
        bias_out,
        bias_fc1,
        bias_fc2,
    )
    sums_qkv, sums_out, sums_fc1, sums_fc2 = weight_sums

    grad_mod = grad_mod.reshape(count, -1)
    grad_mod = lax.psum(grad_mod, "seq").astype(BF16)
    grad_mod = lax.all_gather(grad_mod, "dp", axis=0, tiled=True)
    sums_mod = dot_left_t(cond_mine, grad_mod)
    own = b_mod.shape[0]
    sums_bias_mod = jnp.sum(
        lax.dynamic_slice_in_dim(grad_mod, me * own, own, axis=1).astype(F32), axis=0
    )
    grad_cond_act = lax.all_gather(dot_right_t(grad_mod, w_mod), both, axis=0)
    grad_cond_act = lax.dynamic_slice_in_dim(grad_cond_act, my_dp * count, count, axis=1)
    grad_cond = silu_back(grad_cond_act.transpose(1, 0, 2).reshape(count, width))[0]

    def spread(values, shape):
        blank = jnp.zeros(shape, F32)
        return lax.dynamic_update_slice_in_dim(blank, values, my_seq, 1).reshape(-1)

    joined_sums, out_sums, fc1_sums, fc2_sums = bias_sums
    qv_sums = jnp.stack([joined_sums[:part], joined_sums[2 * part : 3 * part]])
    bias_sums = [
        spread(qv_sums.reshape(2, 1, part), (2, seq, part)),
        out_sums,
        spread(fc1_sums.reshape(dp, 1, units), (dp, seq, units)),
        fc2_sums,
    ]
    joint = jnp.concatenate([item.reshape(dp * seq, -1) for item in bias_sums], axis=1)
    joint = lax.psum_scatter(joint, both, scatter_dimension=0, tiled=True).reshape(-1)
    cuts = [b_qv.shape[0], b_out.shape[0], b_fc1.shape[0]]
    sums_bias_qv, sums_bias_out, sums_bias_fc1, sums_bias_fc2 = jnp.split(
        joint, [cuts[0], cuts[0] + cuts[1], sum(cuts)]
    )
    return (
        output,
        grad_tokens,
        grad_cond.astype(BF16),
        sums_mod,
        sums_bias_mod,
        sums_qkv,
        sums_bias_qv,
        sums_out,
        sums_bias_out,
        sums_fc1,
        sums_bias_fc1,
        sums_fc2,
        sums_bias_fc2,
    )


def solution(mesh):
    both = P(("dp", "seq"))
    wide = P(("dp", "seq"), None)
    tokens = P("dp", "seq", None)
    in_specs = (
        tokens,
        P("dp", None),
        wide,
        both,
        wide,
        both,
        wide,
        both,
        wide,
        both,
        wide,
        both,
        tokens,
    )
    out_specs = (tokens, tokens, P("dp", None)) + (wide, both) * 5
    return jax.shard_map(body, mesh=mesh, in_specs=in_specs, out_specs=out_specs, check_vma=False)
```

```python
from functools import partial
from types import SimpleNamespace
from typing import NamedTuple

import jax
import jax.numpy as jnp
from jax import lax
from jax.experimental import pallas as pl
from jax.experimental.pallas import tpu as pltpu
from jax.sharding import PartitionSpec as P

HEADS = 16
HEAD_DIM = 72
EPSILON = 1e-06
BF16 = jnp.bfloat16
F32 = jnp.float32


def layer_norm(values):
    center = values - jnp.mean(values, axis=-1, keepdims=True)
    inverse = lax.rsqrt(jnp.mean(center * center, axis=-1, keepdims=True) + EPSILON)
    return (center * inverse, inverse)


def norm_back(incoming, normed, inverse):
    return inverse * (
        incoming
        - jnp.mean(incoming, axis=-1, keepdims=True)
        - normed * jnp.mean(incoming * normed, axis=-1, keepdims=True)
    )


def dot(left, right):
    return jnp.dot(left, right, preferred_element_type=F32)


def dot_right_t(left, right):
    return lax.dot_general(left, right, (((1,), (1,)), ((), ())), preferred_element_type=F32)


def dot_left_t(left, right):
    return lax.dot_general(left, right, (((0,), (0,)), ((), ())), preferred_element_type=F32)


MESH = pl.DeviceIdType.MESH
ROOT = HEAD_DIM ** (-0.5)
LANES = 128
ROWS = 64


class Sizes:
    def __init__(self, dp, seq, latents, w_qkv, w_fc2):
        self.dp, self.seq, self.line = dp, seq, dp // 2
        self.count, self.tokens, self.width = latents.shape
        self.rows, self.units = w_qkv.shape[0], w_fc2.shape[0]
        self.chunk = seq * self.rows
        self.hidden = dp * self.units
        self.heads = HEADS // seq
        self.part = self.width // seq
        self.length = seq * self.tokens
        self.total = self.count * self.length
        self.own = self.count * self.tokens
        self.padded_rows = -(-self.rows // 16) * 16
        self.joined = -(-3 * self.part // LANES) * LANES
        self.mod_part = -(-6 * self.width // (seq * LANES)) * LANES

    def fits(self):
        return (
            self.seq == 4
            and self.dp % 2 == 0
            and self.dp == 8
            and self.count == 2
            and self.width == self.dp * self.chunk
            and self.chunk % 16 == 0
            and self.units % 16 == 0
            and self.tokens % 128 == 0
            and self.width % LANES == 0
            and self.hidden == self.width
            and self.chunk == self.units
        )


def column_cuts(width, most=512):
    cuts, start = [], 0
    while start < width:
        size = min(most, width - start)
        cuts.append((start, size))
        start += size
    return cuts


def one_hot(rows, columns, group, padded, flip):
    shape = (columns, rows) if flip else (rows, columns)
    tight = lax.broadcasted_iota(jnp.int32, shape, 1 if flip else 0)
    loose = lax.broadcasted_iota(jnp.int32, shape, 0 if flip else 1)
    hit = jnp.zeros(shape, F32)
    for index in range(rows // group):
        inside = (tight >= index * group) & (tight < (index + 1) * group)
        match = loose == tight + index * (padded - group)
        hit = jnp.where(inside & match, 1.0, hit)
    return hit.astype(BF16)


def block_kernel(sz, *refs):
    names = Inputs._fields + Outputs._fields + tuple(kernel_scratch(sz))
    r = SimpleNamespace(**dict(zip(names, refs)))
    dp_me, s_me = lax.axis_index("dp"), lax.axis_index("seq")
    z_me, x_me = dp_me // 2, dp_me % 2
    y_me, c_me = s_me // 2, s_me % 2
    count, tokens, width = sz.count, sz.tokens, sz.width
    line, seq = sz.line, sz.seq

    def seq_peer(mask):
        flip_y, flip_c = mask // 2, mask % 2
        y = 1 - y_me if flip_y else y_me
        c = 1 - c_me if flip_c else c_me
        return y * 2 + c

    def z_peer(step):
        return lax.rem(z_me + step, line)

    def device_seq(mask):
        return (dp_me, seq_peer(mask))

    def device_z(step):
        return (z_peer(step) * 2 + x_me, s_me)

    inner = z_me % 3 != 0
    outer = z_me % 3 == 0

    def z_flip(mask):
        return (z_me, z_me + 1 - 2 * (z_me % 2), lax.rem(z_me + 2, line), line - 1 - z_me)[mask]

    def device_flip(mask):
        return (z_flip(mask) * 2 + x_me, s_me)

    device_x = (z_me * 2 + (1 - x_me), s_me)
    used = [0, 0]

    def copy_to(src, dst, device, arrival=None):
        index = used[0]
        used[0] += 1
        return pltpu.make_async_remote_copy(
            src_ref=src,
            dst_ref=dst,
            send_sem=r.send_sems.at[index],
            recv_sem=r.recv_sems.at[index] if arrival is None else arrival,
            device_id=device,
            device_id_type=MESH,
        )

    def send(src, dst, device, arrival=None):
        copy = copy_to(src, dst, device, arrival)
        copy.start()
        return copy

    def local(src, dst):
        index = used[1]
        used[1] += 1
        copy = pltpu.make_async_copy(src, dst, r.local_sems.at[index])
        copy.start()
        return copy

    def rows_of(ref, start, size):
        return ref.at[pl.ds(start, size)]

    raw_moves = [
        local(source, target)
        for source, target in (
            (r.qkv_src, r.qkv_raw),
            (r.fc1_src, r.fc1_raw),
            (r.out_src, r.out_raw),
        )
    ]

    peers = [device_seq(mask) for mask in (1, 2, 3)]
    peers += [device_z(step) for step in range(1, line)] + [device_x]
    barrier = pltpu.get_barrier_semaphore()
    for peer in peers:
        pl.semaphore_signal(barrier, inc=1, device_id=peer, device_id_type=MESH)
    pl.semaphore_wait(barrier, len(peers))

    pending = []
    far_moves = []

    def release(copy):
        copy.wait_send()
        pending[:] = [item for item in pending if item is not copy]

    def token_rows(ref, latent, position):
        return rows_of(ref, (latent * seq + position) * tokens, tokens)

    class GatherTokens:
        def __init__(self, ref, latent, source=None):
            self.ref, self.latent = ref, latent
            slot = token_rows(ref, latent, s_me)
            mine = slot if source is None else source
            self.core = send(mine, slot, device_seq(1))
            self.chip = send(mine, slot, device_seq(2))

        def forward(self):
            self.chip.wait_recv()
            slot = token_rows(self.ref, self.latent, seq_peer(2))
            self.last = send(slot, slot, device_seq(1))

        def finish(self):
            self.core.wait_recv()
            self.last.wait_recv()
            for copy in (self.core, self.chip, self.last):
                pending.append(copy)

    class SumTokens:
        def __init__(self, part, slot, latent):
            self.part, self.slot, self.latent = part, slot, latent
            self.first = [
                send(
                    token_rows(part, latent, y * 2 + 1 - c_me),
                    r.sum_core.at[slot, y, latent],
                    device_seq(1),
                )
                for y in range(2)
            ]

        def forward(self):
            for copy in self.first:
                copy.wait_recv()
            other = 1 - y_me
            total = token_rows(self.part, self.latent, other * 2 + c_me)[...].astype(F32)
            total = total + r.sum_core[self.slot, other, self.latent].astype(F32)
            r.sum_send[self.slot, self.latent] = total.astype(BF16)
            self.last = send(
                r.sum_send.at[self.slot, self.latent],
                r.sum_chip.at[self.slot, self.latent],
                device_seq(2),
            )

        def finish(self):
            self.last.wait_recv()
            for copy in self.first + [self.last]:
                copy.wait_send()

        def rows(self, start):
            place = pl.ds((self.latent * seq + s_me) * tokens + start, ROWS)
            here = pl.ds(start, ROWS)
            total = self.part[place, :].astype(F32)
            total = total + r.sum_core[self.slot, y_me, self.latent, here, :].astype(F32)
            return total + r.sum_chip[self.slot, self.latent, here, :].astype(F32)

    def exchange(pick, place):
        return [send(pick(seq_peer(mask)), place(s_me), device_seq(mask)) for mask in (1, 2, 3)]

    def settle(copies):
        for copy in copies:
            copy.wait_recv()
        pending.extend(copies)

    class GatherWeights:
        def __init__(self, ref, chunk, direct=False):
            self.ref, self.chunk, self.direct = ref, chunk, direct

        def slot(self, dp):
            return rows_of(self.ref, dp * self.chunk, self.chunk)

        def push_along(self, source=None):
            own = self.slot(dp_me)
            mine = own if source is None else source
            self.along = [send(mine, own, device_flip(mask)) for mask in (2, 1)]
            self.arrival = r.recv_sems.at[used[0]]
            self.last = copy_to(mine, own, device_flip(3))
            if self.direct:
                self.last.start()
            else:
                pl.when(inner)(self.last.start)
            self.across, self.passed = [], 0

        def push_across(self, source=None):
            own = self.slot(dp_me)
            mine = own if source is None else source
            self.across.append(send(mine, own, device_x))

        def push(self, source=None):
            self.push_along(source)
            self.push_across(source)

        def forward(self, limit=3):
            for mask in (2, 1, 3)[self.passed :][:limit]:
                (self.along + [self.last])[self.passed].wait_recv()
                self.passed += 1
                came = self.slot(z_flip(mask) * 2 + x_me)
                if mask == 2 and not self.direct:
                    self.relay = copy_to(came, came, device_flip(1), self.arrival)
                    pl.when(inner)(self.relay.start)
                self.across.append(send(came, came, device_x))

        def finish(self):
            for copy in self.across:
                copy.wait_recv()

        def drain(self):
            for copy in self.along + self.across:
                copy.wait_send()
            if self.direct:
                self.last.wait_send()
                return

            @pl.when(inner)
            def _():
                self.last.wait_send()
                self.relay.wait_send()

    class SumWeights:
        def __init__(self, ref, chunk, across_ref, along_ref, columns):
            self.ref, self.chunk, self.columns = ref, chunk, columns
            self.across_ref, self.along_ref = across_ref, along_ref
            self.across = {}

        def view(self, ref, index):
            return ref.at[index, :, pl.ds(0, self.columns)]

        def slot(self, dp):
            return rows_of(self.ref, dp * self.chunk, self.chunk)

        def push(self, masks=(3, 2, 1, 0)):
            if not self.across:
                self.across, self.passed = {}, []
            for mask in masks:
                self.across[mask] = send(
                    self.slot(z_flip(mask) * 2 + 1 - x_me),
                    self.view(self.across_ref, mask),
                    device_x,
                )

        def forward(self, limit=3):
            for mask in (3, 2, 1)[len(self.passed) :][:limit]:
                self.passed.append(mask)
                self.across[mask].wait_recv()
                slot = self.slot(z_flip(mask) * 2 + x_me)
                came = self.view(self.across_ref, mask)

                def total():
                    return slot[...].astype(F32) + came[...].astype(F32)

                extra = self.view(self.along_ref, 0)
                if mask == 3:
                    slot[...] = total().astype(BF16)
                    self.direct = copy_to(slot, self.view(self.along_ref, 3), device_flip(3))
                    self.relay = copy_to(slot, extra, device_flip(1))
                    pl.when(inner)(self.direct.start)
                    pl.when(outer)(self.relay.start)
                elif mask == 2:

                    @pl.when(inner)
                    def _():
                        self.relay.wait_recv()
                        slot[...] = (total() + extra[...].astype(F32)).astype(BF16)

                    @pl.when(outer)
                    def _():
                        slot[...] = total().astype(BF16)

                    self.two = send(slot, self.view(self.along_ref, 2), device_flip(2))
                else:
                    slot[...] = total().astype(BF16)
                    self.one = send(slot, self.view(self.along_ref, 1), device_flip(1))

        def finish(self, target):
            self.across[0].wait_recv()
            total = self.slot(dp_me)[...].astype(F32)
            total = total + self.view(self.across_ref, 0)[...].astype(F32)
            for copy, mask in ((self.one, 1), (self.two, 2)):
                copy.wait_recv()
                total = total + self.view(self.along_ref, mask)[...].astype(F32)
            target[...] = total

            @pl.when(inner)
            def _():
                self.direct.wait_recv()
                target[...] += self.view(self.along_ref, 3)[...].astype(F32)
                self.direct.wait_send()

            @pl.when(outer)
            def _():
                self.relay.wait_send()

            for copy in [self.one, self.two] + list(self.across.values()):
                copy.wait_send()

    pad = sz.padded_rows
    qkv_blocks, fc1_blocks = r.qkv_blocks, r.fc1_blocks
    out_wide = sz.dp * pad
    out_mine = rows_of(r.out_blocks, s_me * out_wide, out_wide)

    cond = r.conditioning[...].astype(F32)
    gate_cond = 1.0 / (1.0 + jnp.exp(-cond))
    low_rows = jnp.concatenate([cond * gate_cond, jnp.zeros((16 - count, width), F32)], axis=0)
    rows_of(r.cond_all, dp_me * 16, 16)[...] = low_rows.astype(BF16)
    gather_cond = GatherWeights(r.cond_all, 16)
    gather_cond.push()
    for move in raw_moves:
        move.wait()
    own_out = jnp.concatenate(
        [r.out_raw[...].astype(F32), jnp.zeros((pad - sz.rows, width), F32)], axis=0
    )
    rows_of(out_mine, dp_me * pad, pad)[...] = own_out.astype(BF16)
    gather_out = GatherWeights(out_mine, pad)
    gather_out.push()
    qkv_send, fc1_send = r.qkv_rows, r.fc1_rows
    qkv_send[...] = jnp.zeros_like(qkv_send)
    fc1_send[...] = jnp.zeros_like(fc1_send)
    for position in range(seq):
        here = slice(position * pad, position * pad + sz.rows)
        pieces = [
            r.qkv_raw[:, kind * width + position * sz.part :][:, : sz.part] for kind in range(3)
        ]
        qkv_send[here, : 3 * sz.part] = jnp.concatenate(pieces, axis=1)
        pieces = [
            r.fc1_raw[:, (group * seq + position) * sz.units :][:, : sz.units]
            for group in range(sz.dp)
        ]
        fc1_send[here, :] = jnp.concatenate(pieces, axis=1)
    qkv_local, fc1_local = [
        local(rows_of(source, s_me * pad, pad), rows_of(target, s_me * pad, pad))
        for source, target in ((qkv_send, qkv_blocks), (fc1_send, fc1_blocks))
    ]
    lat_local, og_local = [
        [local(source.at[latent], token_rows(target, latent, s_me)) for latent in range(count)]
        for source, target in ((r.latents, r.lat_all), (r.out_grad, r.grad_branch))
    ]
    fc2_local = local(r.fc2_src, rows_of(r.fc2, dp_me * sz.units, sz.units))

    def place(values, start, size):
        blank = jnp.zeros((1, size - values.shape[1]), F32)
        row = jnp.concatenate([values.astype(F32), blank], axis=1)
        return pltpu.roll(jnp.broadcast_to(row, (8, size)), start, 1)[0:1, :]

    def when(hit, values):
        return jnp.where(hit, values, jnp.zeros_like(values))

    me = dp_me * seq + s_me
    own_mod, own_qv, own_out, own_fc1, own_fc2 = [
        ref[...].astype(F32).reshape(1, -1) for ref in (r.b_mod, r.b_qv, r.b_out, r.b_fc1, r.b_fc2)
    ]
    devices = sz.dp * seq
    half_way = devices // 2
    qv_row = place(own_qv, lax.rem(me, half_way) * (2 * sz.rows), width)
    fc1_row = place(own_fc1, dp_me * sz.units, width)
    bias_rows = [
        place(own_out, me * sz.rows, width),
        place(own_fc2, me * sz.rows, width),
        when(me < half_way, qv_row),
        when(me >= half_way, qv_row),
    ] + [when(s_me == position, fc1_row) for position in range(seq)]
    bias_rows.append(jnp.zeros((16 - len(bias_rows), width), F32))
    bias_mine = rows_of(r.bias_blocks, s_me * 16, 16)
    bias_mine[...] = jnp.concatenate(bias_rows, axis=0).astype(BF16)
    bias_moves = exchange(lambda peer: bias_mine, lambda me: rows_of(r.bias_blocks, me * 16, 16))
    qkv_moves = exchange(
        lambda peer: rows_of(qkv_send, peer * pad, pad),
        lambda me: rows_of(qkv_blocks, me * pad, pad),
    )
    fc1_moves = exchange(
        lambda peer: rows_of(fc1_send, peer * pad, pad),
        lambda me: rows_of(fc1_blocks, me * pad, pad),
    )

    tighten = one_hot(sz.chunk, seq * pad, sz.rows, pad, False)
    loosen = one_hot(sz.chunk, seq * pad, sz.rows, pad, True)
    gather_qkv = GatherWeights(r.qkv, sz.chunk)
    gather_fc1 = GatherWeights(r.fc1, sz.chunk)
    gather_fc2 = GatherWeights(r.fc2, sz.units)
    settle(bias_moves)
    bias_sum = sum(
        r.bias_blocks[position * 16 : (position + 1) * 16, :].astype(F32) for position in range(seq)
    )
    rows_of(r.bias_all, dp_me * 16, 16)[...] = bias_sum.astype(BF16)
    gather_bias = GatherWeights(r.bias_all, 16)
    gather_bias.push()
    gather_cond.forward()
    gather_out.forward(1)
    qkv_local.wait()
    settle(qkv_moves)
    rows_of(r.qkv, dp_me * sz.chunk, sz.chunk)[...] = dot(tighten, qkv_blocks[...]).astype(BF16)
    gather_qkv.push_along()

    gather_cond.finish()
    gather_qkv.push_across()
    iota = partial(lax.broadcasted_iota, jnp.int32)
    hit = iota((width, LANES), 0) == iota((width, LANES), 1) + me * sz.rows
    hit = hit & (iota((width, LANES), 1) < sz.rows)
    cond_mine = dot(r.cond_all[...], jnp.where(hit, 1.0, 0.0).astype(BF16)).astype(BF16)
    r.cond_mine[...] = cond_mine
    order = iota((16, sz.dp * 16), 0)
    across, along, which = order >> 3, (order >> 1) & (line - 1), order & 1
    hit = iota((16, sz.dp * 16), 1) == (along * 2 + across) * 16 + which
    cond_rows = dot(jnp.where(hit, 1.0, 0.0).astype(BF16), cond_mine).astype(BF16)
    cond_rows = cond_rows[:, : sz.rows]
    mod_wide = sz.mod_part * seq
    own_row = place(own_mod, me * (6 * sz.rows), mod_wide)
    for comp in range(6):
        here = slice(comp * width, (comp + 1) * width)
        r.mod_sums[:, here] = dot(cond_rows, r.w_mod[:, here]) + own_row[:, here]
    r.mod_sums[:, 6 * width :] = jnp.zeros((16, mod_wide - 6 * width), F32)

    def mod_part(position):
        return r.mod_sums.at[:, pl.ds(pl.multiple_of(position * sz.mod_part, LANES), sz.mod_part)]

    mod_core = [
        send(mod_part(y * 2 + 1 - c_me), r.mod_core.at[y], device_seq(1)) for y in range(2)
    ]
    gather_out.forward()
    fc1_local.wait()
    settle(fc1_moves)
    rows_of(r.fc1, dp_me * sz.chunk, sz.chunk)[...] = dot(tighten, fc1_blocks[...]).astype(BF16)
    for copy in mod_core:
        copy.wait_recv()
    r.mod_send[...] = mod_part((1 - y_me) * 2 + c_me)[...] + r.mod_core[1 - y_me]
    mod_chip = send(r.mod_send, r.mod_chip, device_seq(2))
    lat_moves = [
        GatherTokens(r.lat_all, latent, r.latents.at[latent]) for latent in range(count)
    ]
    mod_chip.wait_recv()
    r.mod_sum[...] = mod_part(s_me)[...] + r.mod_core[y_me] + r.mod_chip[...]
    mod_x = send(rows_of(r.mod_sum, (1 - x_me) * 8, 8), r.mod_x, device_x)
    gather_bias.forward(1)
    gather_qkv.forward(1)
    mod_x.wait_recv()
    r.mod_half[...] = rows_of(r.mod_sum, x_me * 8, 8)[...] + r.mod_x[...]
    mod_z = [send(r.mod_half, r.mod_z.at[step], device_z(step)) for step in range(1, line)]
    gather_fc1.push_along()
    gather_bias.forward()
    og_moves = [GatherTokens(r.grad_branch, 0, r.out_grad.at[0])]
    gather_fc1.push_across()
    gather_qkv.forward()
    for move in lat_moves:
        move.forward()
    gather_out.finish()
    mod_total = r.mod_half[...]
    for copy, step in zip(mod_z, range(1, line)):
        copy.wait_recv()
        mod_total = mod_total + r.mod_z[step]
    hit = iota((8, sz.mod_part), 0)
    picked = [
        jnp.sum(jnp.where(hit == z_me * count + latent, mod_total, 0.0), axis=0, keepdims=True)
        for latent in range(count)
    ]
    picked.append(jnp.zeros((8 - count, sz.mod_part), F32))
    mod_slot = r.mod_all.at[s_me]
    mod_slot[...] = jnp.concatenate(picked, axis=0)
    mod_moves = [send(mod_slot, mod_slot, device_seq(mask)) for mask in (1, 2)]
    out_core = send(out_mine, out_mine, device_seq(1))
    out_chip = send(out_mine, out_mine, device_seq(2))
    mod_moves[1].wait_recv()
    mod_slot = r.mod_all.at[seq_peer(2)]
    mod_moves.append(send(mod_slot, mod_slot, device_seq(1)))
    gather_bias.finish()
    bias = jnp.sum(r.bias_all[...].astype(F32).reshape(sz.dp, 16, width), axis=0)
    bias_out, bias_fc2 = bias[0:1, :], bias[1:2, :]
    part = sz.part

    def own_part(row):
        return sum(
            when(s_me == position, row[:, position * part : (position + 1) * part])
            for position in range(seq)
        )

    r.bias_joined[...] = jnp.concatenate(
        [
            own_part(bias[2:3, :]),
            jnp.zeros((1, part), F32),
            own_part(bias[3:4, :]),
            jnp.zeros((1, sz.joined - 3 * part), F32),
        ],
        axis=1,
    )
    r.bias_fc1[...] = sum(
        when(s_me == position, bias[4 + position : 5 + position, :]) for position in range(seq)
    )
    r.bias_out[...] = bias_out
    r.bias_fc2[...] = bias_fc2
    mod_moves[0].wait_recv()
    mod_moves[2].wait_recv()
    wide = jnp.concatenate([r.mod_all[position] for position in range(seq)], axis=1)
    mod = r.modulation
    for latent in range(count):
        for comp in range(6):
            mod[latent, comp : comp + 1, :] = wide[
                latent : latent + 1, comp * width : (comp + 1) * width
            ]
    pending.extend(mod_core + [mod_chip, mod_x] + mod_z + mod_moves)
    gather_fc1.forward(1)
    for copy in qkv_moves + fc1_moves:
        release(copy)
    gather_bias.drain()
    gather_cond.drain()
    fc2_local.wait()
    gather_fc2.push()

    for copy in lat_local:
        copy.wait()
    for move in lat_moves:
        move.finish()

    heads, length = sz.heads, sz.length

    def modulate_tokens(step, carry):
        latent = step // (length // ROWS)
        here = pl.ds(pl.multiple_of(step * ROWS, ROWS), ROWS)
        normed, _ = layer_norm(r.lat_all[here, :].astype(F32))
        shift, scale = mod[latent, 0:1, :], mod[latent, 1:2, :]
        r.modded[here, :] = (normed * (1.0 + scale) + shift).astype(BF16)
        return carry

    lax.fori_loop(0, count * length // ROWS, modulate_tokens, 0)

    gather_qkv.finish()
    tile = 2 * tokens
    per_latent = length // tile

    def pad_head(values):
        return jnp.concatenate(
            [values, jnp.zeros((values.shape[0], LANES - HEAD_DIM), values.dtype)], axis=1
        )

    def project(step, carry):
        start = pl.multiple_of(step * tile, tile)
        latent = step // per_latent
        row = pl.multiple_of((step % per_latent) * tile, tile)
        joined = dot(r.modded[pl.ds(start, tile), :], r.qkv[...]) + r.bias_joined[...]
        for kind, target in enumerate((r.q_heads, r.k_heads, r.v_heads)):
            for head in range(heads):
                column = kind * part + head * HEAD_DIM
                piece = pad_head(joined[:, column : column + HEAD_DIM]).astype(BF16)
                target[latent * heads + head, pl.ds(row, tile), :] = piece
        return carry

    lax.fori_loop(0, count * per_latent, project, 0)
    gather_fc1.forward(1)

    half = length // 2

    def attend(index, carry):
        keys, values = r.k_heads[index], r.v_heads[index]

        for row in range(0, length, half):
            here = slice(row, row + half)
            scores = dot_right_t(r.q_heads[index, here, :], keys) * ROOT
            expon = jnp.exp(scores - jnp.max(scores, axis=-1, keepdims=True))
            soft = (expon * (1.0 / jnp.sum(expon, axis=-1, keepdims=True))).astype(BF16)
            r.soft[index, here, :] = soft
            r.o_heads[index, here, :] = dot(soft, values).astype(BF16)
        return carry

    mixed_moves = []
    for latent in range(count):
        lax.fori_loop(latent * heads, (latent + 1) * heads, attend, 0)

        def assemble(block, carry, latent=latent):
            row = pl.multiple_of(block * tokens, tokens)
            pieces = [
                r.o_heads[latent * heads + head, pl.ds(row, tokens), :][:, :HEAD_DIM]
                for head in range(heads)
            ]
            r.mixed_send[block, latent] = jnp.concatenate(pieces, axis=1)
            return carry

        lax.fori_loop(0, seq, assemble, 0)
        own = local(r.mixed_send.at[s_me, latent], r.mixed_recv.at[s_me, latent])
        mixed_moves.append(
            (
                own,
                exchange(
                    lambda peer, latent=latent: r.mixed_send.at[peer, latent],
                    lambda me, latent=latent: r.mixed_recv.at[me, latent],
                ),
            )
        )
        if latent == 0:
            gather_fc1.forward()
            out_chip.wait_recv()
            other = rows_of(r.out_blocks, seq_peer(2) * out_wide, out_wide)
            out_last = send(other, other, device_seq(1))
    og_moves[0].forward()
    gather_fc2.forward(1)

    out_core.wait_recv()
    out_last.wait_recv()
    pending.extend([out_core, out_chip, out_last])

    def tighten_out(step, carry):
        blocks = [
            r.out_blocks[pl.ds(pl.multiple_of(block * out_wide + step * pad, 16), pad), :]
            for block in range(seq)
        ]
        start = pl.multiple_of(step * sz.chunk, 16)
        packed = dot(tighten, jnp.concatenate(blocks, axis=0))
        r.out[pl.ds(start, sz.chunk), :] = packed.astype(BF16)
        return carry

    lax.fori_loop(0, sz.dp, tighten_out, 0)

    m2_moves = []
    for latent in range(count):
        own, moves = mixed_moves[latent]
        own.wait()
        settle(moves)
        pieces = [r.mixed_recv[block, latent] for block in range(seq)]
        mixed = jnp.concatenate(pieces, axis=1)
        here = pl.ds(latent * tokens, tokens)
        r.mixed[here, :] = mixed
        r.attended[here, :] = dot(mixed, r.out[...]) + r.bias_out[...]

        def second_norm(step, carry, latent=latent):
            start = pl.multiple_of(step * ROWS, ROWS)
            here = pl.ds(latent * tokens + start, ROWS)
            tokens_in = r.latents[latent, pl.ds(start, ROWS), :].astype(F32)
            middle = tokens_in + mod[latent, 2:3, :] * r.attended[here, :]
            r.middle[here, :] = middle
            normed, _ = layer_norm(middle)
            modded = normed * (1.0 + mod[latent, 4:5, :]) + mod[latent, 3:4, :]
            place = pl.multiple_of((latent * seq + s_me) * tokens + start, ROWS)
            r.modded_two[pl.ds(place, ROWS), :] = modded.astype(BF16)
            return carry

        lax.fori_loop(0, tokens // ROWS, second_norm, 0)
        m2_moves.append(GatherTokens(r.modded_two, latent))

    for latent in range(1, count):
        og_moves.append(GatherTokens(r.grad_branch, latent, r.out_grad.at[latent]))
    gather_fc2.forward(1)
    for copy in og_local:
        copy.wait()
    for move in lat_moves:
        release(move.last)

    def gate_grads(step, carry):
        here = pl.ds(pl.multiple_of(step * ROWS, ROWS), ROWS)
        gate = mod[step // (length // ROWS), 5:6, :]
        r.grad_branch[here, :] = (r.grad_branch[here, :].astype(F32) * gate).astype(BF16)
        return carry

    def gate_latent(latent):
        og_moves[latent].finish()
        release(og_moves[latent].last)
        steps = length // ROWS
        lax.fori_loop(latent * steps, (latent + 1) * steps, gate_grads, 0)

    gate_latent(0)
    m2_moves[0].forward()
    gather_fc2.forward()

    cuts = column_cuts(sz.hidden, 256)
    gather_fc1.finish()
    for latent in range(count):
        m2_moves[latent].finish()

        def mlp(step, carry, latent=latent):
            start = pl.multiple_of(latent * length + step * tile, tile)
            rows = r.modded_two[pl.ds(start, tile), :]
            for column, size in cuts:
                here = slice(column, column + size)
                hidden = dot(rows, r.fc1[:, here]) + r.bias_fc1[:, here]
                square = hidden * hidden
                inner = 0.7978845608028654 * (hidden + 0.044715 * square * hidden)
                bent = jnp.tanh(inner)
                r.lat_all[pl.ds(start, tile), here] = (0.5 * hidden * (1.0 + bent)).astype(BF16)
                slope = 0.5 * (1.0 + bent) + 0.5 * hidden * (1.0 - bent * bent) * (
                    0.7978845608028654 * (1.0 + 3 * 0.044715 * square)
                )
                r.part_a[pl.ds(start, tile), here] = slope.astype(BF16)
            return carry

        lax.fori_loop(0, per_latent, mlp, 0)
        if latent + 1 < count:
            m2_moves[latent + 1].forward()

    for copy in (out_core, out_chip, out_last):
        release(copy)
    gather_out.drain()

    def weight_grad(left, right, target):
        size = 384 if width % 384 == 0 else LANES

        def tiles(step, carry):
            start = pl.multiple_of(step * size, LANES)
            sums = dot_left_t(left[:, pl.ds(start, size)], right[...])
            target[pl.ds(start, size), :] = sums.astype(BF16)
            return carry

        lax.fori_loop(0, left.shape[1] // size, tiles, 0)

    for latent in range(1, count):
        og_moves[latent].forward()
        gate_latent(latent)
    weight_grad(r.lat_all, r.grad_branch, r.out_blocks)
    sum_fc2 = SumWeights(r.out_blocks, sz.units, r.across_b, r.along_b, width)
    sum_fc2.push()

    gather_fc2.finish()
    r.fc1_sums[...] = jnp.zeros_like(r.fc1_sums)
    grad_moves = []
    for latent in range(count):

        def mlp_back(step, carry, latent=latent):
            start = pl.multiple_of(latent * length + step * tile, tile)
            incoming = r.grad_branch[pl.ds(start, tile), :]
            for column, size in cuts:
                here = slice(column, column + size)
                slope = r.part_a[pl.ds(start, tile), here].astype(F32)
                grads = (dot_right_t(incoming, r.fc2[here, :]) * slope).astype(BF16)
                r.grad_hidden[pl.ds(start, tile), here] = grads
                r.fc1_sums[:, here] += jnp.sum(grads.astype(F32), axis=0, keepdims=True)
            return carry

        lax.fori_loop(0, per_latent, mlp_back, 0)
        if latent:
            grad_moves[latent - 1].forward()

        def back_fc1(step, carry, latent=latent):
            start = pl.multiple_of(latent * length + step * tile, tile)
            rows = r.grad_hidden[pl.ds(start, tile), :]
            for column, size in column_cuts(width):
                here = slice(column, column + size)
                sums = dot_right_t(rows, r.fc1[here, :])
                r.part_a[pl.ds(start, tile), here] = sums.astype(BF16)
            return carry

        lax.fori_loop(0, per_latent, back_fc1, 0)
        grad_moves.append(SumTokens(r.part_a, 0, latent))

    for move in m2_moves:
        for copy in (move.core, move.chip, move.last):
            release(copy)
    gather_fc1.drain()
    grad_moves[-1].forward()
    weight_grad(r.modded_two, r.grad_hidden, r.fc1)
    sum_fc1 = SumWeights(r.fc1, sz.chunk, r.across_a, r.along_a, sz.hidden)
    sum_fc1.push()

    gather_fc2.drain()
    branch_moves = []
    for latent in range(count):

        def branch_out(step, carry, latent=latent):
            start = pl.multiple_of(latent * length + step * tile, tile)
            sums = dot(r.lat_all[pl.ds(start, tile), :], r.fc2[...])
            r.lat_all[pl.ds(start, tile), :] = sums.astype(BF16)
            return carry

        lax.fori_loop(0, per_latent, branch_out, 0)
        branch_moves.append(SumTokens(r.lat_all, 1, latent))

    grad_mod = r.grad_mod
    grad_mod[...] = jnp.zeros_like(grad_mod)

    def total_rows(values):
        return jnp.sum(values, axis=0, keepdims=True)

    r.bias_sums[...] = jnp.zeros_like(r.bias_sums)
    mix_moves = []
    for latent in range(count):
        grad_moves[latent].finish()

        def second_back(step, carry, latent=latent):
            start = pl.multiple_of(step * ROWS, ROWS)
            here = pl.ds(latent * tokens + start, ROWS)
            incoming = grad_moves[latent].rows(start)
            normed, inverse = layer_norm(r.middle[here, :])
            grad_mod[latent, 3:4, :] += total_rows(incoming)
            grad_mod[latent, 4:5, :] += total_rows(incoming * normed)
            grad_middle = r.out_grad[latent, pl.ds(start, ROWS), :].astype(F32) + norm_back(
                incoming * (1.0 + mod[latent, 4:5, :]), normed, inverse
            )
            r.grad_middle[here, :] = grad_middle
            grad_mod[latent, 2:3, :] += total_rows(grad_middle * r.attended[here, :])
            grad_attended = (mod[latent, 2:3, :] * grad_middle).astype(BF16)
            r.grad_attended[here, :] = grad_attended
            r.bias_sums[0:1, :] += total_rows(grad_attended.astype(F32))
            return carry

        lax.fori_loop(0, tokens // ROWS, second_back, 0)
        sum_fc2.forward(1)
        here = pl.ds(latent * tokens, tokens)
        grad_mixed = dot_right_t(r.grad_attended[here, :], r.out[...])
        for copy in mixed_moves[latent][1]:
            release(copy)
        for block in range(seq):
            piece = grad_mixed[:, block * part : (block + 1) * part].astype(BF16)
            r.mixed_send[block, latent] = piece
        own = local(r.mixed_send.at[s_me, latent], r.mixed_recv.at[s_me, latent])
        mix_moves.append(
            (
                own,
                exchange(
                    lambda peer, latent=latent: r.mixed_send.at[peer, latent],
                    lambda me, latent=latent: r.mixed_recv.at[me, latent],
                ),
            )
        )

    sum_fc2.forward()
    weight_grad(r.mixed, r.grad_attended, r.out)

    for move in branch_moves:
        move.forward()

    def attend_back(index, carry):
        queries, keys, values = r.q_heads[index], r.k_heads[index], r.v_heads[index]
        incoming = r.o_heads[index]
        r.v_heads[index] = dot_left_t(r.soft[index], incoming).astype(BF16)

        for row in range(0, length, half):
            here = slice(row, row + half)
            soft = r.soft[index, here, :].astype(F32)
            grad_soft = dot_right_t(r.o_heads[index, here, :], values)
            delta = jnp.sum(soft * grad_soft, axis=-1, keepdims=True)
            r.soft[index, here, :] = (soft * (grad_soft - delta)).astype(BF16)
        r.q_heads[index] = (dot(r.soft[index], keys) * ROOT).astype(BF16)
        r.k_heads[index] = (dot_left_t(r.soft[index], queries) * ROOT).astype(BF16)
        return carry

    fc_rows = rows_of(r.attended, 0, sz.units)
    joined_sums = r.joined_sums
    grad_joined = r.grad_hidden.at[:, pl.ds(0, sz.joined)]
    joined_sums[...] = jnp.zeros_like(joined_sums)
    token_moves = []
    for latent in range(count):
        own, moves = mix_moves[latent]
        own.wait()
        settle(moves)

        def unpack(block, carry, latent=latent):
            row = pl.multiple_of(block * tokens, tokens)
            values = r.mixed_recv[block, latent]
            for head in range(heads):
                piece = pad_head(values[:, head * HEAD_DIM : (head + 1) * HEAD_DIM])
                r.o_heads[latent * heads + head, pl.ds(row, tokens), :] = piece
            return carry

        lax.fori_loop(0, seq, unpack, 0)
        middle_head = latent * heads + heads // 2
        lax.fori_loop(latent * heads, middle_head, attend_back, 0)
        if latent:
            token_moves[latent - 1].forward()
            sum_fc1.forward(1)
        lax.fori_loop(middle_head, (latent + 1) * heads, attend_back, 0)
        sum_fc1.forward(1)

        def join(block, carry, latent=latent):
            row = pl.multiple_of(block * tokens, tokens)
            start = pl.multiple_of(latent * length + block * tokens, tokens)
            pieces = [
                source[latent * heads + head, pl.ds(row, tokens), :][:, :HEAD_DIM]
                for source in (r.q_heads, r.k_heads, r.v_heads)
                for head in range(heads)
            ]
            if sz.joined > 3 * part:
                pieces.append(jnp.zeros((tokens, sz.joined - 3 * part), BF16))
            values = jnp.concatenate(pieces, axis=1)
            joined_sums[...] += total_rows(values.astype(F32))
            grad_joined[pl.ds(start, tokens), :] = values
            return carry

        lax.fori_loop(0, seq, join, 0)

        def back_qkv(step, carry, latent=latent):
            start = pl.multiple_of(latent * length + step * tile, tile)
            rows = grad_joined[pl.ds(start, tile), :]
            for column, size in column_cuts(width):
                here = slice(column, column + size)
                sums = dot_right_t(rows, r.qkv[here, :])
                r.part_a[pl.ds(start, tile), here] = sums.astype(BF16)
            return carry

        lax.fori_loop(0, per_latent, back_qkv, 0)
        token_moves.append(SumTokens(r.part_a, 0, latent))

    token_moves[-1].forward()
    sum_fc2.finish(fc_rows)
    fc2_move = local(fc_rows, r.fc2_out)
    pl.semaphore_signal(r.free_x, inc=1, device_id=device_x, device_id_type=MESH)
    for step in range(1, line):
        pl.semaphore_signal(
            r.free_z, inc=1, device_id=device_z(step), device_id_type=MESH
        )
    gather_qkv.drain()
    weight_grad(r.modded, grad_joined, r.qkv)
    sum_qkv = SumWeights(r.qkv, sz.chunk, r.across_b, r.along_b, sz.joined)
    pl.semaphore_wait(r.free_x, 1)
    sum_qkv.push()
    sum_fc1.forward()
    pl.semaphore_wait(r.free_z, line - 1)


    for latent in range(count):
        branch_moves[latent].finish()

        def final_output(step, carry, latent=latent):
            start = pl.multiple_of(step * ROWS, ROWS)
            here = pl.ds(latent * tokens + start, ROWS)
            branch = branch_moves[latent].rows(start) + r.bias_fc2[...]
            grad_output = r.out_grad[latent, pl.ds(start, ROWS), :].astype(F32)
            gate = mod[latent, 5:6, :]
            r.modded_two[here, :] = (r.middle[here, :] + gate * branch).astype(BF16)
            grad_mod[latent, 5:6, :] += total_rows(grad_output * branch)
            r.bias_sums[1:2, :] += total_rows((gate * grad_output).astype(BF16).astype(F32))
            return carry

        lax.fori_loop(0, tokens // ROWS, final_output, 0)
        slot = rows_of(r.modded_two, latent * tokens, tokens)
        far_moves.append(local(slot, r.output.at[latent]))
    for latent in range(count):
        token_moves[latent].finish()

        def final_grads(step, carry, latent=latent):
            start = pl.multiple_of(step * ROWS, ROWS)
            here = pl.ds(latent * tokens + start, ROWS)
            incoming = token_moves[latent].rows(start)
            normed, inverse = layer_norm(r.latents[latent, pl.ds(start, ROWS), :].astype(F32))
            grad_mod[latent, 0:1, :] += total_rows(incoming)
            grad_mod[latent, 1:2, :] += total_rows(incoming * normed)
            grads = r.grad_middle[here, :] + norm_back(
                incoming * (1.0 + mod[latent, 1:2, :]), normed, inverse
            )
            place = pl.ds((count + latent) * tokens + start, ROWS)
            r.modded_two[place, :] = grads.astype(BF16)
            return carry

        lax.fori_loop(0, tokens // ROWS, final_grads, 0)
        slot = rows_of(r.modded_two, (count + latent) * tokens, tokens)
        far_moves.append(local(slot, r.latents_grad.at[latent]))

    def return_rows(total, send_ref, recv_ref):
        send_ref[...] = dot(loosen, total.astype(BF16)).astype(BF16)
        mine = rows_of(send_ref, s_me * pad, pad)
        own = local(mine, rows_of(recv_ref, s_me * pad, pad))
        moves = exchange(
            lambda peer: rows_of(send_ref, peer * pad, pad),
            lambda me: rows_of(recv_ref, me * pad, pad),
        )
        return own, moves

    def small(values):
        return values.reshape(count * 8, width)

    r.grad_core_send[...] = small(grad_mod[...])
    mod_core = send(r.grad_core_send, r.grad_core, device_seq(1))

    def own_place(sums, column):
        return place(sums[:, column : column + part], s_me * part, width)

    sums = joined_sums[...]
    r.bias_sums[2:3, :] = own_place(sums, 0)
    r.bias_sums[3:4, :] = own_place(sums, 2 * part)
    for position in range(seq):
        r.bias_sums[4 + position : 5 + position, :] = when(s_me == position, r.fc1_sums[...])
    bias_x = send(r.bias_sums, r.bias_x, device_x)
    mod_core.wait_recv()
    r.grad_chip_send[...] = r.grad_core_send[...] + r.grad_core[...]
    mod_chip = send(r.grad_chip_send, r.grad_chip, device_seq(2))

    def loosen_out(step, carry):
        start = pl.multiple_of(step * sz.chunk, 16)
        spread = dot(loosen, r.out[pl.ds(start, sz.chunk), :]).astype(BF16)
        for block in range(seq):
            place = pl.multiple_of(block * out_wide + step * pad, 16)
            r.out_blocks[pl.ds(place, pad), :] = spread[block * pad : (block + 1) * pad, :]
        return carry

    lax.fori_loop(0, sz.dp, loosen_out, 0)
    out_first = [
        send(
            rows_of(r.out_blocks, (y * 2 + 1 - c_me) * out_wide, out_wide),
            rows_of(r.grad_branch, y * out_wide, out_wide),
            device_seq(1),
        )
        for y in range(2)
    ]

    def out_from_core(y):
        return rows_of(r.grad_branch, y * out_wide, out_wide)[...].astype(F32)

    other = rows_of(r.out_blocks, ((1 - y_me) * 2 + c_me) * out_wide, out_wide)
    out_chip_sum = rows_of(r.modded_two, 2 * count * tokens, out_wide)

    def out_half(index):
        start, size = index * (out_wide // 2), out_wide // 2
        return send(rows_of(other, start, size), rows_of(out_chip_sum, start, size), device_seq(2))

    for copy in out_first:
        copy.wait_recv()
    other[...] = (other[...].astype(F32) + out_from_core(1 - y_me)).astype(BF16)
    out_second = [out_half(0), out_half(1)]
    mod_chip.wait_recv()
    rows_of(r.bias_all, dp_me * 16, 16)[...] = (r.grad_chip_send[...] + r.grad_chip[...]).astype(
        BF16
    )
    gather_grad = GatherWeights(r.bias_all, 16, direct=True)
    gather_grad.push()
    sum_qkv.forward(1)
    fc2_move.wait()
    sum_fc1.finish(fc_rows)
    fc1_own, fc1_back = return_rows(fc_rows[...], r.fc1_blocks, r.fc1_rows)
    gather_grad.forward()
    sum_qkv.forward(1)
    bias_x.wait_recv()
    r.bias_half[...] = r.bias_sums[...] + r.bias_x[...]
    room_z = r.mod_z.at[:, :, pl.ds(0, width)]
    bias_z = [send(r.bias_half, room_z.at[step], device_z(step)) for step in range(1, line)]
    pending.extend([mod_core, bias_x, mod_chip] + bias_z)
    sum_qkv.forward(1)

    gather_grad.finish()
    all_grads = r.bias_all[...]
    rows = sz.dp * 16
    comp_of = iota((rows, rows), 0) & 7
    source = (iota((rows, rows), 0) & ~15) + ((iota((rows, rows), 0) >> 3) & 1)
    spread = jnp.where(iota((rows, rows), 1) == source, 1.0, 0.0).astype(BF16)
    cond_spread = dot(spread, r.cond_mine[...])
    comp_of = iota((rows, LANES), 0) & 7
    cond_grads = jnp.zeros((rows, sz.rows), F32)
    mod_rows = r.mod_out.shape[0]
    for comp in range(6):
        back = dot_right_t(all_grads, r.w_mod[:, comp * width : (comp + 1) * width])
        cond_grads = cond_grads + jnp.where(comp_of[:, : sz.rows] == comp, back, 0.0)
    cond_grads = jnp.sum(cond_grads.reshape(rows // 8, 8, sz.rows), axis=1)
    blank = jnp.zeros((16, width - sz.rows), F32)
    cond_grads = pltpu.roll(jnp.concatenate([cond_grads, blank], axis=1), me * sz.rows, 1)
    keep = iota((8, 16), 0)
    hits = []
    for side in range(2):
        hits.append(
            sum(
                when(
                    iota((8, width), 0) == along * count + latent,
                    jnp.broadcast_to(
                        cond_grads[
                            (along * 2 + side) * count + latent : (along * 2 + side) * count
                            + latent
                            + 1,
                            :,
                        ],
                        (8, width),
                    ),
                )
                for along in range(line)
                for latent in range(count)
            )
        )
    r.cond_sides[0] = hits[0]
    r.cond_sides[1] = hits[1]
    cond_x = send(r.cond_sides.at[1 - x_me], r.cond_x, device_x)
    for copy in out_second:
        copy.wait_recv()
    mine = out_mine[...].astype(F32) + out_from_core(y_me)
    out_mine[...] = (mine + out_chip_sum[...].astype(F32)).astype(BF16)
    pending.extend(out_first + out_second)
    sum_out = SumWeights(out_mine, pad, r.across_out, r.along_out, width)
    sum_out.push()
    bias_total = r.bias_half[...]
    for copy, step in zip(bias_z, range(1, line)):
        copy.wait_recv()
        bias_total = bias_total + room_z[step]
    r.bias_line[...] = bias_total
    bias_core = send(r.bias_line, r.bias_core, device_seq(1))
    cond_x.wait_recv()
    r.cond_half[...] = r.cond_sides[x_me] + r.cond_x[...]
    cond_z = [send(r.cond_half, r.cond_z.at[step], device_z(step)) for step in range(1, line)]
    bias_core.wait_recv()
    r.bias_pair[...] = r.bias_line[...] + r.bias_core[...]
    bias_chip = send(r.bias_pair, r.bias_chip, device_seq(2))
    comp_rows = iota((8, rows), 0) == (iota((8, rows), 1) & 7)
    mod_bias = dot(jnp.where(comp_rows, 1.0, 0.0).astype(BF16), all_grads)
    cond_total = r.cond_half[...]
    for copy, step in zip(cond_z, range(1, line)):
        copy.wait_recv()
        cond_total = cond_total + r.cond_z[step]
    r.cond_line[...] = cond_total
    cond_seq = exchange(lambda peer: r.cond_line, lambda me: r.cond_seq.at[me])
    for comp in range(6):
        chosen = jnp.where(comp_of == comp, cond_spread, 0.0).astype(BF16)
        place_rows = rows_of(r.grad_middle, comp * mod_rows, mod_rows)
        place_rows[...] = dot_left_t(chosen, all_grads)[:mod_rows, :]
        far_moves.append(local(place_rows, r.mod_out.at[:, pl.ds(comp * width, width)]))
    sum_out.forward(1)
    bias_chip.wait_recv()
    bias_full = r.bias_pair[...] + r.bias_chip[...]

    def own_lanes(row, start):
        size = row.shape[1]
        turned = pltpu.roll(jnp.broadcast_to(row, (8, size)), lax.rem(size - start, size), 1)
        return turned[0:1, : 2 * LANES]

    qv_total = when(me < half_way, bias_full[2:3, :]) + when(me >= half_way, bias_full[3:4, :])
    fc1_total = sum(
        when(s_me == position, bias_full[4 + position : 5 + position, :])
        for position in range(seq)
    )
    first = me * (6 * sz.rows) // width
    comp_row = iota((8, width), 0)
    pair = [
        jnp.sum(jnp.where(comp_row == first + more, mod_bias, 0.0), axis=0, keepdims=True)
        for more in range(2)
    ]
    r.small_out[...] = jnp.concatenate(
        [
            own_lanes(bias_full[0:1, :], me * sz.rows),
            own_lanes(bias_full[1:2, :], me * sz.rows),
            own_lanes(qv_total, lax.rem(me, half_way) * (2 * sz.rows)),
            own_lanes(fc1_total, dp_me * sz.units),
            own_lanes(jnp.concatenate(pair, axis=1), me * (6 * sz.rows) - first * width),
            jnp.zeros((3, 2 * LANES), F32),
        ],
        axis=0,
    )
    qkv_total = fc_rows.at[:, pl.ds(0, sz.joined)]
    sum_out.forward()
    sum_qkv.finish(qkv_total)
    qkv_own, qkv_back = return_rows(qkv_total[...], r.qkv_blocks, r.qkv_rows)
    out_rows = rows_of(r.middle, 0, pad)
    sum_out.finish(out_rows)
    far_moves.append(local(out_rows, r.out_out))
    gather_grad.drain()
    cond_full = r.cond_line[...]
    for copy, mask in zip(cond_seq, (1, 2, 3)):
        copy.wait_recv()
        cond_full = cond_full + r.cond_seq[seq_peer(mask)]
    picked = [
        jnp.sum(
            jnp.where(comp_row == z_me * count + latent, cond_full, 0.0), axis=0, keepdims=True
        )
        for latent in range(count)
    ]
    slope = gate_cond * (1.0 + cond * (1.0 - gate_cond))
    r.cond_grad[...] = (jnp.concatenate(picked, axis=0) * slope).astype(BF16)
    pending.extend([bias_core, bias_chip, cond_x] + cond_seq + cond_z)
    for own, moves in ((fc1_own, fc1_back), (qkv_own, qkv_back)):
        own.wait()
        settle(moves)
    far_moves.append(local(r.fc1_rows, r.fc1_out))
    far_moves.append(local(r.qkv_rows, r.qkv_out))
    for copy in far_moves:
        copy.wait()
    for copy in pending:
        copy.wait_send()


class Inputs(NamedTuple):
    latents: object
    out_grad: object
    conditioning: object
    b_mod: object
    b_qv: object
    b_out: object
    b_fc1: object
    b_fc2: object
    w_mod: object
    qkv_src: object
    fc1_src: object
    out_src: object
    fc2_src: object


class Outputs(NamedTuple):
    output: object
    latents_grad: object
    cond_grad: object
    mod_out: object
    small_out: object
    qkv_out: object
    out_out: object
    fc1_out: object
    fc2_out: object


def kernel_scratch(sz):
    low = lambda *shape: pltpu.VMEM(shape, BF16)
    full = lambda *shape: pltpu.VMEM(shape, F32)
    count, tokens, width, seq = sz.count, sz.tokens, sz.width, sz.seq
    pad, groups = sz.padded_rows, sz.count * sz.heads
    tall = sz.chunk if sz.chunk > sz.units else sz.units
    wide = max(sz.joined, sz.hidden, width)
    return dict(
        lat_all=low(sz.total, max(width, sz.hidden)),
        grad_branch=low(sz.total, width),
        modded=low(sz.total, width),
        q_heads=low(groups, sz.length, LANES),
        k_heads=low(groups, sz.length, LANES),
        v_heads=low(groups, sz.length, LANES),
        o_heads=low(groups, sz.length, LANES),
        soft=low(groups, sz.length, sz.length),
        mixed_send=low(seq, count, tokens, sz.part),
        mixed_recv=low(seq, count, tokens, sz.part),
        mixed=low(sz.own, width),
        attended=full(sz.own, width),
        middle=full(sz.own, width),
        grad_middle=full(sz.own, width),
        grad_attended=low(sz.own, width),
        modded_two=low(sz.total, width),
        grad_hidden=low(sz.total, sz.hidden),
        part_a=low(sz.total, width),
        sum_core=low(2, 2, count, tokens, width),
        sum_send=low(2, count, tokens, width),
        sum_chip=low(2, count, tokens, width),
        qkv_raw=low(sz.rows, 3 * width),
        fc1_raw=low(sz.rows, seq * sz.hidden),
        out_raw=low(sz.rows, width),
        qkv_blocks=low(seq * pad, sz.joined),
        fc1_blocks=low(seq * pad, sz.hidden),
        qkv_rows=low(seq * pad, sz.joined),
        fc1_rows=low(seq * pad, sz.hidden),
        out_blocks=low(seq * sz.dp * pad, width),
        qkv=low(width, sz.joined),
        fc1=low(width, sz.hidden),
        fc2=low(sz.hidden, width),
        out=low(width, width),
        across_a=low(sz.line, sz.chunk, wide),
        along_a=low(sz.line, sz.chunk, wide),
        across_b=low(sz.line, tall, wide),
        along_b=low(sz.line, tall, wide),
        across_out=low(sz.line, pad, width),
        along_out=low(sz.line, pad, width),
        cond_all=low(sz.dp * 16, width),
        cond_mine=low(sz.dp * 16, LANES),
        bias_blocks=low(seq * 16, width),
        bias_all=low(sz.dp * 16, width),
        mod_sums=full(16, sz.mod_part * seq),
        mod_core=full(2, 16, sz.mod_part),
        mod_send=full(16, sz.mod_part),
        mod_chip=full(16, sz.mod_part),
        mod_sum=full(16, sz.mod_part),
        mod_x=full(8, sz.mod_part),
        mod_half=full(8, sz.mod_part),
        mod_z=full(sz.line, 8, sz.mod_part),
        mod_all=full(seq, 8, sz.mod_part),
        modulation=full(count, 8, width),
        bias_joined=full(1, sz.joined),
        bias_out=full(1, width),
        bias_fc1=full(1, width),
        bias_fc2=full(1, width),
        joined_sums=full(1, sz.joined),
        fc1_sums=full(1, sz.hidden),
        grad_mod=full(count, 8, width),
        grad_core_send=full(16, width),
        grad_core=full(16, width),
        grad_chip_send=full(16, width),
        grad_chip=full(16, width),
        bias_sums=full(8, width),
        bias_x=full(8, width),
        bias_half=full(8, width),
        bias_line=full(8, width),
        bias_core=full(8, width),
        bias_pair=full(8, width),
        bias_chip=full(8, width),
        cond_sides=full(2, 8, width),
        cond_x=full(8, width),
        cond_half=full(8, width),
        cond_z=full(sz.line, 8, width),
        cond_line=full(8, width),
        cond_seq=full(seq, 8, width),
        send_sems=pltpu.SemaphoreType.DMA((200,)),
        recv_sems=pltpu.SemaphoreType.DMA((200,)),
        free_x=pltpu.SemaphoreType.REGULAR,
        free_z=pltpu.SemaphoreType.REGULAR,
        local_sems=pltpu.SemaphoreType.DMA((40,)),
    )


def kernel_outputs(sz):
    low = lambda *shape: jax.ShapeDtypeStruct(shape, BF16)
    full = lambda *shape: jax.ShapeDtypeStruct(shape, F32)
    count, tokens, width, pad = sz.count, sz.tokens, sz.width, sz.padded_rows
    return [
        low(count, tokens, width),
        low(count, tokens, width),
        low(count, width),
        full(-(-sz.rows // 8) * 8, 6 * width),
        full(8, 2 * LANES),
        low(sz.seq * pad, sz.joined),
        full(pad, width),
        low(sz.seq * pad, sz.hidden),
        full(sz.units, width),
    ]


def run_kernel(sz, *operands):
    vmem = pl.BlockSpec(memory_space=pltpu.VMEM)
    far = pl.BlockSpec(memory_space=pl.ANY)
    outputs = kernel_outputs(sz)
    return pl.pallas_call(
        partial(block_kernel, sz),
        out_shape=outputs,
        in_specs=[vmem] * 9 + [far] * 4,
        out_specs=[far, far, vmem, far, vmem, far, far, far, far],
        scratch_shapes=list(kernel_scratch(sz).values()),
        compiler_params=pltpu.CompilerParams(
            collective_id=0, has_side_effects=True, vmem_limit_bytes=66584576
        ),
    )(*operands)


def general_path(
    latents, out_grad, modulation, blocks, w_out, w_fc2, bias_qv, bias_out, bias_fc1, bias_fc2
):
    count, tokens, width = latents.shape
    dp, seq = lax.axis_size("dp"), lax.axis_size("seq")
    both = ("dp", "seq")
    qkv_blocks, fc1_blocks = blocks
    rows = qkv_blocks.shape[1]
    part, heads, length = width // seq, HEADS // seq, seq * tokens
    shift_att, scale_att, gate_att, shift_mlp, scale_mlp, gate_mlp = [
        modulation[:, index : index + 1] for index in range(6)
    ]

    def to_columns(blocks):
        mine = lax.all_to_all(blocks, "seq", 0, 0, tiled=True).reshape(seq * rows, -1)
        return lax.all_gather(mine, "dp", axis=0, tiled=True)

    full_qkv = to_columns(qkv_blocks)
    full_out = lax.all_gather(w_out, both, axis=0, tiled=True)
    full_fc1 = to_columns(fc1_blocks)
    full_fc2 = lax.all_gather(w_fc2, "dp", axis=0, tiled=True)

    def gather_tokens(values):
        return lax.all_gather(values, "seq", axis=1, tiled=True)

    def flat(values):
        return values.reshape(-1, values.shape[-1])

    tokens_f = latents.astype(F32)
    normed, inverse = layer_norm(tokens_f)
    modded = (normed * (1.0 + scale_att) + shift_att).astype(BF16)
    modded_all = flat(gather_tokens(modded))
    joined = dot(modded_all, full_qkv).reshape(count, length, 3, heads, HEAD_DIM)
    bias_q = bias_qv[0].reshape(heads, HEAD_DIM)
    bias_v = bias_qv[1].reshape(heads, HEAD_DIM)
    queries = (joined[:, :, 0] + bias_q).astype(BF16)
    keys = joined[:, :, 1].astype(BF16)
    values = (joined[:, :, 2] + bias_v).astype(BF16)
    scores = jnp.einsum("bqhd,bkhd->bhqk", queries, keys, preferred_element_type=F32) * (
        HEAD_DIM ** (-0.5)
    )
    soft = jax.nn.softmax(scores, axis=-1)
    soft_low = soft.astype(BF16)
    mixed = jnp.einsum("bhqk,bkhd->bqhd", soft_low, values, preferred_element_type=F32)
    mixed = mixed.astype(BF16).reshape(count, length, part)
    mixed_mine = lax.all_to_all(mixed, "seq", 1, 2, tiled=True)
    attended = dot(mixed_mine, full_out) + bias_out
    middle = tokens_f + gate_att * attended
    normed_two, inverse_two = layer_norm(middle)
    modded_two = (normed_two * (1.0 + scale_mlp) + shift_mlp).astype(BF16)
    modded_two_all = flat(gather_tokens(modded_two))
    hidden = dot(modded_two_all, full_fc1) + bias_fc1
    active, gelu_back = jax.vjp(partial(jax.nn.gelu, approximate=True), hidden)
    active = active.astype(BF16)

    def sum_tokens(partial_sums):
        parts = partial_sums.astype(BF16).reshape(count, length, width)
        return lax.psum_scatter(parts, "seq", scatter_dimension=1, tiled=True).astype(F32)

    branch = sum_tokens(dot(active, full_fc2)) + bias_fc2
    output = middle + gate_mlp * branch

    grad_output = out_grad.astype(F32)
    grad_gate_mlp = jnp.sum(grad_output * branch, axis=1)
    grad_branch = (gate_mlp * grad_output).astype(BF16)
    grad_branch_all = flat(gather_tokens(grad_branch))
    grad_hidden = gelu_back(dot_right_t(grad_branch_all, full_fc2))[0].astype(BF16)
    grad_modded_two = sum_tokens(dot_right_t(grad_hidden, full_fc1))
    grad_shift_mlp = jnp.sum(grad_modded_two, axis=1)
    grad_scale_mlp = jnp.sum(grad_modded_two * normed_two, axis=1)
    grad_middle = grad_output + norm_back(
        grad_modded_two * (1.0 + scale_mlp), normed_two, inverse_two
    )
    grad_gate_att = jnp.sum(grad_middle * attended, axis=1)
    grad_attended = (gate_att * grad_middle).astype(BF16)
    grad_mixed = dot_right_t(flat(grad_attended), full_out).astype(BF16)
    grad_mixed = lax.all_to_all(grad_mixed.reshape(latents.shape), "seq", 2, 1, tiled=True)
    grad_mixed = grad_mixed.reshape(count, length, heads, HEAD_DIM)
    grad_soft = jnp.einsum("bqhd,bkhd->bhqk", grad_mixed, values, preferred_element_type=F32)
    delta = jnp.sum(soft * grad_soft, axis=-1, keepdims=True)
    grad_scores = (soft * (grad_soft - delta)).astype(BF16)
    scale = HEAD_DIM ** (-0.5)
    grad_q = jnp.einsum("bhqk,bkhd->bqhd", grad_scores, keys, preferred_element_type=F32) * scale
    grad_k = jnp.einsum("bhqk,bqhd->bkhd", grad_scores, queries, preferred_element_type=F32) * scale
    grad_v = jnp.einsum("bhqk,bqhd->bkhd", soft_low, grad_mixed, preferred_element_type=F32)
    grad_joined = jnp.concatenate(
        [item.astype(BF16).reshape(count * length, part) for item in (grad_q, grad_k, grad_v)],
        axis=1,
    )
    grad_modded = sum_tokens(dot_right_t(grad_joined, full_qkv))
    grad_shift_att = jnp.sum(grad_modded, axis=1)
    grad_scale_att = jnp.sum(grad_modded * normed, axis=1)
    grad_tokens = grad_middle + norm_back(grad_modded * (1.0 + scale_att), normed, inverse)

    def from_columns(sums, groups):
        mine = lax.psum_scatter(sums.astype(BF16), "dp", scatter_dimension=0, tiled=True)
        blocks = lax.all_to_all(mine.reshape(seq, rows, -1), "seq", 0, 0, tiled=True)
        blocks = blocks.astype(F32).reshape(seq, rows, groups, -1)
        return blocks.transpose(1, 2, 0, 3).reshape(rows, -1)

    sums_fc2 = lax.psum_scatter(
        dot_left_t(active, grad_branch_all).astype(BF16), "dp", scatter_dimension=0, tiled=True
    ).astype(F32)
    sums_fc1 = from_columns(dot_left_t(modded_two_all, grad_hidden), dp)
    sums_out = lax.psum_scatter(
        dot_left_t(flat(mixed_mine), flat(grad_attended)).astype(BF16),
        both,
        scatter_dimension=0,
        tiled=True,
    ).astype(F32)
    sums_qkv = from_columns(dot_left_t(modded_all, grad_joined), 3)

    grad_mod = jnp.stack(
        [
            grad_shift_att,
            grad_scale_att,
            grad_gate_att,
            grad_shift_mlp,
            grad_scale_mlp,
            grad_gate_mlp,
        ],
        axis=1,
    )
    bias_sums = [
        jnp.sum(item.astype(F32), axis=0)
        for item in (grad_joined, flat(grad_attended), grad_hidden, flat(grad_branch))
    ]
    weight_sums = [sums_qkv, sums_out, sums_fc1, sums_fc2]
    return output.astype(BF16), grad_tokens.astype(BF16), grad_mod, bias_sums, weight_sums


def kernel_path(sz, latents, conditioning, w_mod, w_qkv, w_out, w_fc1, w_fc2, biases, out_grad):
    output, grad_tokens, grad_cond, sums_mod, small, sums_qkv, sums_out, sums_fc1, sums_fc2 = (
        run_kernel(
            sz,
            latents,
            out_grad,
            conditioning,
            *biases,
            w_mod,
            w_qkv,
            w_fc1,
            w_out,
            w_fc2,
        )
    )

    return arrange(
        sz, output, grad_tokens, sums_fc2, grad_cond, sums_mod, sums_qkv, sums_out, sums_fc1, small
    )


def arrange_kernel(sz, *refs):
    output, grad_tokens, fc2, cond, mod, qkv, out, fc1, small = refs[:9]
    (to_output, to_tokens, to_cond, to_mod, to_b_mod, to_qkv, to_b_qv) = refs[9:16]
    (to_out, to_b_out, to_fc1, to_b_fc1, to_fc2, to_b_fc2, sems) = refs[16:23]
    near = refs[23:]
    moves = [
        pltpu.make_async_copy(source, target, sems.at[index])
        for index, (source, target) in enumerate(zip(refs[:9], near))
    ]
    for move in moves:
        move.start()
    for move in moves:
        move.wait()
    output, grad_tokens, fc2, cond, mod, qkv, out, fc1, small = near
    moves = [
        pltpu.make_async_copy(source, target, sems.at[index])
        for index, (source, target) in enumerate(
            ((output, to_output), (grad_tokens, to_tokens), (fc2, to_fc2))
        )
    ]
    for move in moves:
        move.start()
    rows, pad, seq = sz.rows, sz.padded_rows, sz.seq

    def join(source, groups, size):
        pieces = [
            source[position * pad : (position + 1) * pad, group * size : (group + 1) * size]
            for group in range(groups)
            for position in range(seq)
        ]
        return jnp.concatenate([piece.astype(F32) for piece in pieces], axis=1)[:rows, :]

    to_cond[...] = cond[...]
    to_mod[...] = mod[:rows, :]
    to_out[...] = out[:rows, :]
    to_qkv[...] = join(qkv, 3, sz.part)
    to_fc1[...] = join(fc1, sz.dp, sz.units)
    for index, target in enumerate((to_b_out, to_b_fc2, to_b_qv, to_b_fc1, to_b_mod)):
        target[...] = small[index : index + 1, : target.shape[1]]
    for move in moves:
        move.wait()


def arrange(sz, output, grad_tokens, fc2, cond, mod, qkv, out, fc1, small):
    vmem = pl.BlockSpec(memory_space=pltpu.VMEM)
    far = pl.BlockSpec(memory_space=pl.ANY)
    low = lambda *shape: jax.ShapeDtypeStruct(shape, BF16)
    full = lambda *shape: jax.ShapeDtypeStruct(shape, F32)
    rows, width, hidden = sz.rows, sz.width, sz.hidden * sz.seq
    results = pl.pallas_call(
        partial(arrange_kernel, sz),
        out_shape=[
            low(*output.shape),
            low(*output.shape),
            low(sz.count, width),
            full(rows, 6 * width),
            full(1, 6 * rows),
            full(rows, 3 * width),
            full(1, 2 * rows),
            full(rows, width),
            full(1, rows),
            full(rows, hidden),
            full(1, sz.units),
            full(sz.units, width),
            full(1, rows),
        ],
        in_specs=[far] * 9,
        out_specs=[far, far] + [vmem] * 9 + [far, vmem],
        scratch_shapes=[pltpu.SemaphoreType.DMA((9,))]
        + [
            pltpu.VMEM(item.shape, item.dtype)
            for item in (output, grad_tokens, fc2, cond, mod, qkv, out, fc1, small)
        ],
        compiler_params=pltpu.CompilerParams(vmem_limit_bytes=66584576),
    )(output, grad_tokens, fc2, cond, mod, qkv, out, fc1, small)
    return tuple(item.reshape(-1) if item.shape[0] == 1 else item for item in results)


def column_blocks(seq, dp, w_qkv, w_fc1, units):
    rows = w_qkv.shape[0]
    qkv_blocks = w_qkv.reshape(rows, 3, seq, -1).transpose(2, 0, 1, 3).reshape(seq, rows, -1)
    fc1_blocks = w_fc1.reshape(rows, dp, seq, units).transpose(2, 0, 1, 3).reshape(seq, rows, -1)
    return qkv_blocks, fc1_blocks


def body(
    latents,
    conditioning,
    w_mod,
    b_mod,
    w_qkv,
    b_qv,
    w_out,
    b_out,
    w_fc1,
    b_fc1,
    w_fc2,
    b_fc2,
    out_grad,
):
    count, tokens, width = latents.shape
    dp, seq = lax.axis_size("dp"), lax.axis_size("seq")
    sz = Sizes(dp, seq, latents, w_qkv, w_fc2)
    if sz.fits():
        biases = (b_mod, b_qv, b_out, b_fc1, b_fc2)
        return kernel_path(
            sz, latents, conditioning, w_mod, w_qkv, w_out, w_fc1, w_fc2, biases, out_grad
        )
    both = ("dp", "seq")
    my_dp, my_seq = lax.axis_index("dp"), lax.axis_index("seq")
    me = my_dp * seq + my_seq
    rows, units = w_qkv.shape[0], w_fc2.shape[0]
    part = width // seq

    cond = conditioning.astype(F32)
    cond_act, silu_back = jax.vjp(jax.nn.silu, cond)
    cond_low = lax.all_gather(cond_act.astype(BF16), "dp", axis=0, tiled=True)
    cond_mine = lax.dynamic_slice_in_dim(cond_low, me * rows, rows, axis=1)
    mod_part = dot(cond_mine, w_mod)
    mod_sum = lax.psum(lax.psum_scatter(mod_part, "dp", scatter_dimension=0, tiled=True), "seq")
    biases = lax.all_gather(jnp.concatenate([b_mod, b_qv, b_out, b_fc1, b_fc2]), both, axis=0)
    pieces, start = [], 0
    for item in (b_mod, b_qv, b_out, b_fc1, b_fc2):
        pieces.append(biases[:, start : start + item.shape[0]].reshape(-1).astype(F32))
        start += item.shape[0]
    bias_mod, bias_qv, bias_out, bias_fc1, bias_fc2 = pieces
    bias_qv = lax.dynamic_index_in_dim(bias_qv.reshape(2, seq, part), my_seq, 1, keepdims=False)
    bias_fc1 = lax.dynamic_index_in_dim(
        bias_fc1.reshape(dp, seq, units), my_seq, 1, keepdims=False
    ).reshape(-1)
    modulation = (mod_sum + bias_mod).reshape(count, 6, width)

    blocks = column_blocks(seq, dp, w_qkv, w_fc1, units)
    output, grad_tokens, grad_mod, bias_sums, weight_sums = general_path(
        latents,
        out_grad,
        modulation,
        blocks,
        w_out,
        w_fc2,
        bias_qv,
        bias_out,
        bias_fc1,
        bias_fc2,
    )
    sums_qkv, sums_out, sums_fc1, sums_fc2 = weight_sums

    grad_mod = grad_mod.reshape(count, -1)
    grad_mod = lax.psum(grad_mod, "seq").astype(BF16)
    grad_mod = lax.all_gather(grad_mod, "dp", axis=0, tiled=True)
    sums_mod = dot_left_t(cond_mine, grad_mod)
    own = b_mod.shape[0]
    sums_bias_mod = jnp.sum(
        lax.dynamic_slice_in_dim(grad_mod, me * own, own, axis=1).astype(F32), axis=0
    )
    grad_cond_act = lax.all_gather(dot_right_t(grad_mod, w_mod), both, axis=0)
    grad_cond_act = lax.dynamic_slice_in_dim(grad_cond_act, my_dp * count, count, axis=1)
    grad_cond = silu_back(grad_cond_act.transpose(1, 0, 2).reshape(count, width))[0]

    def spread(values, shape):
        blank = jnp.zeros(shape, F32)
        return lax.dynamic_update_slice_in_dim(blank, values, my_seq, 1).reshape(-1)

    joined_sums, out_sums, fc1_sums, fc2_sums = bias_sums
    qv_sums = jnp.stack([joined_sums[:part], joined_sums[2 * part : 3 * part]])
    bias_sums = [
        spread(qv_sums.reshape(2, 1, part), (2, seq, part)),
        out_sums,
        spread(fc1_sums.reshape(dp, 1, units), (dp, seq, units)),
        fc2_sums,
    ]
    joint = jnp.concatenate([item.reshape(dp * seq, -1) for item in bias_sums], axis=1)
    joint = lax.psum_scatter(joint, both, scatter_dimension=0, tiled=True).reshape(-1)
    cuts = [b_qv.shape[0], b_out.shape[0], b_fc1.shape[0]]
    sums_bias_qv, sums_bias_out, sums_bias_fc1, sums_bias_fc2 = jnp.split(
        joint, [cuts[0], cuts[0] + cuts[1], sum(cuts)]
    )
    return (
        output,
        grad_tokens,
        grad_cond.astype(BF16),
        sums_mod,
        sums_bias_mod,
        sums_qkv,
        sums_bias_qv,
        sums_out,
        sums_bias_out,
        sums_fc1,
        sums_bias_fc1,
        sums_fc2,
        sums_bias_fc2,
    )


def solution(mesh):
    both = P(("dp", "seq"))
    wide = P(("dp", "seq"), None)
    tokens = P("dp", "seq", None)
    in_specs = (
        tokens,
        P("dp", None),
        wide,
        both,
        wide,
        both,
        wide,
        both,
        wide,
        both,
        wide,
        both,
        tokens,
    )
    out_specs = (tokens, tokens, P("dp", None)) + (wide, both) * 5
    return jax.shard_map(body, mesh=mesh, in_specs=in_specs, out_specs=out_specs, check_vma=False)
```
